32 devices in a mesh: groups: 2 (over y), vocab: 4 (over z), rows: 2 (over x), cfg: 2 (over core).
Axes of the slice: x: 2, y: 2, z: 4, core: 2. Of those that a mesh axis runs over, the one named last changes fastest.
Arguments:
- final_hidden: bfloat16 [2, 512, 8192], P(None, ('groups', 'vocab'), ('rows', 'cfg')), parts along dimension 1
- positions: int32 [352], P('groups'), parts along dimension 0, may hold values from 0 to 255, as said below
- norm_gain: float32 [8192], P(('rows', 'cfg')), may hold values from 0.1 to 1.9
- unembedding: bfloat16 [8192, 19008], P(('rows', 'cfg'), 'vocab')
Outputs:
- guided_logprobs: float32 [352, 19008], P(('groups', 'rows', 'cfg'), 'vocab'), parts along dimension 0
The draws below stay inside these ranges and needn't reach their ends.
There are 2 independent parts, one for each index of `groups`. The reference program is written for one: setup_inputs(seed, part) draws one part's arguments, and reference() takes and returns one part's arrays. A program takes and returns all parts, laid end to end along the dimension named above; an argument that names none is the same for every part. Nothing has to cross between parts.
Inputs may be any that keep to these rules, and one draw needn't show every extreme that they name: 176 distinct positions in increasing order; 0 and 255 are always among them.
All inputs are finite; a program needn't handle non-finite values.
Results may differ from the reference program's by a relative error of at most 0.0008.
Values may be sent and summed in bfloat16 or wider, within the bound.
No kernel may reach another device: no remote copies, remote signals or barrier semaphores. Data moves between devices by JAX's collectives and lax.ppermute only.
A program may use at most 128 MiB of HBM per device.

```python
import jax
import jax.numpy as jnp
from jax import lax

D = 8192
MASKED = 176
VOCAB = 19008
SEQ = 256


def draw_final_hidden(key, part):
    key = jax.random.fold_in(key, 11)
    key_noise, key_cols, key_rows = jax.random.split(key, 3)
    column_scale = jnp.exp(jnp.log(3.0) * jnp.arange(D).astype(jnp.float32) / D + jax.random.uniform(key_cols, (D,), minval=0.0, maxval=jnp.log(10.0))) / 3.0
    noise_part = jax.random.truncated_normal(key_noise, -4.0, 4.0, (2, SEQ, D))
    row_scale = jnp.exp(jax.random.uniform(key_rows, (2, SEQ, 1), minval=0.0, maxval=jnp.log(10.0)))
    values = noise_part * column_scale
    return (values * row_scale).astype(jnp.bfloat16)


def draw_positions(key, part):
    key = jax.random.fold_in(key, 5)
    inner = jax.random.permutation(key, SEQ - 2)[:MASKED - 2].astype(jnp.int32) + 1
    chosen = jnp.concatenate([jnp.zeros((1,), jnp.int32), inner, jnp.full((1,), SEQ - 1, jnp.int32)])
    return jnp.sort(chosen).astype(jnp.int32)


def draw_unembedding(key, part):
    key = jax.random.fold_in(key, 23)
    key_noise, key_cols = jax.random.split(key, 2)
    column_scale = jnp.exp(jax.random.uniform(key_cols, (1, VOCAB), minval=jnp.log(0.4), maxval=jnp.log(4.0)))
    noise_part = jax.random.truncated_normal(key_noise, -4.0, 4.0, (D, VOCAB))
    values = noise_part * column_scale / D ** 0.5
    return values.astype(jnp.bfloat16)


def setup_inputs(seed: int = 0, part: int = 0) -> dict:
    key_list = jax.random.split(jax.random.key(seed), 5)
    own_keys = jax.random.split(jax.random.fold_in(key_list[4], part), 5)
    final_hidden = draw_final_hidden(jax.random.fold_in(jax.random.fold_in(key_list[4], part), 71), part)
    positions = draw_positions(jax.random.fold_in(jax.random.fold_in(key_list[4], part), 71), part)
    norm_gain = jnp.clip(1.0 + 0.18 * jax.random.normal(key_list[2], (D,), jnp.float32), 0.1, 1.9)
    unembedding = draw_unembedding(jax.random.fold_in(key_list[4], 71), part)
    return dict(final_hidden=final_hidden, positions=positions, norm_gain=norm_gain, unembedding=unembedding)


epsilon = 1e-06
guidance = 2.0

def reference(final_hidden, positions, norm_gain, unembedding):
    picked = jnp.take(final_hidden, positions.astype(jnp.int32), axis=1)
    widened = picked.astype(jnp.float32)
    inv_rms = lax.rsqrt(lax.optimization_barrier(jnp.mean(widened * widened, axis=2)) + epsilon)
    normed = (widened * norm_gain).astype(jnp.bfloat16)
    cond_logits = jnp.dot(normed[0], unembedding, preferred_element_type=jnp.float32)
    uncond_logits = jnp.dot(normed[1], unembedding, preferred_element_type=jnp.float32)
    guided = (1.0 + guidance) * inv_rms[0][:, None] * cond_logits - guidance * inv_rms[1][:, None] * uncond_logits
    return jax.nn.log_softmax(guided, axis=1)
```

```python
import functools

import jax
import jax.numpy as jnp
from jax import lax
from jax.experimental import pallas as pl
from jax.experimental.pallas import tpu as pltpu
from jax.sharding import PartitionSpec as P

epsilon = 1e-06
guidance = 2.0
TILE = 256
LANES = 128
MIB = 1 << 20


def in_vmem(count):
    return [pl.BlockSpec(memory_space=pltpu.VMEM)] * count


def keep_in_vmem(*arrays):
    return [pltpu.with_memory_space_constraint(a, pltpu.VMEM) for a in arrays]


def call(body, outs, args, far=(), limit=8, cost=None, **kwargs):
    return pl.pallas_call(
        body,
        out_shape=[pltpu.VMEM(shape, dtype) for shape, dtype in outs],
        in_specs=[pl.BlockSpec(memory_space=pltpu.HBM)] * len(far) + in_vmem(len(args)),
        out_specs=in_vmem(len(outs)),
        compiler_params=pltpu.CompilerParams(vmem_limit_bytes=limit * MIB),
        cost_estimate=cost and pl.CostEstimate(flops=cost[0], bytes_accessed=cost[1], transcendentals=0),
        **kwargs,
    )(*[pltpu.with_memory_space_constraint(a, pltpu.HBM) for a in far], *keep_in_vmem(*args))


def diagonal(n):
    return lax.broadcasted_iota(jnp.int32, (n, n), 0) == lax.broadcasted_iota(jnp.int32, (n, n), 1)


def as_column(row):
    return jnp.sum(jnp.where(diagonal(row.shape[1]), row, 0.0), axis=1, keepdims=True)


def as_row(column):
    return jnp.sum(jnp.where(diagonal(column.shape[0]), column, 0.0), axis=0, keepdims=True)


def squares_kernel(hidden_far, gain_far, normed_ref, out_ref, hidden_ref, gain_ref, sems):
    copies = [
        pltpu.make_async_copy(hidden_far.at[0], hidden_ref.at[0], sems.at[0]),
        pltpu.make_async_copy(hidden_far.at[1], hidden_ref.at[1], sems.at[1]),
        pltpu.make_async_copy(gain_far, gain_ref, sems.at[2]),
    ]
    for copy in copies:
        copy.start()
    for b in range(2):
        copies[b].wait()
        widened = hidden_ref[b].astype(jnp.float32)
        out_ref[b : b + 1] = as_row(jnp.sum(widened * widened, axis=1, keepdims=True))
    copies[2].wait()
    gain = gain_ref[...]
    for b in range(2):
        normed_ref[b] = (hidden_ref[b].astype(jnp.float32) * gain).astype(jnp.bfloat16)


def combine_kernel(width, normed_ref, totals_ref, *out_refs):
    inv_rms = lax.rsqrt(totals_ref[...] / width + epsilon)
    factor = [as_column((1.0 + guidance) * inv_rms[0:1]), as_column(guidance * inv_rms[1:2])]
    piece = out_refs[0].shape[0]
    for i, out_ref in enumerate(out_refs):
        rows = slice(i * piece, (i + 1) * piece)
        terms = [factor[b][rows] * normed_ref[b, rows, :].astype(jnp.float32) for b in range(2)]
        out_ref[...] = (terms[0] - terms[1]).astype(jnp.bfloat16)


def load_kernel(weights_far, *refs):
    *chunk_refs, sems = refs
    copies, start = [], 0
    for j, ref in enumerate(chunk_refs):
        size = ref.shape[0]
        copies.append(pltpu.make_async_copy(weights_far.at[pl.ds(start, size)], ref, sems.at[j]))
        start += size
    for copy in copies:
        copy.start()
    for copy in copies:
        copy.wait()


def multiply(rows_ref, weights_ref, keep_ref, send_ref):
    half, width = keep_ref.shape
    for at in range(0, width, TILE):
        size = min(TILE, width - at)
        product = lax.dot_general(
            rows_ref[...],
            weights_ref[at : at + size, :],
            (((1,), (1,)), ((), ())),
            preferred_element_type=jnp.float32,
        )
        keep_ref[:, at : at + size] = product[:half]
        send_ref[:, at : at + size] = product[half:]


def first_kernel(chooser_ref, weights_ref, *refs):
    *block_refs, rows_ref, keep_ref, send_ref = refs
    blocks = jnp.concatenate([ref[...] for ref in block_refs], axis=0)
    rows_ref[...] = jnp.dot(chooser_ref[...], blocks, preferred_element_type=jnp.float32).astype(jnp.bfloat16)
    multiply(rows_ref, weights_ref, keep_ref, send_ref)


def later_kernel(rows_ref, weights_ref, keep_ref, send_ref):
    multiply(rows_ref, weights_ref, keep_ref, send_ref)


def lanes_diagonal(n):
    return lax.broadcasted_iota(jnp.int32, (n, LANES), 0) == lax.broadcasted_iota(jnp.int32, (n, LANES), 1)


def add_kernel(own, keep_ref, got_ref, own_ref, *out_refs):
    segment = own_ref.shape[0]
    own_ref[...] = keep_ref[:segment] + got_ref[:segment]
    for s, out_ref in enumerate(out_refs, 1):
        rows = slice(s * segment, (s + 1) * segment)
        value = keep_ref[rows] + got_ref[rows]
        peak = jnp.max(jnp.abs(value), axis=1, keepdims=True)
        exponent = jnp.clip(jnp.ceil(jnp.log2(jnp.maximum(peak, 1e-30))), -90.0, 127.0)
        scaled = jnp.clip(jnp.round(value * jnp.exp2(15.0 - exponent)), -32767.0, 32767.0)
        out_ref[:, LANES:] = scaled[:, LANES:].astype(jnp.int32).astype(jnp.int16)
        as_lanes = jnp.sum(jnp.where(lanes_diagonal(segment), exponent, 0.0), axis=0, keepdims=True)
        spare = lax.broadcasted_iota(jnp.int32, (segment, LANES), 0) == own
        out_ref[:, :LANES] = jnp.where(spare, as_lanes, scaled[:, :LANES]).astype(jnp.int32).astype(jnp.int16)


def restored(own, got_ref):
    value = got_ref[...].astype(jnp.int32).astype(jnp.float32)
    segment = value.shape[0]
    exponent = jnp.sum(
        jnp.where(lanes_diagonal(segment), value[own : own + 1, :LANES], 0.0), axis=1, keepdims=True
    )
    return value * jnp.exp2(exponent - 15.0)


def stats_kernel(chunks, own, *refs):
    ins, guided_refs, out_ref = refs[: -chunks - 1], refs[-chunks - 1 : -1], refs[-1]
    each = len(ins) // chunks
    top = None
    for j in range(chunks):
        guided = ins[j * each][...]
        for got in ins[j * each + 1 : (j + 1) * each]:
            guided = guided + restored(own, got)
        guided_refs[j][...] = guided
        peak = jnp.max(guided, axis=1, keepdims=True)
        top = peak if top is None else jnp.maximum(top, peak)
    total = sum(jnp.sum(jnp.exp(ref[...] - top), axis=1, keepdims=True) for ref in guided_refs)
    segment = top.shape[0]
    out_ref[0:1, :segment] = as_row(top)
    out_ref[1:2, :segment] = as_row(total)


def final_kernel(chunks, segment, *refs):
    guided_refs, stats, out_ref = refs[:chunks], refs[chunks:-1], refs[-1]
    top = functools.reduce(jnp.maximum, [ref[0:1, :segment] for ref in stats])
    total = sum(ref[1:2, :segment] * jnp.exp(ref[0:1, :segment] - top) for ref in stats)
    own = out_ref.shape[0]
    shift = as_column(top)[:own]
    log_total = as_column(jnp.log(total))[:own]
    at = 0
    for ref in guided_refs:
        out_ref[:, at : at + ref.shape[1]] = ref[:own] - shift - log_total
        at += ref.shape[1]


def shifted(value, axis, by):
    size = lax.axis_size(axis)
    return lax.ppermute(value, axis, [(i, (i + by) % size) for i in range(size)])


def chunk_starts(vocab):
    each = -(-vocab // (3 * TILE)) * TILE
    return list(range(0, vocab, each))


def per_device(final_hidden, positions, norm_gain, unembedding):
    bf16, f32 = jnp.bfloat16, jnp.float32
    _, block, width_local = final_hidden.shape
    masked = positions.shape[0]
    vocab = unembedding.shape[1]
    n_z, n_x, n_c = lax.axis_size("vocab"), lax.axis_size("rows"), lax.axis_size("cfg")
    z, x, c = lax.axis_index("vocab"), lax.axis_index("rows"), lax.axis_index("cfg")
    own = masked // (n_x * n_c)
    segment = -(-(own + 1) // 16) * 16

    normed, squares = call(
        squares_kernel,
        [((2, block, width_local), bf16), ((2, block), f32)],
        [],
        far=[final_hidden, norm_gain[None, :]],
        scratch_shapes=[
            pltpu.VMEM((2, block, width_local), bf16),
            pltpu.VMEM((1, width_local), f32),
            pltpu.SemaphoreType.DMA((3,)),
        ],
    )
    for axis in ("cfg", "rows"):
        squares = sum([shifted(squares, axis, s) for s in range(1, lax.axis_size(axis))], squares)
    (block_rows,) = call(
        functools.partial(combine_kernel, width_local * n_x * n_c),
        [((block, width_local), bf16)],
        [normed, squares],
    )

    arrivals, offsets = [block_rows], [0]
    ahead = behind = block_rows
    for step in range(1, n_z // 2 + 1):
        ahead = shifted(ahead, "vocab", 1)
        arrivals.append(ahead)
        offsets.append(step)
        if step == 1:
            first_arrival = ahead
        if 2 * step < n_z:
            behind = shifted(behind, "vocab", -1)
            arrivals.append(behind)
            offsets.append(-step)

    starts = chunk_starts(vocab)
    sizes = [end - start for start, end in zip(starts, starts[1:] + [vocab])]
    weights, positions, first_arrival = lax.optimization_barrier((unembedding.T, positions, first_arrival))
    chunks = call(
        load_kernel,
        [((size, width_local), bf16) for size in sizes],
        [],
        far=[weights],
        limit=2,
        cost=(0, 2 * vocab * width_local),
        scratch_shapes=[pltpu.SemaphoreType.DMA((len(sizes),))],
    )

    by_owner = positions.reshape(n_x, n_c, own)
    by_owner = jnp.take(by_owner, (x + jnp.arange(n_x)) % n_x, axis=0)
    by_owner = jnp.take(by_owner, (c + jnp.arange(n_c)) % n_c, axis=1)
    wanted = jnp.transpose(by_owner, (1, 0, 2)).reshape(n_x * n_c, own)
    wanted = jnp.pad(wanted, ((0, 0), (0, segment - own)), constant_values=-1).reshape(-1)
    arrived = (z - jnp.array(offsets)) % n_z
    held = (arrived[:, None] * block + jnp.arange(block)[None, :]).reshape(-1)
    chooser = (wanted[:, None] == held[None, :]).astype(bf16)

    half = n_x * segment
    parts = []
    for j, size in enumerate(sizes):
        outs = [((half, size), f32)] * 2
        cost = (4 * half * width_local * size, 2 * width_local * size)
        if j == 0:
            rows, keep, send = call(
                first_kernel,
                [((n_x * n_c * segment, width_local), bf16)] + outs,
                [chooser, chunks[0], *arrivals],
                cost=cost,
            )
        else:
            keep, send = call(later_kernel, outs, [rows, chunks[j]], cost=cost)
        got = shifted(send, "cfg", 1)
        own_sum, *sends = call(
            functools.partial(add_kernel, own),
            [((segment, size), f32)] + [((segment, size), jnp.int16)] * (n_x - 1),
            [keep, got],
        )
        parts += [own_sum] + [shifted(s_rows, "rows", s) for s, s_rows in enumerate(sends, 1)]
    *guided, stats = call(
        functools.partial(stats_kernel, len(starts), own),
        [((segment, size), f32) for size in sizes] + [((8, 128), f32)],
        parts,
    )
    all_stats = [stats] + [shifted(stats, "vocab", s) for s in range(1, n_z)]
    return pl.pallas_call(
        functools.partial(final_kernel, len(starts), segment),
        out_shape=jax.ShapeDtypeStruct((own, vocab), f32),
        in_specs=in_vmem(len(guided) + n_z),
        out_specs=pl.BlockSpec(memory_space=pltpu.VMEM),
        compiler_params=pltpu.CompilerParams(vmem_limit_bytes=16 * MIB),
    )(*keep_in_vmem(*guided, *all_stats))


def solution(mesh):
    placed = (
        P(None, ("groups", "vocab"), ("rows", "cfg")),
        P("groups"),
        P(("rows", "cfg")),
        P(("rows", "cfg"), "vocab"),
    )
    return jax.shard_map(
        per_device,
        mesh=mesh,
        in_specs=placed,
        out_specs=P(("groups", "rows", "cfg"), "vocab"),
        check_vma=False,
    )
```

```python
import functools

import jax
import jax.numpy as jnp
from jax import lax
from jax.experimental import pallas as pl
from jax.experimental.pallas import tpu as pltpu
from jax.sharding import PartitionSpec as P

epsilon = 1e-06
guidance = 2.0
TILE = 256
LANES = 128
MIB = 1 << 20


def in_vmem(count):
    return [pl.BlockSpec(memory_space=pltpu.VMEM)] * count


def keep_in_vmem(*arrays):
    return [pltpu.with_memory_space_constraint(a, pltpu.VMEM) for a in arrays]


def call(body, outs, args, far=(), limit=8, cost=None, **kwargs):
    return pl.pallas_call(
        body,
        out_shape=[pltpu.VMEM(shape, dtype) for shape, dtype in outs],
        in_specs=[pl.BlockSpec(memory_space=pltpu.HBM)] * len(far) + in_vmem(len(args)),
        out_specs=in_vmem(len(outs)),
        compiler_params=pltpu.CompilerParams(vmem_limit_bytes=limit * MIB),
        cost_estimate=cost and pl.CostEstimate(flops=cost[0], bytes_accessed=cost[1], transcendentals=0),
        **kwargs,
    )(*[pltpu.with_memory_space_constraint(a, pltpu.HBM) for a in far], *keep_in_vmem(*args))


def diagonal(n):
    return lax.broadcasted_iota(jnp.int32, (n, n), 0) == lax.broadcasted_iota(jnp.int32, (n, n), 1)


def as_column(row):
    return jnp.sum(jnp.where(diagonal(row.shape[1]), row, 0.0), axis=1, keepdims=True)


def as_row(column):
    return jnp.sum(jnp.where(diagonal(column.shape[0]), column, 0.0), axis=0, keepdims=True)


def squares_kernel(hidden_far, gain_far, normed_ref, out_ref, hidden_ref, gain_ref, sems):
    copies = [
        pltpu.make_async_copy(hidden_far.at[0], hidden_ref.at[0], sems.at[0]),
        pltpu.make_async_copy(hidden_far.at[1], hidden_ref.at[1], sems.at[1]),
        pltpu.make_async_copy(gain_far, gain_ref, sems.at[2]),
    ]
    for copy in copies:
        copy.start()
    for b in range(2):
        copies[b].wait()
        widened = hidden_ref[b].astype(jnp.float32)
        out_ref[b : b + 1] = as_row(jnp.sum(widened * widened, axis=1, keepdims=True))
    copies[2].wait()
    gain = gain_ref[...]
    for b in range(2):
        normed_ref[b] = (hidden_ref[b].astype(jnp.float32) * gain).astype(jnp.bfloat16)


def combine_kernel(width, normed_ref, totals_ref, *out_refs):
    inv_rms = lax.rsqrt(totals_ref[...] / width + epsilon)
    factor = [as_column((1.0 + guidance) * inv_rms[0:1]), as_column(guidance * inv_rms[1:2])]
    piece = out_refs[0].shape[0]
    for i, out_ref in enumerate(out_refs):
        rows = slice(i * piece, (i + 1) * piece)
        terms = [factor[b][rows] * normed_ref[b, rows, :].astype(jnp.float32) for b in range(2)]
        out_ref[...] = (terms[0] - terms[1]).astype(jnp.bfloat16)


def load_kernel(start, weights_far, *refs):
    *_, out_ref, tiles_ref, sems = refs
    size, slots = out_ref.shape[1], tiles_ref.shape[0]
    tiles = [(at, min(TILE, size - at)) for at in range(0, size, TILE)]
    copies = [
        pltpu.make_async_copy(
            weights_far.at[pl.ds(start + at, rows)],
            tiles_ref.at[i % slots, pl.ds(0, rows)],
            sems.at[i % slots],
        )
        for i, (at, rows) in enumerate(tiles)
    ]
    for copy in copies[:slots]:
        copy.start()
    for i, (at, rows) in enumerate(tiles):
        copies[i].wait()
        out_ref[:, at : at + rows] = tiles_ref[i % slots, :rows].T
        if i + slots < len(tiles):
            copies[i + slots].start()


def chooser_kernel(own, offsets, n_z, n_x, n_c, block, positions_ref, out_ref):
    z, x, c = (lax.axis_index(axis) for axis in ("vocab", "rows", "cfg"))
    masked = positions_ref.shape[1]
    segment = out_ref.shape[0] // (n_x * n_c)
    places = (positions_ref[...] + 1).astype(jnp.float32)
    i = lax.broadcasted_iota(jnp.int32, (segment, masked), 0)
    rank = lax.broadcasted_iota(jnp.int32, (segment, masked), 1)
    lane = lax.broadcasted_iota(jnp.int32, (segment, out_ref.shape[1]), 1)
    held = lane
    for k, offset in enumerate(offsets):
        moved = lane + (lax.rem(z - offset + n_z, n_z) - k) * block
        held = jnp.where(lane >= k * block, moved, held)
    for t in range(n_c):
        for s in range(n_x):
            owner = lax.rem(x + s, n_x) * n_c + lax.rem(c + t, n_c)
            match = (rank == owner * own + i) & (i < own)
            wanted = jnp.sum(jnp.where(match, places, 0.0), axis=1, keepdims=True).astype(jnp.int32) - 1
            at = (t * n_x + s) * segment
            out_ref[at : at + segment] = (wanted == held).astype(jnp.float32).astype(jnp.bfloat16)


def multiply(rows_ref, weights_ref, keep_ref, send_ref):
    half, width = keep_ref.shape
    for at in range(0, width, TILE):
        size = min(TILE, width - at)
        product = jnp.dot(
            rows_ref[...], weights_ref[:, at : at + size], preferred_element_type=jnp.float32
        )
        keep_ref[:, at : at + size] = product[:half]
        send_ref[:, at : at + size] = product[half:]


def first_kernel(chooser_ref, weights_ref, *refs):
    *block_refs, rows_ref, keep_ref, send_ref = refs
    blocks = jnp.concatenate([ref[...] for ref in block_refs], axis=0)
    rows_ref[...] = jnp.dot(chooser_ref[...], blocks, preferred_element_type=jnp.float32).astype(jnp.bfloat16)
    multiply(rows_ref, weights_ref, keep_ref, send_ref)


def later_kernel(rows_ref, weights_ref, keep_ref, send_ref):
    multiply(rows_ref, weights_ref, keep_ref, send_ref)


def lanes_diagonal(n):
    return lax.broadcasted_iota(jnp.int32, (n, LANES), 0) == lax.broadcasted_iota(jnp.int32, (n, LANES), 1)


def add_kernel(own, keep_ref, got_ref, own_ref, *out_refs):
    segment = own_ref.shape[0]
    own_ref[...] = keep_ref[:segment] + got_ref[:segment]
    for s, out_ref in enumerate(out_refs, 1):
        rows = slice(s * segment, (s + 1) * segment)
        value = keep_ref[rows] + got_ref[rows]
        peak = jnp.max(jnp.abs(value), axis=1, keepdims=True)
        exponent = jnp.clip(jnp.ceil(jnp.log2(jnp.maximum(peak, 1e-30))), -90.0, 127.0)
        scaled = jnp.clip(jnp.round(value * jnp.exp2(15.0 - exponent)), -32767.0, 32767.0)
        out_ref[:, LANES:] = scaled[:, LANES:].astype(jnp.int32).astype(jnp.int16)
        as_lanes = jnp.sum(jnp.where(lanes_diagonal(segment), exponent, 0.0), axis=0, keepdims=True)
        spare = lax.broadcasted_iota(jnp.int32, (segment, LANES), 0) == own
        out_ref[:, :LANES] = jnp.where(spare, as_lanes, scaled[:, :LANES]).astype(jnp.int32).astype(jnp.int16)


def restored(own, got_ref):
    value = got_ref[...].astype(jnp.int32).astype(jnp.float32)
    segment = value.shape[0]
    exponent = jnp.sum(
        jnp.where(lanes_diagonal(segment), value[own : own + 1, :LANES], 0.0), axis=1, keepdims=True
    )
    return value * jnp.exp2(exponent - 15.0)


def stats_kernel(chunks, own, *refs):
    ins, guided_refs, out_ref = refs[: -chunks - 1], refs[-chunks - 1 : -1], refs[-1]
    each = len(ins) // chunks
    top = None
    for j in range(chunks):
        guided = ins[j * each][...]
        for got in ins[j * each + 1 : (j + 1) * each]:
            guided = guided + restored(own, got)
        guided_refs[j][...] = guided
        peak = jnp.max(guided, axis=1, keepdims=True)
        top = peak if top is None else jnp.maximum(top, peak)
    total = sum(jnp.sum(jnp.exp(ref[...] - top), axis=1, keepdims=True) for ref in guided_refs)
    segment = top.shape[0]
    out_ref[0:1, :segment] = as_row(top)
    out_ref[1:2, :segment] = as_row(total)


def final_kernel(chunks, segment, *refs):
    guided_refs, stats, out_ref = refs[:chunks], refs[chunks:-1], refs[-1]
    top = functools.reduce(jnp.maximum, [ref[0:1, :segment] for ref in stats])
    total = sum(ref[1:2, :segment] * jnp.exp(ref[0:1, :segment] - top) for ref in stats)
    own = out_ref.shape[0]
    shift = as_column(top)[:own]
    log_total = as_column(jnp.log(total))[:own]
    at = 0
    for ref in guided_refs:
        out_ref[:, at : at + ref.shape[1]] = ref[:own] - shift - log_total
        at += ref.shape[1]


def shifted(value, axis, by):
    size = lax.axis_size(axis)
    return lax.ppermute(value, axis, [(i, (i + by) % size) for i in range(size)])


def chunk_starts(vocab):
    each = -(-vocab // (3 * TILE)) * TILE
    return list(range(0, vocab, each))


def per_device(final_hidden, positions, norm_gain, unembedding):
    bf16, f32 = jnp.bfloat16, jnp.float32
    _, block, width_local = final_hidden.shape
    masked = positions.shape[0]
    vocab = unembedding.shape[1]
    n_z, n_x, n_c = lax.axis_size("vocab"), lax.axis_size("rows"), lax.axis_size("cfg")
    z, x, c = lax.axis_index("vocab"), lax.axis_index("rows"), lax.axis_index("cfg")
    own = masked // (n_x * n_c)
    segment = -(-(own + 1) // 16) * 16

    normed, squares = call(
        squares_kernel,
        [((2, block, width_local), bf16), ((2, block), f32)],
        [],
        far=[final_hidden, norm_gain[None, :]],
        scratch_shapes=[
            pltpu.VMEM((2, block, width_local), bf16),
            pltpu.VMEM((1, width_local), f32),
            pltpu.SemaphoreType.DMA((3,)),
        ],
    )
    for axis in ("cfg", "rows"):
        squares = sum([shifted(squares, axis, s) for s in range(1, lax.axis_size(axis))], squares)
    (block_rows,) = call(
        functools.partial(combine_kernel, width_local * n_x * n_c),
        [((block, width_local), bf16)],
        [normed, squares],
    )

    starts = chunk_starts(vocab)
    sizes = [end - start for start, end in zip(starts, starts[1:] + [vocab])]
    weights = unembedding.T
    chunks = []

    def load(after):
        nonlocal weights
        if len(chunks) == len(sizes):
            return after
        start, size = starts[len(chunks)], sizes[len(chunks)]
        weights, after = lax.optimization_barrier((weights, after))
        (chunk,) = call(
            functools.partial(load_kernel, start),
            [((width_local, size), bf16)],
            [],
            far=[weights],
            cost=(0, 2 * size * width_local),
            scratch_shapes=[pltpu.VMEM((3, TILE, width_local), bf16), pltpu.SemaphoreType.DMA((3,))],
        )
        chunk, after = lax.optimization_barrier((chunk, after))
        chunks.append(chunk)
        return after

    arrivals, offsets = [block_rows], [0]
    ahead = shifted(block_rows, "vocab", 1)
    behind = load(block_rows)
    for step in range(1, n_z // 2 + 1):
        if step > 1:
            ahead = shifted(ahead, "vocab", 1)
        arrivals.append(ahead)
        offsets.append(step)
        if 2 * step < n_z:
            behind = shifted(behind, "vocab", -1)
            arrivals.append(behind)
            offsets.append(-step)
        if step == 1:
            chunks[-1], ahead = lax.optimization_barrier((chunks[-1], ahead))
    while len(chunks) < len(sizes):
        load(arrivals[1])
    (chooser,) = call(
        functools.partial(chooser_kernel, own, offsets, n_z, n_x, n_c, block),
        [((n_x * n_c * segment, n_z * block), bf16)],
        [lax.optimization_barrier((positions[None, :], chunks[0]))[0]],
    )
    chooser, *chunks = lax.optimization_barrier((chooser, *chunks))

    half = n_x * segment
    parts, leaving = [], []
    for j, size in enumerate(sizes):
        outs = [((half, size), f32)] * 2
        cost = (4 * half * width_local * size, 2 * width_local * size)
        if j == 0:
            rows, keep, send = call(
                first_kernel,
                [((n_x * n_c * segment, width_local), bf16)] + outs,
                [chooser, chunks[0], *arrivals],
                cost=cost,
            )
        else:
            if j > 1:
                rows, leaving[j - 2] = lax.optimization_barrier((rows, leaving[j - 2]))
            keep, send = call(later_kernel, outs, [rows, chunks[j]], cost=cost)
        got = shifted(send, "cfg", 1)
        own_sum, *sends = call(
            functools.partial(add_kernel, own),
            [((segment, size), f32)] + [((segment, size), jnp.int16)] * (n_x - 1),
            [keep, got],
        )
        parts.append(own_sum)
        leaving.append(sends)
    arrived = [[shifted(s_rows, "rows", s) for s, s_rows in enumerate(sends, 1)] for sends in leaving]
    parts = [part for own_sum, got in zip(parts, arrived) for part in (own_sum, *got)]
    *guided, stats = call(
        functools.partial(stats_kernel, len(starts), own),
        [((segment, size), f32) for size in sizes] + [((8, 128), f32)],
        parts,
    )
    all_stats = [stats] + [shifted(stats, "vocab", s) for s in range(1, n_z)]
    return pl.pallas_call(
        functools.partial(final_kernel, len(starts), segment),
        out_shape=jax.ShapeDtypeStruct((own, vocab), f32),
        in_specs=in_vmem(len(guided) + n_z),
        out_specs=pl.BlockSpec(memory_space=pltpu.VMEM),
        compiler_params=pltpu.CompilerParams(vmem_limit_bytes=16 * MIB),
    )(*keep_in_vmem(*guided, *all_stats))


def solution(mesh):
    placed = (
        P(None, ("groups", "vocab"), ("rows", "cfg")),
        P("groups"),
        P(("rows", "cfg")),
        P(("rows", "cfg"), "vocab"),
    )
    return jax.shard_map(
        per_device,
        mesh=mesh,
        in_specs=placed,
        out_specs=P(("groups", "rows", "cfg"), "vocab"),
        check_vma=False,
    )
```

```python
import functools

import jax
import jax.numpy as jnp
from jax import lax
from jax.experimental import pallas as pl
from jax.experimental.pallas import tpu as pltpu
from jax.sharding import PartitionSpec as P

epsilon = 1e-06
guidance = 2.0
TILE = 256
LANES = 128
MIB = 1 << 20
LOADS = (5, 3, 5)
LOADS_BEHIND = 1
LOADS_AHEAD = 1
CHUNKS = (10,)


def in_vmem(count):
    return [pl.BlockSpec(memory_space=pltpu.VMEM)] * count


def keep_in_vmem(*arrays):
    return [pltpu.with_memory_space_constraint(a, pltpu.VMEM) for a in arrays]


def call(body, outs, args, far=(), limit=8, cost=None, **kwargs):
    return pl.pallas_call(
        body,
        out_shape=[pltpu.VMEM(shape, dtype) for shape, dtype in outs],
        in_specs=[pl.BlockSpec(memory_space=pltpu.HBM)] * len(far) + in_vmem(len(args)),
        out_specs=in_vmem(len(outs)),
        compiler_params=pltpu.CompilerParams(vmem_limit_bytes=limit * MIB),
        cost_estimate=cost and pl.CostEstimate(flops=cost[0], bytes_accessed=cost[1], transcendentals=0),
        **kwargs,
    )(*[pltpu.with_memory_space_constraint(a, pltpu.HBM) for a in far], *keep_in_vmem(*args))


def diagonal(n):
    return lax.broadcasted_iota(jnp.int32, (n, n), 0) == lax.broadcasted_iota(jnp.int32, (n, n), 1)


def as_column(row):
    return jnp.sum(jnp.where(diagonal(row.shape[1]), row, 0.0), axis=1, keepdims=True)


def as_row(column):
    return jnp.sum(jnp.where(diagonal(column.shape[0]), column, 0.0), axis=0, keepdims=True)


def squares_kernel(hidden_far, gain_far, normed_ref, out_ref, hidden_ref, gain_ref, sems):
    copies = [
        pltpu.make_async_copy(hidden_far.at[0], hidden_ref.at[0], sems.at[0]),
        pltpu.make_async_copy(hidden_far.at[1], hidden_ref.at[1], sems.at[1]),
        pltpu.make_async_copy(gain_far, gain_ref, sems.at[2]),
    ]
    for copy in copies:
        copy.start()
    for b in range(2):
        copies[b].wait()
        widened = hidden_ref[b].astype(jnp.float32)
        out_ref[b : b + 1] = as_row(jnp.sum(widened * widened, axis=1, keepdims=True))
    copies[2].wait()
    gain = gain_ref[...]
    for b in range(2):
        normed_ref[b] = (hidden_ref[b].astype(jnp.float32) * gain).astype(jnp.bfloat16)


def combine_kernel(width, normed_ref, totals_ref, *out_refs):
    inv_rms = lax.rsqrt(totals_ref[...] / width + epsilon)
    factor = [as_column((1.0 + guidance) * inv_rms[0:1]), as_column(guidance * inv_rms[1:2])]
    piece = out_refs[0].shape[0]
    for i, out_ref in enumerate(out_refs):
        rows = slice(i * piece, (i + 1) * piece)
        terms = [factor[b][rows] * normed_ref[b, rows, :].astype(jnp.float32) for b in range(2)]
        out_ref[...] = (terms[0] - terms[1]).astype(jnp.bfloat16)


def load_kernel(start, weights_far, *refs):
    *_, out_ref, tiles_ref, sems = refs
    size, slots = out_ref.shape[1], tiles_ref.shape[0]
    tiles = [(at, min(TILE, size - at)) for at in range(0, size, TILE)]
    copies = [
        pltpu.make_async_copy(
            weights_far.at[pl.ds(start + at, rows)],
            tiles_ref.at[i % slots, pl.ds(0, rows)],
            sems.at[i % slots],
        )
        for i, (at, rows) in enumerate(tiles)
    ]
    for copy in copies[:slots]:
        copy.start()
    for i, (at, rows) in enumerate(tiles):
        copies[i].wait()
        out_ref[:, at : at + rows] = tiles_ref[i % slots, :rows].T
        if i + slots < len(tiles):
            copies[i + slots].start()


def chooser_kernel(own, offsets, n_z, n_x, n_c, block, positions_ref, out_ref):
    z, x, c = (lax.axis_index(axis) for axis in ("vocab", "rows", "cfg"))
    masked = positions_ref.shape[1]
    segment = out_ref.shape[0] // (n_x * n_c)
    places = (positions_ref[...] + 1).astype(jnp.float32)
    i = lax.broadcasted_iota(jnp.int32, (segment, masked), 0)
    rank = lax.broadcasted_iota(jnp.int32, (segment, masked), 1)
    lane = lax.broadcasted_iota(jnp.int32, (segment, out_ref.shape[1]), 1)
    held = lane
    for k, offset in enumerate(offsets):
        moved = lane + (lax.rem(z - offset + n_z, n_z) - k) * block
        held = jnp.where(lane >= k * block, moved, held)
    for t in range(n_c):
        for s in range(n_x):
            owner = lax.rem(x + s, n_x) * n_c + lax.rem(c + t, n_c)
            match = (rank == owner * own + i) & (i < own)
            wanted = jnp.sum(jnp.where(match, places, 0.0), axis=1, keepdims=True).astype(jnp.int32) - 1
            at = (t * n_x + s) * segment
            out_ref[at : at + segment] = (wanted == held).astype(jnp.float32).astype(jnp.bfloat16)


def multiply(start, rows_ref, weights_refs, keep_ref, send_ref):
    half, width = keep_ref.shape
    at, skip = 0, start
    for ref in weights_refs:
        held = ref.shape[1]
        while at < width and skip < held:
            size = min(TILE, width - at, held - skip)
            product = jnp.dot(rows_ref[...], ref[:, skip : skip + size], preferred_element_type=jnp.float32)
            keep_ref[:, at : at + size] = product[:half]
            send_ref[:, at : at + size] = product[half:]
            at, skip = at + size, skip + size
        skip = max(0, skip - held)


def first_kernel(start, loads, chooser_ref, *refs):
    weights_refs, block_refs, (rows_ref, keep_ref, send_ref) = refs[:loads], refs[loads:-3], refs[-3:]
    blocks = jnp.concatenate([ref[...] for ref in block_refs], axis=0)
    rows_ref[...] = jnp.dot(chooser_ref[...], blocks, preferred_element_type=jnp.float32).astype(jnp.bfloat16)
    multiply(start, rows_ref, weights_refs, keep_ref, send_ref)


def later_kernel(start, rows_ref, *refs):
    *weights_refs, keep_ref, send_ref = refs
    multiply(start, rows_ref, weights_refs, keep_ref, send_ref)


def lanes_diagonal(n):
    return lax.broadcasted_iota(jnp.int32, (n, LANES), 0) == lax.broadcasted_iota(jnp.int32, (n, LANES), 1)


def add_kernel(own, keep_ref, got_ref, own_ref, *out_refs):
    segment = own_ref.shape[0]
    own_ref[...] = keep_ref[:segment] + got_ref[:segment]
    for s, out_ref in enumerate(out_refs, 1):
        rows = slice(s * segment, (s + 1) * segment)
        value = keep_ref[rows] + got_ref[rows]
        peak = jnp.max(jnp.abs(value), axis=1, keepdims=True)
        exponent = jnp.clip(jnp.ceil(jnp.log2(jnp.maximum(peak, 1e-30))), -90.0, 127.0)
        scaled = jnp.clip(jnp.round(value * jnp.exp2(15.0 - exponent)), -32767.0, 32767.0)
        out_ref[:, LANES:] = scaled[:, LANES:].astype(jnp.int32).astype(jnp.int16)
        as_lanes = jnp.sum(jnp.where(lanes_diagonal(segment), exponent, 0.0), axis=0, keepdims=True)
        spare = lax.broadcasted_iota(jnp.int32, (segment, LANES), 0) == own
        out_ref[:, :LANES] = jnp.where(spare, as_lanes, scaled[:, :LANES]).astype(jnp.int32).astype(jnp.int16)


def restored(own, got_ref):
    value = got_ref[...].astype(jnp.int32).astype(jnp.float32)
    segment = value.shape[0]
    exponent = jnp.sum(
        jnp.where(lanes_diagonal(segment), value[own : own + 1, :LANES], 0.0), axis=1, keepdims=True
    )
    return value * jnp.exp2(exponent - 15.0)


def stats_kernel(own, *refs):
    *in_refs, guided_ref, out_ref = refs
    before = in_refs.pop(0) if in_refs[0].shape == out_ref.shape else None
    guided = in_refs[0][...]
    for got in in_refs[1:]:
        guided = guided + restored(own, got)
    guided_ref[...] = guided
    segment = guided.shape[0]
    top = jnp.max(guided, axis=1, keepdims=True)
    if before is not None:
        earlier = as_column(before[0:1, :segment])
        top = jnp.maximum(top, earlier)
    total = jnp.sum(jnp.exp(guided - top), axis=1, keepdims=True)
    if before is not None:
        total = total + as_column(before[1:2, :segment]) * jnp.exp(earlier - top)
    out_ref[0:1, :segment] = as_row(top)
    out_ref[1:2, :segment] = as_row(total)


def final_kernel(chunks, segment, *refs):
    guided_refs, stats, out_ref = refs[:chunks], refs[chunks:-1], refs[-1]
    top = functools.reduce(jnp.maximum, [ref[0:1, :segment] for ref in stats])
    total = sum(ref[1:2, :segment] * jnp.exp(ref[0:1, :segment] - top) for ref in stats)
    own = out_ref.shape[0]
    shift = as_column(top)[:own]
    log_total = as_column(jnp.log(total))[:own]
    at = 0
    for ref in guided_refs:
        out_ref[:, at : at + ref.shape[1]] = ref[:own] - shift - log_total
        at += ref.shape[1]


def shifted(value, axis, by):
    size = lax.axis_size(axis)
    return lax.ppermute(value, axis, [(i, (i + by) % size) for i in range(size)])


def cut(vocab, tiles):
    edges = [0]
    for count in tiles:
        edges.append(min(vocab, edges[-1] + count * TILE))
    edges.append(vocab)
    return [(start, end - start) for start, end in zip(edges, edges[1:]) if end > start]


def per_device(final_hidden, positions, norm_gain, unembedding):
    bf16, f32 = jnp.bfloat16, jnp.float32
    _, block, width_local = final_hidden.shape
    masked = positions.shape[0]
    vocab = unembedding.shape[1]
    n_z, n_x, n_c = lax.axis_size("vocab"), lax.axis_size("rows"), lax.axis_size("cfg")
    z, x, c = lax.axis_index("vocab"), lax.axis_index("rows"), lax.axis_index("cfg")
    own = masked // (n_x * n_c)
    segment = -(-(own + 1) // 16) * 16

    normed, squares = call(
        squares_kernel,
        [((2, block, width_local), bf16), ((2, block), f32)],
        [],
        far=[final_hidden, norm_gain[None, :]],
        scratch_shapes=[
            pltpu.VMEM((2, block, width_local), bf16),
            pltpu.VMEM((1, width_local), f32),
            pltpu.SemaphoreType.DMA((3,)),
        ],
    )
    for axis in ("cfg", "rows"):
        squares = sum([shifted(squares, axis, s) for s in range(1, lax.axis_size(axis))], squares)
    (block_rows,) = call(
        functools.partial(combine_kernel, width_local * n_x * n_c),
        [((block, width_local), bf16)],
        [normed, squares],
    )

    weights = unembedding.T
    loads, loaded = cut(vocab, LOADS), []

    def load(count, after):
        nonlocal weights
        for start, size in loads[len(loaded) : len(loaded) + count]:
            weights, after = lax.optimization_barrier((weights, after))
            (piece,) = call(
                functools.partial(load_kernel, start),
                [((width_local, size), bf16)],
                [],
                far=[weights],
                cost=(0, 2 * size * width_local),
                scratch_shapes=[pltpu.VMEM((3, TILE, width_local), bf16), pltpu.SemaphoreType.DMA((3,))],
            )
            piece, after = lax.optimization_barrier((piece, after))
            loaded.append(piece)
        return after

    ahead = shifted(block_rows, "vocab", 1)
    arrivals, offsets = [block_rows, ahead], [0, 1]
    behind = load(LOADS_BEHIND, block_rows)
    for step in range(1, (n_z - 1) // 2 + 1):
        behind = shifted(behind, "vocab", -1)
        arrivals.append(behind)
        offsets.append(-step)
    if LOADS_AHEAD:
        load(LOADS_AHEAD, loaded[-1] if loaded else block_rows)
        ahead, loaded[-1] = lax.optimization_barrier((ahead, loaded[-1]))
    load_after = ahead
    for step in range(2, n_z // 2 + 1):
        ahead = shifted(ahead, "vocab", 1)
        arrivals.append(ahead)
        offsets.append(step)
    load(len(loads), load_after)
    (chooser,) = call(
        functools.partial(chooser_kernel, own, offsets, n_z, n_x, n_c, block),
        [((n_x * n_c * segment, n_z * block), bf16)],
        [lax.optimization_barrier((positions[None, :], loaded[0]))[0]],
    )
    chooser, *loaded = lax.optimization_barrier((chooser, *loaded))

    half = n_x * segment
    chunks = cut(vocab, CHUNKS)
    parts, leaving = [], []
    for j, (start, size) in enumerate(chunks):
        outs = [((half, size), f32)] * 2
        cost = (4 * half * width_local * size, 2 * width_local * size)
        needed = [i for i, (at, held) in enumerate(loads) if at < start + size and start < at + held]
        skip = start - loads[needed[0]][0]
        pieces = [loaded[i] for i in needed]
        if j == 0:
            rows, keep, send = call(
                functools.partial(first_kernel, skip, len(pieces)),
                [((n_x * n_c * segment, width_local), bf16)] + outs,
                [chooser, *pieces, *arrivals],
                cost=cost,
            )
        else:
            keep, send = call(functools.partial(later_kernel, skip), outs, [rows, *pieces], cost=cost)
        got = shifted(send, "cfg", 1)
        own_sum, *sends = call(
            functools.partial(add_kernel, own),
            [((segment, size), f32)] + [((segment, size), jnp.int16)] * (n_x - 1),
            [keep, got],
        )
        parts.append(own_sum)
        leaving.append(sends)
    guided, stats = [], None
    for own_sum, sends in zip(parts, leaving):
        got = [shifted(s_rows, "rows", s) for s, s_rows in enumerate(sends, 1)]
        chunk, stats = call(
            functools.partial(stats_kernel, own),
            [(own_sum.shape, f32), ((8, LANES), f32)],
            ([] if stats is None else [stats]) + [own_sum, *got],
        )
        guided.append(chunk)
    all_stats = [stats] + [shifted(stats, "vocab", s) for s in range(1, n_z)]
    return pl.pallas_call(
        functools.partial(final_kernel, len(chunks), segment),
        out_shape=jax.ShapeDtypeStruct((own, vocab), f32),
        in_specs=in_vmem(len(guided) + n_z),
        out_specs=pl.BlockSpec(memory_space=pltpu.VMEM),
        compiler_params=pltpu.CompilerParams(vmem_limit_bytes=16 * MIB),
    )(*keep_in_vmem(*guided, *all_stats))


def solution(mesh):
    placed = (
        P(None, ("groups", "vocab"), ("rows", "cfg")),
        P("groups"),
        P(("rows", "cfg")),
        P(("rows", "cfg"), "vocab"),
    )
    return jax.shard_map(
        per_device,
        mesh=mesh,
        in_specs=placed,
        out_specs=P(("groups", "rows", "cfg"), "vocab"),
        check_vma=False,
    )
```

```python
import functools

import jax
import jax.numpy as jnp
from jax import lax
from jax.experimental import pallas as pl
from jax.experimental.pallas import tpu as pltpu
from jax.sharding import PartitionSpec as P

epsilon = 1e-06
guidance = 2.0
TILE = 256
LANES = 128
MIB = 1 << 20
LOADS = (1280, 512, 704, 1280)
LOADS_BEHIND = 1
LOADS_AHEAD = 1
CHUNKS = (2496,)
ROWS = 8


def in_vmem(count):
    return [pl.BlockSpec(memory_space=pltpu.VMEM)] * count


def keep_in_vmem(*arrays):
    return [pltpu.with_memory_space_constraint(a, pltpu.VMEM) for a in arrays]


def call(body, outs, args, far=(), limit=8, cost=None, **kwargs):
    return pl.pallas_call(
        body,
        out_shape=[pltpu.VMEM(shape, dtype) for shape, dtype in outs],
        in_specs=[pl.BlockSpec(memory_space=pltpu.HBM)] * len(far) + in_vmem(len(args)),
        out_specs=in_vmem(len(outs)),
        compiler_params=pltpu.CompilerParams(vmem_limit_bytes=limit * MIB),
        cost_estimate=cost and pl.CostEstimate(flops=cost[0], bytes_accessed=cost[1], transcendentals=0),
        **kwargs,
    )(*[pltpu.with_memory_space_constraint(a, pltpu.HBM) for a in far], *keep_in_vmem(*args))


def diagonal(n):
    return lax.broadcasted_iota(jnp.int32, (n, n), 0) == lax.broadcasted_iota(jnp.int32, (n, n), 1)


def as_column(row):
    return jnp.sum(jnp.where(diagonal(row.shape[1]), row, 0.0), axis=1, keepdims=True)


def as_row(column):
    return jnp.sum(jnp.where(diagonal(column.shape[0]), column, 0.0), axis=0, keepdims=True)


def squares_kernel(hidden_far, gain_far, normed_ref, out_ref, hidden_ref, gain_ref, sems):
    copies = [
        pltpu.make_async_copy(hidden_far.at[0], hidden_ref.at[0], sems.at[0]),
        pltpu.make_async_copy(hidden_far.at[1], hidden_ref.at[1], sems.at[1]),
        pltpu.make_async_copy(gain_far, gain_ref, sems.at[2]),
    ]
    for copy in copies:
        copy.start()
    for b in range(2):
        copies[b].wait()
        widened = hidden_ref[b].astype(jnp.float32)
        out_ref[b : b + 1] = as_row(jnp.sum(widened * widened, axis=1, keepdims=True))
    copies[2].wait()
    gain = gain_ref[...]
    for b in range(2):
        normed_ref[b] = (hidden_ref[b].astype(jnp.float32) * gain).astype(jnp.bfloat16)


def combine_kernel(width, normed_ref, totals_ref, *out_refs):
    inv_rms = lax.rsqrt(totals_ref[...] / width + epsilon)
    factor = [as_column((1.0 + guidance) * inv_rms[0:1]), as_column(guidance * inv_rms[1:2])]
    piece = out_refs[0].shape[0]
    for i, out_ref in enumerate(out_refs):
        rows = slice(i * piece, (i + 1) * piece)
        terms = [factor[b][rows] * normed_ref[b, rows, :].astype(jnp.float32) for b in range(2)]
        out_ref[...] = (terms[0] - terms[1]).astype(jnp.bfloat16)


def load_kernel(start, weights_far, *refs):
    *_, out_ref, tiles_ref, sems = refs
    size, slots = out_ref.shape[1], tiles_ref.shape[0]
    tiles = [(at, min(TILE, size - at)) for at in range(0, size, TILE)]
    copies = [
        pltpu.make_async_copy(
            weights_far.at[pl.ds(start + at, rows)],
            tiles_ref.at[i % slots, pl.ds(0, rows)],
            sems.at[i % slots],
        )
        for i, (at, rows) in enumerate(tiles)
    ]
    for copy in copies[:slots]:
        copy.start()
    for i, (at, rows) in enumerate(tiles):
        copies[i].wait()
        out_ref[:, at : at + rows] = tiles_ref[i % slots, :rows].T
        if i + slots < len(tiles):
            copies[i + slots].start()


def chooser_kernel(own, offsets, n_z, n_x, n_c, block, positions_ref, out_ref):
    z, x, c = (lax.axis_index(axis) for axis in ("vocab", "rows", "cfg"))
    masked = positions_ref.shape[1]
    segment = out_ref.shape[0] // (n_x * n_c)
    places = (positions_ref[...] + 1).astype(jnp.float32)
    i = lax.broadcasted_iota(jnp.int32, (segment, masked), 0)
    rank = lax.broadcasted_iota(jnp.int32, (segment, masked), 1)
    lane = lax.broadcasted_iota(jnp.int32, (segment, out_ref.shape[1]), 1)
    held = lane
    for k, offset in enumerate(offsets):
        moved = lane + (lax.rem(z - offset + n_z, n_z) - k) * block
        held = jnp.where(lane >= k * block, moved, held)
    for t in range(n_c):
        for s in range(n_x):
            owner = lax.rem(x + s, n_x) * n_c + lax.rem(c + t, n_c)
            match = (rank == owner * own + i) & (i < own)
            wanted = jnp.sum(jnp.where(match, places, 0.0), axis=1, keepdims=True).astype(jnp.int32) - 1
            at = (t * n_x + s) * segment
            out_ref[at : at + segment] = (wanted == held).astype(jnp.float32).astype(jnp.bfloat16)


def multiply(start, size, rows_ref, weights_refs, keep_ref, send_ref):
    half, width = keep_ref.shape
    at, skip = 0, start
    for ref in weights_refs:
        held = ref.shape[1]
        while at < size and skip < held:
            step = min(TILE, size - at, held - skip)
            product = jnp.dot(rows_ref[...], ref[:, skip : skip + step], preferred_element_type=jnp.float32)
            keep_ref[:, at : at + step] = product[:half]
            send_ref[:, at : at + step] = product[half:]
            at, skip = at + step, skip + step
        skip = max(0, skip - held)
    for ref in (keep_ref, send_ref):
        ref[:, size:] = jnp.zeros((half, width - size), jnp.float32)


def first_kernel(start, size, loads, chooser_ref, *refs):
    weights_refs, block_refs, (rows_ref, keep_ref, send_ref) = refs[:loads], refs[loads:-3], refs[-3:]
    blocks = jnp.concatenate([ref[...] for ref in block_refs], axis=0)
    rows_ref[...] = jnp.dot(chooser_ref[...], blocks, preferred_element_type=jnp.float32).astype(jnp.bfloat16)
    multiply(start, size, rows_ref, weights_refs, keep_ref, send_ref)


def later_kernel(start, size, rows_ref, *refs):
    *weights_refs, keep_ref, send_ref = refs
    multiply(start, size, rows_ref, weights_refs, keep_ref, send_ref)


def add_kernel(own, size, keep_ref, got_ref, own_ref, *out_refs):
    segment, width = own_ref.shape
    own_ref[...] = keep_ref[:segment] + got_ref[:segment]
    last = width - TILE
    spare = lax.broadcasted_iota(jnp.int32, (ROWS, TILE), 1) >= size - last
    for s, out_ref in enumerate(out_refs, 1):
        for t in range(-(-own // ROWS)):
            rows = slice(s * segment + t * ROWS, s * segment + (t + 1) * ROWS)
            value = keep_ref[rows] + got_ref[rows]
            peak = jnp.max(jnp.abs(value), axis=1, keepdims=True)
            exponent = jnp.clip(jnp.ceil(jnp.log2(jnp.maximum(peak, 1e-30))), -90.0, 127.0)
            scaled = jnp.clip(jnp.round(value * jnp.exp2(15.0 - exponent)), -32767.0, 32767.0)
            ending = jnp.where(spare, exponent, scaled[:, last:])
            scaled = jnp.concatenate([scaled[:, :last], ending], axis=1) if last else ending
            if own - t * ROWS <= ROWS // 2:
                half = ROWS // 2
                scaled = jnp.concatenate([scaled[:half, : width // 2], scaled[:half, width // 2 :]], axis=0)
            out_ref[:, t * width : t * width + scaled.shape[1]] = scaled.astype(jnp.int32).astype(jnp.int16)


def restored(own, size, width, got_ref, t):
    half = own - t * ROWS <= ROWS // 2
    value = got_ref[:, t * width : t * width + (width // 2 if half else width)]
    value = value.astype(jnp.int32).astype(jnp.float32)
    if half:
        value = jnp.concatenate([value[: ROWS // 2], value[ROWS // 2 :]], axis=1)
        value = jnp.concatenate([value, jnp.zeros_like(value)], axis=0)
    return value * jnp.exp2(value[:, size : size + 1] - 15.0)


def stats_kernel(own, size, *refs):
    *in_refs, guided_ref, out_ref = refs
    before = in_refs.pop(0) if in_refs[0].shape == out_ref.shape else None
    segment, width = guided_ref.shape
    real = lax.broadcasted_iota(jnp.int32, (ROWS, width), 1) < size
    tops, totals = [], []
    for t in range(segment // ROWS):
        rows = slice(t * ROWS, (t + 1) * ROWS)
        guided = in_refs[0][rows]
        if t * ROWS < own:
            for got in in_refs[1:]:
                guided = guided + restored(own, size, width, got, t)
        guided_ref[rows] = guided
        top = jnp.max(jnp.where(real, guided, -jnp.inf), axis=1, keepdims=True)
        tops.append(top)
        totals.append(jnp.sum(jnp.where(real, jnp.exp(guided - top), 0.0), axis=1, keepdims=True))
    top, total = as_row(jnp.concatenate(tops, axis=0)), as_row(jnp.concatenate(totals, axis=0))
    if before is not None:
        top, total = merged((top, total), (before[0:1, :segment], before[1:2, :segment]))
    out_ref[0:1, :segment] = top
    out_ref[1:2, :segment] = total


def merged(one, other):
    top = jnp.maximum(one[0], other[0])
    return top, one[1] * jnp.exp(one[0] - top) + other[1] * jnp.exp(other[0] - top)


def merge_kernel(one_ref, *refs):
    *other_refs, out_ref = refs
    top, total = one_ref[0:1], one_ref[1:2]
    for ref in other_refs:
        top, total = merged((top, total), (ref[0:1], ref[1:2]))
    out_ref[0:1] = top
    out_ref[1:2] = total


def final_kernel(sizes, segment, *refs):
    guided_refs, stats, (out_far, out_ref, sems) = refs[: len(sizes)], refs[len(sizes) : -3], refs[-3:]
    top, total = stats[0][0:1, :segment], stats[0][1:2, :segment]
    for ref in stats[1:]:
        top, total = merged((top, total), (ref[0:1, :segment], ref[1:2, :segment]))
    own = out_ref.shape[0]
    shift, log_total = as_column(top), as_column(jnp.log(total))
    copies = []
    for t, first in enumerate(range(0, own, ROWS)):
        rows = slice(first, min(first + ROWS, own))
        at = 0
        for ref, size in zip(guided_refs, sizes):
            out_ref[rows, at : at + size] = ref[rows, :size] - shift[rows] - log_total[rows]
            at += size
        copies.append(pltpu.make_async_copy(out_ref.at[rows], out_far.at[rows], sems.at[t]))
        copies[-1].start()
    for copy in copies:
        copy.wait()


def shifted(value, axis, by):
    size = lax.axis_size(axis)
    return lax.ppermute(value, axis, [(i, (i + by) % size) for i in range(size)])


def cut(vocab, widths):
    edges = [0]
    for width in widths:
        edges.append(min(vocab, edges[-1] + width))
    edges.append(vocab)
    return [(start, end - start) for start, end in zip(edges, edges[1:]) if end > start]


def padded(size):
    return -(-(size + 1) // TILE) * TILE


def packed_shape(own, width):
    blocks, rest = divmod(own, ROWS)
    lanes = blocks * width + (0 if rest == 0 else width // 2 if rest <= ROWS // 2 else width)
    return (ROWS, lanes)


def per_device(final_hidden, positions, norm_gain, unembedding):
    bf16, f32 = jnp.bfloat16, jnp.float32
    _, block, width_local = final_hidden.shape
    masked = positions.shape[0]
    vocab = unembedding.shape[1]
    n_z, n_x, n_c = lax.axis_size("vocab"), lax.axis_size("rows"), lax.axis_size("cfg")
    z, x, c = lax.axis_index("vocab"), lax.axis_index("rows"), lax.axis_index("cfg")
    own = masked // (n_x * n_c)
    segment = -(-(own + 1) // 16) * 16

    normed, squares = call(
        squares_kernel,
        [((2, block, width_local), bf16), ((2, block), f32)],
        [],
        far=[final_hidden, norm_gain[None, :]],
        scratch_shapes=[
            pltpu.VMEM((2, block, width_local), bf16),
            pltpu.VMEM((1, width_local), f32),
            pltpu.SemaphoreType.DMA((3,)),
        ],
    )
    for axis in ("cfg", "rows"):
        squares = sum([shifted(squares, axis, s) for s in range(1, lax.axis_size(axis))], squares)
    (block_rows,) = call(
        functools.partial(combine_kernel, width_local * n_x * n_c),
        [((block, width_local), bf16)],
        [normed, squares],
    )

    weights = unembedding.T
    loads, loaded = cut(vocab, LOADS), []

    def load(count, after):
        nonlocal weights
        for start, size in loads[len(loaded) : len(loaded) + count]:
            weights, after = lax.optimization_barrier((weights, after))
            (piece,) = call(
                functools.partial(load_kernel, start),
                [((width_local, size), bf16)],
                [],
                far=[weights],
                cost=(0, 2 * size * width_local),
                scratch_shapes=[pltpu.VMEM((3, TILE, width_local), bf16), pltpu.SemaphoreType.DMA((3,))],
            )
            piece, after = lax.optimization_barrier((piece, after))
            loaded.append(piece)
        return after

    ahead = shifted(block_rows, "vocab", 1)
    arrivals, offsets = [block_rows, ahead], [0, 1]
    behind = load(LOADS_BEHIND, block_rows)
    for step in range(1, (n_z - 1) // 2 + 1):
        behind = shifted(behind, "vocab", -1)
        arrivals.append(behind)
        offsets.append(-step)
    if LOADS_AHEAD:
        load(LOADS_AHEAD, loaded[-1] if loaded else block_rows)
        ahead, loaded[-1] = lax.optimization_barrier((ahead, loaded[-1]))
    load_after = ahead
    for step in range(2, n_z // 2 + 1):
        ahead = shifted(ahead, "vocab", 1)
        arrivals.append(ahead)
        offsets.append(step)
    load(len(loads), load_after)
    (chooser,) = call(
        functools.partial(chooser_kernel, own, offsets, n_z, n_x, n_c, block),
        [((n_x * n_c * segment, n_z * block), bf16)],
        [lax.optimization_barrier((positions[None, :], loaded[0]))[0]],
    )
    chooser, *loaded = lax.optimization_barrier((chooser, *loaded))

    half = n_x * segment
    chunks = cut(vocab, CHUNKS)
    parts, leaving = [], []
    for j, (start, size) in enumerate(chunks):
        width = padded(size)
        outs = [((half, width), f32)] * 2
        cost = (4 * half * width_local * size, 2 * width_local * size)
        needed = [i for i, (at, held) in enumerate(loads) if at < start + size and start < at + held]
        skip = start - loads[needed[0]][0]
        pieces = [loaded[i] for i in needed]
        if j == 0:
            rows, keep, send = call(
                functools.partial(first_kernel, skip, size, len(pieces)),
                [((n_x * n_c * segment, width_local), bf16)] + outs,
                [chooser, *pieces, *arrivals],
                cost=cost,
            )
        else:
            keep, send = call(functools.partial(later_kernel, skip, size), outs, [rows, *pieces], cost=cost)
        got = shifted(send, "cfg", 1)
        own_sum, *sends = call(
            functools.partial(add_kernel, own, size),
            [((segment, width), f32)] + [(packed_shape(own, width), jnp.int16)] * (n_x - 1),
            [keep, got],
        )
        parts.append(own_sum)
        leaving.append(sends)
    guided, stats = [], None
    for (_, size), own_sum, sends in zip(chunks, parts, leaving):
        got = [shifted(s_rows, "rows", s) for s, s_rows in enumerate(sends, 1)]
        chunk, stats = call(
            functools.partial(stats_kernel, own, size),
            [(own_sum.shape, f32), ((2, LANES), f32)],
            ([] if stats is None else [stats]) + [own_sum, *got],
        )
        guided.append(chunk)
    if n_z & (n_z - 1) == 0:
        all_stats = [stats] + [
            lax.ppermute(stats, "vocab", [(i, i ^ far) for i in range(n_z)]) for far in range(1, n_z)
        ]
    else:
        all_stats = [stats] + [shifted(stats, "vocab", s) for s in range(1, n_z)]
    return pl.pallas_call(
        functools.partial(final_kernel, [size for _, size in chunks], segment),
        out_shape=jax.ShapeDtypeStruct((own, vocab), f32),
        in_specs=in_vmem(len(guided) + len(all_stats)),
        out_specs=pl.BlockSpec(memory_space=pltpu.HBM),
        scratch_shapes=[pltpu.VMEM((own, vocab), f32), pltpu.SemaphoreType.DMA((-(-own // ROWS),))],
        compiler_params=pltpu.CompilerParams(vmem_limit_bytes=8 * MIB),
    )(*keep_in_vmem(*guided, *all_stats))


def solution(mesh):
    placed = (
        P(None, ("groups", "vocab"), ("rows", "cfg")),
        P("groups"),
        P(("rows", "cfg")),
        P(("rows", "cfg"), "vocab"),
    )
    return jax.shard_map(
        per_device,
        mesh=mesh,
        in_specs=placed,
        out_specs=P(("groups", "rows", "cfg"), "vocab"),
        check_vma=False,
    )
```

```python
import functools

import jax
import jax.numpy as jnp
from jax import lax
from jax.experimental import pallas as pl
from jax.experimental.pallas import tpu as pltpu
from jax.sharding import PartitionSpec as P

epsilon = 1e-06
guidance = 2.0
TILE = 256
LANES = 128
MIB = 1 << 20
LOADS = ((1280,), (1216,))
CHUNKS = (2496,)
ROWS = 8
USUAL = 7 / 8


def in_vmem(count):
    return [pl.BlockSpec(memory_space=pltpu.VMEM)] * count


def keep_in_vmem(*arrays):
    return [pltpu.with_memory_space_constraint(a, pltpu.VMEM) for a in arrays]


def call(body, outs, args, far=(), limit=8, cost=None, **kwargs):
    return pl.pallas_call(
        body,
        out_shape=[pltpu.VMEM(shape, dtype) for shape, dtype in outs],
        in_specs=[pl.BlockSpec(memory_space=pltpu.HBM)] * len(far) + in_vmem(len(args)),
        out_specs=in_vmem(len(outs)),
        compiler_params=pltpu.CompilerParams(vmem_limit_bytes=limit * MIB),
        cost_estimate=cost and pl.CostEstimate(flops=cost[0], bytes_accessed=cost[1], transcendentals=0),
        **kwargs,
    )(*[pltpu.with_memory_space_constraint(a, pltpu.HBM) for a in far], *keep_in_vmem(*args))


def diagonal(n):
    return lax.broadcasted_iota(jnp.int32, (n, n), 0) == lax.broadcasted_iota(jnp.int32, (n, n), 1)


def as_column(row):
    return jnp.sum(jnp.where(diagonal(row.shape[1]), row, 0.0), axis=1, keepdims=True)


def as_row(column):
    return jnp.sum(jnp.where(diagonal(column.shape[0]), column, 0.0), axis=0, keepdims=True)


def squares_kernel(hidden_far, gain_far, places_far, normed_ref, out_ref, places_ref, hidden_ref, gain_ref, sems):
    copies = [
        pltpu.make_async_copy(hidden_far.at[0], hidden_ref.at[0], sems.at[0]),
        pltpu.make_async_copy(hidden_far.at[1], hidden_ref.at[1], sems.at[1]),
        pltpu.make_async_copy(gain_far, gain_ref, sems.at[2]),
        pltpu.make_async_copy(places_far, places_ref, sems.at[3]),
    ]
    for copy in copies:
        copy.start()
    for b in range(2):
        copies[b].wait()
        widened = hidden_ref[b].astype(jnp.float32)
        out_ref[b : b + 1] = as_row(jnp.sum(widened * widened, axis=1, keepdims=True))
    copies[2].wait()
    gain = gain_ref[...]
    for b in range(2):
        normed_ref[b] = (hidden_ref[b].astype(jnp.float32) * gain).astype(jnp.bfloat16)
    copies[3].wait()


def combine_kernel(width, normed_ref, totals_ref, compact_ref, usual_ref, rest_ref):
    inv_rms = lax.rsqrt(totals_ref[...] / width + epsilon)
    factor = [as_column((1.0 + guidance) * inv_rms[0:1]), as_column(guidance * inv_rms[1:2])]
    terms = [factor[b] * normed_ref[b].astype(jnp.float32) for b in range(2)]
    rows = (terms[0] - terms[1]).astype(jnp.bfloat16)
    rows = jnp.dot(compact_ref[...], rows, preferred_element_type=jnp.float32)
    usual = usual_ref.shape[0]
    usual_ref[...] = rows[:usual].astype(jnp.bfloat16)
    rest_ref[...] = rows[usual:].astype(jnp.bfloat16)


def load_kernel(start, weights_far, *refs):
    *out_refs, tiles_ref, sems = refs
    slots = tiles_ref.shape[0]
    tiles = []
    for ref in out_refs:
        size = ref.shape[1]
        tiles += [(ref, at, min(TILE, size - at), start + at) for at in range(0, size, TILE)]
        start += size
    copies = [
        pltpu.make_async_copy(
            weights_far.at[pl.ds(column, rows)],
            tiles_ref.at[i % slots, pl.ds(0, rows)],
            sems.at[i % slots],
        )
        for i, (_, _, rows, column) in enumerate(tiles)
    ]
    for copy in copies[:slots]:
        copy.start()
    for i, (ref, at, rows, _) in enumerate(tiles):
        copies[i].wait()
        ref[:, at : at + rows] = tiles_ref[i % slots, :rows].T
        if i + slots < len(tiles):
            copies[i + slots].start()


def first_rank(positions_ref, at):
    return jnp.sum((positions_ref[...] < at).astype(jnp.float32), axis=1, keepdims=True).astype(jnp.int32)


def compact_kernel(usual, n_z, positions_ref, out_ref, crowded_ref):
    block, masked = out_ref.shape[0], positions_ref.shape[1]
    ranks = [first_rank(positions_ref, b * block) for b in range(n_z + 1)]
    most = functools.reduce(jnp.maximum, [end - first for first, end in zip(ranks, ranks[1:])])
    crowded_ref[0, 0] = (jnp.max(most) > usual).astype(jnp.int32)
    at = lax.axis_index("vocab") * block
    first = first_rank(positions_ref, at)
    rank = lax.broadcasted_iota(jnp.int32, (block, masked), 1)
    match = rank == first + lax.broadcasted_iota(jnp.int32, (block, masked), 0)
    places = (positions_ref[...] + 1).astype(jnp.float32)
    wanted = jnp.sum(jnp.where(match, places, 0.0), axis=1, keepdims=True).astype(jnp.int32) - 1
    held = at + lax.broadcasted_iota(jnp.int32, (block, block), 1)
    out_ref[...] = (wanted == held).astype(jnp.float32).astype(jnp.bfloat16)


def chooser_kernel(own, block, offsets, n_z, n_x, n_c, positions_ref, usual_ref, rest_ref):
    z, x, c = (lax.axis_index(axis) for axis in ("vocab", "rows", "cfg"))
    rows, usual = usual_ref.shape[1:]
    extra = block - usual
    segment = rows // (n_x * n_c)
    row = lax.broadcasted_iota(jnp.int32, (rows, 1), 0)
    wanted = jnp.full((rows, 1), -1, jnp.int32)
    for t in range(n_c):
        for s in range(n_x):
            owner = lax.rem(x + s, n_x) * n_c + lax.rem(c + t, n_c)
            i = row - (t * n_x + s) * segment
            wanted = jnp.where((i >= 0) & (i < own), owner * own + i, wanted)
    lane = lax.broadcasted_iota(jnp.int32, (1, usual), 1)
    rest_lane = lax.broadcasted_iota(jnp.int32, (1, rest_ref.shape[1]), 1)
    rest_rank = jnp.full(rest_lane.shape, -2, jnp.int32)
    for k, offset in enumerate(offsets):
        at = lax.rem(z - offset + n_z, n_z) * block
        first, end = first_rank(positions_ref, at), first_rank(positions_ref, at + block)
        rank = first + lane
        held = jnp.where(rank < end, rank, -2)
        usual_ref[k] = (wanted == held).astype(jnp.float32).astype(jnp.bfloat16)
        i = rest_lane - k * extra
        rank = first + usual + i
        rest_rank = jnp.where((i >= 0) & (i < extra) & (rank < end), rank, rest_rank)
    rest_ref[...] = (wanted == rest_rank).astype(jnp.float32).astype(jnp.bfloat16)


def multiply(start, size, rows_ref, weights_refs, keep_ref, send_ref):
    half, width = keep_ref.shape
    at, skip = 0, start
    for ref in weights_refs:
        held = ref.shape[1]
        while at < size and skip < held:
            step = min(TILE, size - at, held - skip)
            product = jnp.dot(rows_ref[...], ref[:, skip : skip + step], preferred_element_type=jnp.float32)
            keep_ref[:, at : at + step] = product[:half]
            send_ref[:, at : at + step] = product[half:]
            at, skip = at + step, skip + step
        skip = max(0, skip - held)
    for ref in (keep_ref, send_ref):
        ref[:, size:] = jnp.zeros((half, width - size), jnp.float32)


def early_kernel(chooser_ref, rest_chooser_ref, *refs):
    *block_refs, rest_ref, rows_ref = refs
    rows = jnp.dot(rest_chooser_ref[...], rest_ref[...], preferred_element_type=jnp.float32)
    for k, ref in enumerate(block_refs):
        rows = rows + jnp.dot(chooser_ref[k], ref[...], preferred_element_type=jnp.float32)
    rows_ref[...] = rows.astype(jnp.bfloat16)


def first_kernel(start, size, chooser_ref, early_ref, block_ref, *refs):
    *weights_refs, rows_ref, keep_ref, send_ref = refs
    last = jnp.dot(chooser_ref[chooser_ref.shape[0] - 1], block_ref[...], preferred_element_type=jnp.float32)
    rows_ref[...] = (early_ref[...].astype(jnp.float32) + last).astype(jnp.bfloat16)
    multiply(start, size, rows_ref, weights_refs, keep_ref, send_ref)


def later_kernel(start, size, rows_ref, *refs):
    *weights_refs, keep_ref, send_ref = refs
    multiply(start, size, rows_ref, weights_refs, keep_ref, send_ref)


def add_kernel(own, size, keep_ref, got_ref, own_ref, *out_refs):
    segment, width = own_ref.shape
    own_ref[...] = keep_ref[:segment] + got_ref[:segment]
    last = width - TILE
    spare = lax.broadcasted_iota(jnp.int32, (ROWS, TILE), 1) >= size - last
    for s, out_ref in enumerate(out_refs, 1):
        for t in range(-(-own // ROWS)):
            rows = slice(s * segment + t * ROWS, s * segment + (t + 1) * ROWS)
            value = keep_ref[rows] + got_ref[rows]
            peak = jnp.max(jnp.abs(value), axis=1, keepdims=True)
            exponent = jnp.clip(jnp.ceil(jnp.log2(jnp.maximum(peak, 1e-30))), -90.0, 127.0)
            scaled = jnp.clip(jnp.round(value * jnp.exp2(15.0 - exponent)), -32767.0, 32767.0)
            ending = jnp.where(spare, exponent, scaled[:, last:])
            scaled = jnp.concatenate([scaled[:, :last], ending], axis=1) if last else ending
            if own - t * ROWS <= ROWS // 2:
                half = ROWS // 2
                scaled = jnp.concatenate([scaled[:half, : width // 2], scaled[:half, width // 2 :]], axis=0)
            out_ref[:, t * width : t * width + scaled.shape[1]] = scaled.astype(jnp.int32).astype(jnp.int16)


def restored(own, size, width, got_ref, t):
    half = own - t * ROWS <= ROWS // 2
    value = got_ref[:, t * width : t * width + (width // 2 if half else width)]
    value = value.astype(jnp.int32).astype(jnp.float32)
    if half:
        value = jnp.concatenate([value[: ROWS // 2], value[ROWS // 2 :]], axis=1)
        value = jnp.concatenate([value, jnp.zeros_like(value)], axis=0)
    return value * jnp.exp2(value[:, size : size + 1] - 15.0)


def stats_kernel(own, size, *refs):
    *in_refs, guided_ref, out_ref = refs
    before = in_refs.pop(0) if in_refs[0].shape == out_ref.shape else None
    segment, width = guided_ref.shape
    real = lax.broadcasted_iota(jnp.int32, (ROWS, width), 1) < size
    tops, totals = [], []
    for t in range(segment // ROWS):
        rows = slice(t * ROWS, (t + 1) * ROWS)
        guided = in_refs[0][rows]
        if t * ROWS < own:
            for got in in_refs[1:]:
                guided = guided + restored(own, size, width, got, t)
        guided_ref[rows] = guided
        top = jnp.max(jnp.where(real, guided, -jnp.inf), axis=1, keepdims=True)
        tops.append(top)
        totals.append(jnp.sum(jnp.where(real, jnp.exp(guided - top), 0.0), axis=1, keepdims=True))
    top, total = as_row(jnp.concatenate(tops, axis=0)), as_row(jnp.concatenate(totals, axis=0))
    if before is not None:
        top, total = merged((top, total), (before[0:1, :segment], before[1:2, :segment]))
    out_ref[0:1, :segment] = top
    out_ref[1:2, :segment] = total


def merged(one, other):
    top = jnp.maximum(one[0], other[0])
    return top, one[1] * jnp.exp(one[0] - top) + other[1] * jnp.exp(other[0] - top)


def merge_kernel(one_ref, *refs):
    *other_refs, out_ref = refs
    top, total = one_ref[0:1], one_ref[1:2]
    for ref in other_refs:
        top, total = merged((top, total), (ref[0:1], ref[1:2]))
    out_ref[0:1] = top
    out_ref[1:2] = total


def final_kernel(sizes, segment, *refs):
    guided_refs, stats, (out_far, out_ref, sems) = refs[: len(sizes)], refs[len(sizes) : -3], refs[-3:]
    top, total = stats[0][0:1, :segment], stats[0][1:2, :segment]
    for ref in stats[1:]:
        top, total = merged((top, total), (ref[0:1, :segment], ref[1:2, :segment]))
    own = out_ref.shape[0]
    shift, log_total = as_column(top), as_column(jnp.log(total))
    copies = []
    for t, first in enumerate(range(0, own, ROWS)):
        rows = slice(first, min(first + ROWS, own))
        at = 0
        for ref, size in zip(guided_refs, sizes):
            out_ref[rows, at : at + size] = ref[rows, :size] - shift[rows] - log_total[rows]
            at += size
        copies.append(pltpu.make_async_copy(out_ref.at[rows], out_far.at[rows], sems.at[t]))
        copies[-1].start()
    for copy in copies:
        copy.wait()


def shifted(value, axis, by):
    size = lax.axis_size(axis)
    return lax.ppermute(value, axis, [(i, (i + by) % size) for i in range(size)])


def cut(vocab, widths):
    edges = [0]
    for width in widths:
        edges.append(min(vocab, edges[-1] + width))
    edges.append(vocab)
    return [(start, end - start) for start, end in zip(edges, edges[1:]) if end > start]


def padded(size):
    return -(-(size + 1) // TILE) * TILE


def packed_shape(own, width):
    blocks, rest = divmod(own, ROWS)
    lanes = blocks * width + (0 if rest == 0 else width // 2 if rest <= ROWS // 2 else width)
    return (ROWS, lanes)


def per_device(final_hidden, positions, norm_gain, unembedding):
    bf16, f32 = jnp.bfloat16, jnp.float32
    _, block, width_local = final_hidden.shape
    masked = positions.shape[0]
    vocab = unembedding.shape[1]
    n_z, n_x, n_c = lax.axis_size("vocab"), lax.axis_size("rows"), lax.axis_size("cfg")
    z, x, c = lax.axis_index("vocab"), lax.axis_index("rows"), lax.axis_index("cfg")
    own = masked // (n_x * n_c)
    segment = -(-(own + 1) // 16) * 16

    normed, squares, places = call(
        squares_kernel,
        [((2, block, width_local), bf16), ((2, block), f32), ((1, masked), jnp.int32)],
        [],
        far=[final_hidden, norm_gain[None, :], positions[None, :]],
        scratch_shapes=[
            pltpu.VMEM((2, block, width_local), bf16),
            pltpu.VMEM((1, width_local), f32),
            pltpu.SemaphoreType.DMA((4,)),
        ],
    )
    for axis in ("cfg", "rows"):
        squares = sum([shifted(squares, axis, s) for s in range(1, lax.axis_size(axis))], squares)
    usual = int(block * USUAL) // ROWS * ROWS
    compact, crowded = pl.pallas_call(
        functools.partial(compact_kernel, usual, n_z),
        out_shape=[pltpu.VMEM((block, block), bf16), jax.ShapeDtypeStruct((1, 1), jnp.int32)],
        in_specs=in_vmem(1),
        out_specs=[*in_vmem(1), pl.BlockSpec(memory_space=pltpu.SMEM)],
        compiler_params=pltpu.CompilerParams(vmem_limit_bytes=8 * MIB),
    )(*keep_in_vmem(places))
    block_rows, rest_rows = call(
        functools.partial(combine_kernel, width_local * n_x * n_c),
        [((usual, width_local), bf16), ((block - usual, width_local), bf16)],
        [normed, squares, compact],
    )

    weights = unembedding.T
    loads, loaded = cut(vocab, [width for group in LOADS for width in group]), []

    def load(count, after):
        nonlocal weights
        pieces = loads[len(loaded) : len(loaded) + count]
        if not pieces:
            return after
        weights, after = lax.optimization_barrier((weights, after))
        arrays = call(
            functools.partial(load_kernel, pieces[0][0]),
            [((width_local, size), bf16) for _, size in pieces],
            [],
            far=[weights],
            cost=(0, 2 * sum(size for _, size in pieces) * width_local),
            scratch_shapes=[pltpu.VMEM((3, TILE, width_local), bf16), pltpu.SemaphoreType.DMA((3,))],
        )
        *arrays, after = lax.optimization_barrier((*arrays, after))
        loaded.extend(arrays)
        return after

    def both_ways(own_block):
        ahead = behind = own_block
        gathered = [own_block]
        for step in range(1, n_z // 2 + 1):
            ahead = shifted(ahead, "vocab", 1)
            gathered.append(ahead)
            if 2 * step < n_z:
                behind = shifted(behind, "vocab", -1)
                gathered.append(behind)
        return gathered

    offsets = [0] + [sign * step for step in range(1, n_z // 2 + 1) for sign in (1, -1) if sign > 0 or 2 * step < n_z]
    rest = lax.cond(
        crowded[0, 0] > 0,
        lambda rest: jnp.concatenate(both_ways(rest), axis=0),
        lambda rest: jnp.zeros((n_z * rest.shape[0], rest.shape[1]), rest.dtype),
        rest_rows,
    )
    weights, places, rest = lax.optimization_barrier((weights, places, rest))
    ahead = shifted(block_rows, "vocab", 1)
    behind = load(len(LOADS[0]), block_rows)
    aheads, behinds = [ahead], []
    for step in range(1, (n_z - 1) // 2 + 1):
        behind = shifted(behind, "vocab", -1)
        behinds.append(behind)
    for step in range(2, n_z // 2 + 1):
        ahead = shifted(ahead, "vocab", 1)
        aheads.append(ahead)
    arrivals = [block_rows]
    for step in range(n_z // 2):
        arrivals += aheads[step : step + 1] + behinds[step : step + 1]

    chooser, rest_chooser = call(
        functools.partial(chooser_kernel, own, block, offsets, n_z, n_x, n_c),
        [((n_z, n_x * n_c * segment, usual), bf16), ((n_x * n_c * segment, n_z * (block - usual)), bf16)],
        [places],
    )
    load(len(loads), aheads[0])
    chooser, rest_chooser, *loaded = lax.optimization_barrier((chooser, rest_chooser, *loaded))
    (early,) = call(
        early_kernel,
        [((n_x * n_c * segment, width_local), bf16)],
        [chooser, rest_chooser, *arrivals[:-1], rest],
    )

    half = n_x * segment
    chunks = cut(vocab, CHUNKS)
    parts, leaving = [], []
    for j, (start, size) in enumerate(chunks):
        width = padded(size)
        outs = [((half, width), f32)] * 2
        cost = (4 * half * width_local * size, 2 * width_local * size)
        needed = [i for i, (at, held) in enumerate(loads) if at < start + size and start < at + held]
        skip = start - loads[needed[0]][0]
        pieces = [loaded[i] for i in needed]
        if j == 0:
            rows, keep, send = call(
                functools.partial(first_kernel, skip, size),
                [((n_x * n_c * segment, width_local), bf16)] + outs,
                [chooser, early, arrivals[-1], *pieces],
                cost=cost,
            )
        else:
            keep, send = call(functools.partial(later_kernel, skip, size), outs, [rows, *pieces], cost=cost)
        got = shifted(send, "cfg", 1)
        own_sum, *sends = call(
            functools.partial(add_kernel, own, size),
            [((segment, width), f32)] + [(packed_shape(own, width), jnp.int16)] * (n_x - 1),
            [keep, got],
        )
        parts.append(own_sum)
        leaving.append(sends)
    guided, stats = [], None
    for (_, size), own_sum, sends in zip(chunks, parts, leaving):
        got = [shifted(s_rows, "rows", s) for s, s_rows in enumerate(sends, 1)]
        chunk, stats = call(
            functools.partial(stats_kernel, own, size),
            [(own_sum.shape, f32), ((2, LANES), f32)],
            ([] if stats is None else [stats]) + [own_sum, *got],
        )
        guided.append(chunk)
    if n_z & (n_z - 1) == 0:
        all_stats = [stats] + [
            lax.ppermute(stats, "vocab", [(i, i ^ far) for i in range(n_z)]) for far in range(1, n_z)
        ]
    else:
        all_stats = [stats] + [shifted(stats, "vocab", s) for s in range(1, n_z)]
    return pl.pallas_call(
        functools.partial(final_kernel, [size for _, size in chunks], segment),
        out_shape=jax.ShapeDtypeStruct((own, vocab), f32),
        in_specs=in_vmem(len(guided) + len(all_stats)),
        out_specs=pl.BlockSpec(memory_space=pltpu.HBM),
        scratch_shapes=[pltpu.VMEM((own, vocab), f32), pltpu.SemaphoreType.DMA((-(-own // ROWS),))],
        compiler_params=pltpu.CompilerParams(vmem_limit_bytes=8 * MIB),
    )(*keep_in_vmem(*guided, *all_stats))


def solution(mesh):
    placed = (
        P(None, ("groups", "vocab"), ("rows", "cfg")),
        P("groups"),
        P(("rows", "cfg")),
        P(("rows", "cfg"), "vocab"),
    )
    return jax.shard_map(
        per_device,
        mesh=mesh,
        in_specs=placed,
        out_specs=P(("groups", "rows", "cfg"), "vocab"),
        check_vma=False,
    )
```

```python
import functools

import jax
import jax.numpy as jnp
from jax import lax
from jax.experimental import pallas as pl
from jax.experimental.pallas import tpu as pltpu
from jax.sharding import PartitionSpec as P

epsilon = 1e-06
guidance = 2.0
TILE = 256
LANES = 128
MIB = 1 << 20
LOADS = ((1280,), (1216,))
SLOTS = 5
CHUNKS = (2496,)
ROWS = 8
USUAL = 13 / 16
DEEP = 16


def in_vmem(count):
    return [pl.BlockSpec(memory_space=pltpu.VMEM)] * count


def keep_in_vmem(*arrays):
    return [pltpu.with_memory_space_constraint(a, pltpu.VMEM) for a in arrays]


def call(body, outs, args, far=(), limit=8, cost=None, **kwargs):
    return pl.pallas_call(
        body,
        out_shape=[pltpu.VMEM(shape, dtype) for shape, dtype in outs],
        in_specs=[pl.BlockSpec(memory_space=pltpu.HBM)] * len(far) + in_vmem(len(args)),
        out_specs=in_vmem(len(outs)),
        compiler_params=pltpu.CompilerParams(vmem_limit_bytes=limit * MIB),
        cost_estimate=cost and pl.CostEstimate(flops=cost[0], bytes_accessed=cost[1], transcendentals=0),
        **kwargs,
    )(*[pltpu.with_memory_space_constraint(a, pltpu.HBM) for a in far], *keep_in_vmem(*args))


def diagonal(n):
    return lax.broadcasted_iota(jnp.int32, (n, n), 0) == lax.broadcasted_iota(jnp.int32, (n, n), 1)


def as_column(row):
    return jnp.sum(jnp.where(diagonal(row.shape[1]), row, 0.0), axis=1, keepdims=True)


def as_row(column):
    return jnp.sum(jnp.where(diagonal(column.shape[0]), column, 0.0), axis=0, keepdims=True)


def squares_kernel(hidden_far, gain_far, places_far, normed_ref, out_ref, places_ref, hidden_ref, gain_ref, sems):
    copies = [
        pltpu.make_async_copy(hidden_far.at[0], hidden_ref.at[0], sems.at[0]),
        pltpu.make_async_copy(hidden_far.at[1], hidden_ref.at[1], sems.at[1]),
        pltpu.make_async_copy(gain_far, gain_ref, sems.at[2]),
        pltpu.make_async_copy(places_far, places_ref, sems.at[3]),
    ]
    for copy in copies:
        copy.start()
    for b in range(2):
        copies[b].wait()
        widened = hidden_ref[b].astype(jnp.float32)
        out_ref[b : b + 1] = as_row(jnp.sum(widened * widened, axis=1, keepdims=True))
    copies[2].wait()
    gain = gain_ref[...]
    for b in range(2):
        normed_ref[b] = (hidden_ref[b].astype(jnp.float32) * gain).astype(jnp.bfloat16)
    copies[3].wait()


def combine_kernel(width, usual, normed_ref, totals_ref, compact_ref, usual_ref, rest_ref):
    inv_rms = lax.rsqrt(totals_ref[...] / width + epsilon)
    factor = [as_column((1.0 + guidance) * inv_rms[0:1]), as_column(guidance * inv_rms[1:2])]
    terms = [factor[b] * normed_ref[b].astype(jnp.float32) for b in range(2)]
    rows = (terms[0] - terms[1]).astype(jnp.bfloat16)
    rows = jnp.dot(compact_ref[...], rows, preferred_element_type=jnp.float32)
    whole, last = divmod(usual, DEEP)
    columns = rows.shape[1]
    for t in range(whole):
        usual_ref[:, t * columns : (t + 1) * columns] = rows[t * DEEP : (t + 1) * DEEP].astype(jnp.bfloat16)
    if last:
        share = columns * last // DEEP
        ending = rows[whole * DEEP : usual]
        ending = jnp.concatenate([ending[:, at : at + share] for at in range(0, columns, share)], axis=0)
        usual_ref[:, whole * columns :] = ending.astype(jnp.bfloat16)
    rest_ref[...] = rows[whole * DEEP :].astype(jnp.bfloat16)


def unpacked(ref, usual, columns):
    whole, last = divmod(usual, DEEP)
    blocks = [ref[:, t * columns : (t + 1) * columns] for t in range(whole)]
    if last:
        ending = ref[:, whole * columns :].astype(jnp.float32)
        ending = jnp.concatenate([ending[at : at + last] for at in range(0, DEEP, last)], axis=1)
        ending = jnp.concatenate([ending, jnp.zeros((DEEP - last, columns), jnp.float32)], axis=0)
        blocks.append(ending.astype(jnp.bfloat16))
    return blocks


def load_kernel(start, weights_far, *refs):
    *out_refs, tiles_ref, sems = refs
    slots = tiles_ref.shape[0]
    tiles = []
    for ref in out_refs:
        size = ref.shape[1]
        tiles += [(ref, at, min(TILE, size - at), start + at) for at in range(0, size, TILE)]
        start += size
    copies = [
        pltpu.make_async_copy(
            weights_far.at[pl.ds(column, rows)],
            tiles_ref.at[i % slots, pl.ds(0, rows)],
            sems.at[i % slots],
        )
        for i, (_, _, rows, column) in enumerate(tiles)
    ]
    for copy in copies[:slots]:
        copy.start()
    for i, (ref, at, rows, _) in enumerate(tiles):
        copies[i].wait()
        ref[:, at : at + rows] = tiles_ref[i % slots, :rows].T
        if i + slots < len(tiles):
            copies[i + slots].start()


def first_rank(positions_ref, at):
    return jnp.sum((positions_ref[...] < at).astype(jnp.float32), axis=1, keepdims=True).astype(jnp.int32)


def compact_kernel(usual, n_z, positions_ref, out_ref, crowded_ref):
    block, masked = out_ref.shape[0], positions_ref.shape[1]
    ranks = [first_rank(positions_ref, b * block) for b in range(n_z + 1)]
    most = functools.reduce(jnp.maximum, [end - first for first, end in zip(ranks, ranks[1:])])
    crowded_ref[0, 0] = (jnp.max(most) > usual).astype(jnp.int32)
    at = lax.axis_index("vocab") * block
    first = first_rank(positions_ref, at)
    rank = lax.broadcasted_iota(jnp.int32, (block, masked), 1)
    match = rank == first + lax.broadcasted_iota(jnp.int32, (block, masked), 0)
    places = (positions_ref[...] + 1).astype(jnp.float32)
    wanted = jnp.sum(jnp.where(match, places, 0.0), axis=1, keepdims=True).astype(jnp.int32) - 1
    held = at + lax.broadcasted_iota(jnp.int32, (block, block), 1)
    out_ref[...] = (wanted == held).astype(jnp.float32).astype(jnp.bfloat16)


def chooser_kernel(own, block, usual, offsets, n_z, n_x, n_c, positions_ref, early_ref, last_ref):
    z, x, c = (lax.axis_index(axis) for axis in ("vocab", "rows", "cfg"))
    rows, deep = last_ref.shape
    segment = rows // (n_x * n_c)
    row = lax.broadcasted_iota(jnp.int32, (rows, 1), 0)
    wanted = jnp.full((rows, 1), -1, jnp.int32)
    for t in range(n_c):
        for s in range(n_x):
            owner = lax.rem(x + s, n_x) * n_c + lax.rem(c + t, n_c)
            i = row - (t * n_x + s) * segment
            wanted = jnp.where((i >= 0) & (i < own), owner * own + i, wanted)
    lane = lax.broadcasted_iota(jnp.int32, (1, early_ref.shape[1]), 1)
    held = jnp.full(lane.shape, -2, jnp.int32)
    skipped = usual // DEEP * DEEP
    for k, offset in enumerate(offsets):
        at = lax.rem(z - offset + n_z, n_z) * block
        first, end = first_rank(positions_ref, at), first_rank(positions_ref, at + block)
        if k < n_z - 1:
            i = lane - k * deep
            held = jnp.where((i >= 0) & (i < usual) & (first + i < end), first + i, held)
        else:
            i = lax.broadcasted_iota(jnp.int32, (1, deep), 1)
            last = jnp.where((i < usual) & (first + i < end), first + i, -2)
        i = lane - (n_z - 1) * deep - k * (block - skipped) + skipped
        held = jnp.where((i >= usual) & (i < block) & (first + i < end), first + i, held)
    early_ref[...] = (wanted == held).astype(jnp.float32).astype(jnp.bfloat16)
    last_ref[...] = (wanted == last).astype(jnp.float32).astype(jnp.bfloat16)


def multiply(start, size, rows_ref, weights_refs, keep_ref, send_ref):
    half, width = keep_ref.shape
    at, skip = 0, start
    for ref in weights_refs:
        held = ref.shape[1]
        while at < size and skip < held:
            step = min(TILE, size - at, held - skip)
            product = jnp.dot(rows_ref[...], ref[:, skip : skip + step], preferred_element_type=jnp.float32)
            keep_ref[:, at : at + step] = product[:half]
            send_ref[:, at : at + step] = product[half:]
            at, skip = at + step, skip + step
        skip = max(0, skip - held)
    for ref in (keep_ref, send_ref):
        ref[:, size:] = jnp.zeros((half, width - size), jnp.float32)


def early_kernel(usual, chooser_ref, *refs):
    *block_refs, rest_ref, rows_ref = refs
    blocks = [part for ref in block_refs for part in unpacked(ref, usual, rows_ref.shape[1])]
    blocks = jnp.concatenate([*blocks, rest_ref[...]], axis=0)
    rows_ref[...] = jnp.dot(chooser_ref[...], blocks, preferred_element_type=jnp.float32).astype(jnp.bfloat16)


def first_kernel(start, size, usual, chooser_ref, early_ref, block_ref, *refs):
    *weights_refs, rows_ref, keep_ref, send_ref = refs
    block = jnp.concatenate(unpacked(block_ref, usual, rows_ref.shape[1]), axis=0)
    last = jnp.dot(chooser_ref[...], block, preferred_element_type=jnp.float32)
    rows_ref[...] = (early_ref[...].astype(jnp.float32) + last).astype(jnp.bfloat16)
    multiply(start, size, rows_ref, weights_refs, keep_ref, send_ref)


def later_kernel(start, size, rows_ref, *refs):
    *weights_refs, keep_ref, send_ref = refs
    multiply(start, size, rows_ref, weights_refs, keep_ref, send_ref)


def add_kernel(own, size, keep_ref, got_ref, own_ref, *out_refs):
    segment, width = own_ref.shape
    own_ref[...] = keep_ref[:segment] + got_ref[:segment]
    last = width - TILE
    spare = lax.broadcasted_iota(jnp.int32, (ROWS, TILE), 1) >= size - last
    for s, out_ref in enumerate(out_refs, 1):
        for t in range(-(-own // ROWS)):
            rows = slice(s * segment + t * ROWS, s * segment + (t + 1) * ROWS)
            value = keep_ref[rows] + got_ref[rows]
            peak = jnp.max(jnp.abs(value), axis=1, keepdims=True)
            exponent = jnp.clip(jnp.ceil(jnp.log2(jnp.maximum(peak, 1e-30))), -90.0, 127.0)
            scaled = jnp.clip(jnp.round(value * jnp.exp2(15.0 - exponent)), -32767.0, 32767.0)
            ending = jnp.where(spare, exponent, scaled[:, last:])
            scaled = jnp.concatenate([scaled[:, :last], ending], axis=1) if last else ending
            if own - t * ROWS <= ROWS // 2:
                half = ROWS // 2
                scaled = jnp.concatenate([scaled[:half, : width // 2], scaled[:half, width // 2 :]], axis=0)
            out_ref[:, t * width : t * width + scaled.shape[1]] = scaled.astype(jnp.int32).astype(jnp.int16)


def restored(own, size, width, got_ref, t):
    half = own - t * ROWS <= ROWS // 2
    value = got_ref[:, t * width : t * width + (width // 2 if half else width)]
    value = value.astype(jnp.int32).astype(jnp.float32)
    if half:
        value = jnp.concatenate([value[: ROWS // 2], value[ROWS // 2 :]], axis=1)
        value = jnp.concatenate([value, jnp.zeros_like(value)], axis=0)
    return value * jnp.exp2(value[:, size : size + 1] - 15.0)


def stats_kernel(own, size, *refs):
    *in_refs, guided_ref, out_ref = refs
    before = in_refs.pop(0) if in_refs[0].shape == out_ref.shape else None
    segment, width = guided_ref.shape
    real = lax.broadcasted_iota(jnp.int32, (ROWS, width), 1) < size
    tops, totals = [], []
    for t in range(segment // ROWS):
        rows = slice(t * ROWS, (t + 1) * ROWS)
        guided = in_refs[0][rows]
        if t * ROWS < own:
            for got in in_refs[1:]:
                guided = guided + restored(own, size, width, got, t)
        guided_ref[rows] = guided
        top = jnp.max(jnp.where(real, guided, -jnp.inf), axis=1, keepdims=True)
        tops.append(top)
        totals.append(jnp.sum(jnp.where(real, jnp.exp(guided - top), 0.0), axis=1, keepdims=True))
    top, total = as_row(jnp.concatenate(tops, axis=0)), as_row(jnp.concatenate(totals, axis=0))
    if before is not None:
        top, total = merged((top, total), (before[0:1, :segment], before[1:2, :segment]))
    out_ref[0:1, :segment] = top
    out_ref[1:2, :segment] = total


def merged(one, other):
    top = jnp.maximum(one[0], other[0])
    return top, one[1] * jnp.exp(one[0] - top) + other[1] * jnp.exp(other[0] - top)


def merge_kernel(one_ref, *refs):
    *other_refs, out_ref = refs
    top, total = one_ref[0:1], one_ref[1:2]
    for ref in other_refs:
        top, total = merged((top, total), (ref[0:1], ref[1:2]))
    out_ref[0:1] = top
    out_ref[1:2] = total


def final_kernel(sizes, segment, *refs):
    guided_refs, stats, (out_far, out_ref, sems) = refs[: len(sizes)], refs[len(sizes) : -3], refs[-3:]
    top, total = stats[0][0:1, :segment], stats[0][1:2, :segment]
    for ref in stats[1:]:
        top, total = merged((top, total), (ref[0:1, :segment], ref[1:2, :segment]))
    own = out_ref.shape[0]
    shift, log_total = as_column(top), as_column(jnp.log(total))
    copies = []
    for t, first in enumerate(range(0, own, ROWS)):
        rows = slice(first, min(first + ROWS, own))
        at = 0
        for ref, size in zip(guided_refs, sizes):
            out_ref[rows, at : at + size] = ref[rows, :size] - shift[rows] - log_total[rows]
            at += size
        copies.append(pltpu.make_async_copy(out_ref.at[rows], out_far.at[rows], sems.at[t]))
        copies[-1].start()
    for copy in copies:
        copy.wait()


def shifted(value, axis, by):
    size = lax.axis_size(axis)
    return lax.ppermute(value, axis, [(i, (i + by) % size) for i in range(size)])


def cut(vocab, widths):
    edges = [0]
    for width in widths:
        edges.append(min(vocab, edges[-1] + width))
    edges.append(vocab)
    return [(start, end - start) for start, end in zip(edges, edges[1:]) if end > start]


def padded(size):
    return -(-(size + 1) // TILE) * TILE


def packed_shape(own, width):
    blocks, rest = divmod(own, ROWS)
    lanes = blocks * width + (0 if rest == 0 else width // 2 if rest <= ROWS // 2 else width)
    return (ROWS, lanes)


def per_device(final_hidden, positions, norm_gain, unembedding):
    bf16, f32 = jnp.bfloat16, jnp.float32
    _, block, width_local = final_hidden.shape
    masked = positions.shape[0]
    vocab = unembedding.shape[1]
    n_z, n_x, n_c = lax.axis_size("vocab"), lax.axis_size("rows"), lax.axis_size("cfg")
    z, x, c = lax.axis_index("vocab"), lax.axis_index("rows"), lax.axis_index("cfg")
    own = masked // (n_x * n_c)
    segment = -(-(own + 1) // 16) * 16

    normed, squares, places = call(
        squares_kernel,
        [((2, block, width_local), bf16), ((2, block), f32), ((1, masked), jnp.int32)],
        [],
        far=[final_hidden, norm_gain[None, :], positions[None, :]],
        scratch_shapes=[
            pltpu.VMEM((2, block, width_local), bf16),
            pltpu.VMEM((1, width_local), f32),
            pltpu.SemaphoreType.DMA((4,)),
        ],
    )
    for axis in ("cfg", "rows"):
        squares = sum([shifted(squares, axis, s) for s in range(1, lax.axis_size(axis))], squares)
    usual = int(block * USUAL)
    skipped = usual // DEEP * DEEP
    compact, crowded = pl.pallas_call(
        functools.partial(compact_kernel, usual, n_z),
        out_shape=[pltpu.VMEM((block, block), bf16), jax.ShapeDtypeStruct((1, 1), jnp.int32)],
        in_specs=in_vmem(1),
        out_specs=[*in_vmem(1), pl.BlockSpec(memory_space=pltpu.SMEM)],
        compiler_params=pltpu.CompilerParams(vmem_limit_bytes=8 * MIB),
    )(*keep_in_vmem(places))
    block_rows, rest_rows = call(
        functools.partial(combine_kernel, width_local * n_x * n_c, usual),
        [((DEEP, usual * width_local // DEEP), bf16), ((block - skipped, width_local), bf16)],
        [normed, squares, compact],
    )

    weights = unembedding.T
    loads, loaded = cut(vocab, [width for group in LOADS for width in group]), []

    def load(count, after):
        nonlocal weights
        pieces = loads[len(loaded) : len(loaded) + count]
        if not pieces:
            return after
        weights, after = lax.optimization_barrier((weights, after))
        arrays = call(
            functools.partial(load_kernel, pieces[0][0]),
            [((width_local, size), bf16) for _, size in pieces],
            [],
            far=[weights],
            cost=(0, 2 * sum(size for _, size in pieces) * width_local),
            scratch_shapes=[pltpu.VMEM((SLOTS, TILE, width_local), bf16), pltpu.SemaphoreType.DMA((SLOTS,))],
        )
        *arrays, after = lax.optimization_barrier((*arrays, after))
        loaded.extend(arrays)
        return after

    def both_ways(own_block):
        ahead = behind = own_block
        gathered = [own_block]
        for step in range(1, n_z // 2 + 1):
            ahead = shifted(ahead, "vocab", 1)
            gathered.append(ahead)
            if 2 * step < n_z:
                behind = shifted(behind, "vocab", -1)
                gathered.append(behind)
        return gathered

    offsets = [0] + [sign * step for step in range(1, n_z // 2 + 1) for sign in (1, -1) if sign > 0 or 2 * step < n_z]
    rest = lax.cond(
        crowded[0, 0] > 0,
        lambda rest: jnp.concatenate(both_ways(rest), axis=0),
        lambda rest: jnp.zeros((n_z * rest.shape[0], rest.shape[1]), rest.dtype),
        rest_rows,
    )
    weights, places, rest = lax.optimization_barrier((weights, places, rest))
    ahead = shifted(block_rows, "vocab", 1)
    behind = load(len(LOADS[0]), block_rows)
    aheads, behinds = [ahead], []
    for step in range(1, (n_z - 1) // 2 + 1):
        behind = shifted(behind, "vocab", -1)
        behinds.append(behind)
    for step in range(2, n_z // 2 + 1):
        ahead = shifted(ahead, "vocab", 1)
        aheads.append(ahead)
    arrivals = [block_rows]
    for step in range(n_z // 2):
        arrivals += aheads[step : step + 1] + behinds[step : step + 1]

    selected, deep = n_x * n_c * segment, -(-usual // DEEP) * DEEP
    early_chooser, last_chooser = call(
        functools.partial(chooser_kernel, own, block, usual, offsets, n_z, n_x, n_c),
        [((selected, (n_z - 1) * deep + n_z * (block - skipped)), bf16), ((selected, deep), bf16)],
        [places],
    )
    load(len(loads), aheads[0])
    early_chooser, last_chooser, *loaded = lax.optimization_barrier((early_chooser, last_chooser, *loaded))
    (early,) = call(
        functools.partial(early_kernel, usual),
        [((selected, width_local), bf16)],
        [early_chooser, *arrivals[:-1], rest],
    )

    half = n_x * segment
    chunks = cut(vocab, CHUNKS)
    parts, leaving = [], []
    for j, (start, size) in enumerate(chunks):
        width = padded(size)
        outs = [((half, width), f32)] * 2
        cost = (4 * half * width_local * size, 2 * width_local * size)
        needed = [i for i, (at, held) in enumerate(loads) if at < start + size and start < at + held]
        skip = start - loads[needed[0]][0]
        pieces = [loaded[i] for i in needed]
        if j == 0:
            rows, keep, send = call(
                functools.partial(first_kernel, skip, size, usual),
                [((selected, width_local), bf16)] + outs,
                [last_chooser, early, arrivals[-1], *pieces],
                cost=cost,
            )
        else:
            keep, send = call(functools.partial(later_kernel, skip, size), outs, [rows, *pieces], cost=cost)
        got = shifted(send, "cfg", 1)
        own_sum, *sends = call(
            functools.partial(add_kernel, own, size),
            [((segment, width), f32)] + [(packed_shape(own, width), jnp.int16)] * (n_x - 1),
            [keep, got],
        )
        parts.append(own_sum)
        leaving.append(sends)
    guided, stats = [], None
    for (_, size), own_sum, sends in zip(chunks, parts, leaving):
        got = [shifted(s_rows, "rows", s) for s, s_rows in enumerate(sends, 1)]
        chunk, stats = call(
            functools.partial(stats_kernel, own, size),
            [(own_sum.shape, f32), ((2, LANES), f32)],
            ([] if stats is None else [stats]) + [own_sum, *got],
        )
        guided.append(chunk)
    if n_z & (n_z - 1) == 0:
        all_stats = [stats] + [
            lax.ppermute(stats, "vocab", [(i, i ^ far) for i in range(n_z)]) for far in range(1, n_z)
        ]
    else:
        all_stats = [stats] + [shifted(stats, "vocab", s) for s in range(1, n_z)]
    return pl.pallas_call(
        functools.partial(final_kernel, [size for _, size in chunks], segment),
        out_shape=jax.ShapeDtypeStruct((own, vocab), f32),
        in_specs=in_vmem(len(guided) + len(all_stats)),
        out_specs=pl.BlockSpec(memory_space=pltpu.HBM),
        scratch_shapes=[pltpu.VMEM((own, vocab), f32), pltpu.SemaphoreType.DMA((-(-own // ROWS),))],
        compiler_params=pltpu.CompilerParams(vmem_limit_bytes=8 * MIB),
    )(*keep_in_vmem(*guided, *all_stats))


def solution(mesh):
    placed = (
        P(None, ("groups", "vocab"), ("rows", "cfg")),
        P("groups"),
        P(("rows", "cfg")),
        P(("rows", "cfg"), "vocab"),
    )
    return jax.shard_map(
        per_device,
        mesh=mesh,
        in_specs=placed,
        out_specs=P(("groups", "rows", "cfg"), "vocab"),
        check_vma=False,
    )
```

```python
import functools

import jax
import jax.numpy as jnp
from jax import lax
from jax.experimental import pallas as pl
from jax.experimental.pallas import tpu as pltpu
from jax.sharding import PartitionSpec as P

epsilon = 1e-06
guidance = 2.0
TILE = 256
LANES = 128
MIB = 1 << 20
LOADS = ((768,), (1728,))
SLOTS = 5
CHUNKS = (2496,)
ROWS = 8
USUAL = 13 / 16
DEEP = 16


def in_vmem(count):
    return [pl.BlockSpec(memory_space=pltpu.VMEM)] * count


def keep_in_vmem(*arrays):
    return [pltpu.with_memory_space_constraint(a, pltpu.VMEM) for a in arrays]


def call(body, outs, args, far=(), limit=8, cost=None, **kwargs):
    return pl.pallas_call(
        body,
        out_shape=[pltpu.VMEM(shape, dtype) for shape, dtype in outs],
        in_specs=[pl.BlockSpec(memory_space=pltpu.HBM)] * len(far) + in_vmem(len(args)),
        out_specs=in_vmem(len(outs)),
        compiler_params=pltpu.CompilerParams(vmem_limit_bytes=limit * MIB),
        cost_estimate=cost and pl.CostEstimate(flops=cost[0], bytes_accessed=cost[1], transcendentals=0),
        **kwargs,
    )(*[pltpu.with_memory_space_constraint(a, pltpu.HBM) for a in far], *keep_in_vmem(*args))


def diagonal(n):
    return lax.broadcasted_iota(jnp.int32, (n, n), 0) == lax.broadcasted_iota(jnp.int32, (n, n), 1)


def as_column(row):
    return jnp.sum(jnp.where(diagonal(row.shape[1]), row, 0.0), axis=1, keepdims=True)


def as_row(column):
    return jnp.sum(jnp.where(diagonal(column.shape[0]), column, 0.0), axis=0, keepdims=True)


def squares_kernel(hidden_far, gain_far, places_far, normed_ref, out_ref, places_ref, hidden_ref, gain_ref, sems):
    copies = [
        pltpu.make_async_copy(hidden_far.at[0], hidden_ref.at[0], sems.at[0]),
        pltpu.make_async_copy(hidden_far.at[1], hidden_ref.at[1], sems.at[1]),
        pltpu.make_async_copy(gain_far, gain_ref, sems.at[2]),
        pltpu.make_async_copy(places_far, places_ref, sems.at[3]),
    ]
    for copy in copies:
        copy.start()
    for b in range(2):
        copies[b].wait()
        widened = hidden_ref[b].astype(jnp.float32)
        out_ref[b : b + 1] = as_row(jnp.sum(widened * widened, axis=1, keepdims=True))
    copies[2].wait()
    gain = gain_ref[...]
    for b in range(2):
        normed_ref[b] = (hidden_ref[b].astype(jnp.float32) * gain).astype(jnp.bfloat16)
    copies[3].wait()


def combine_kernel(width, usual, normed_ref, totals_ref, compact_ref, usual_ref, rest_ref):
    inv_rms = lax.rsqrt(totals_ref[...] / width + epsilon)
    factor = [as_column((1.0 + guidance) * inv_rms[0:1]), as_column(guidance * inv_rms[1:2])]
    terms = [factor[b] * normed_ref[b].astype(jnp.float32) for b in range(2)]
    rows = (terms[0] - terms[1]).astype(jnp.bfloat16)
    rows = jnp.dot(compact_ref[...], rows, preferred_element_type=jnp.float32)
    whole, last = divmod(usual, DEEP)
    columns = rows.shape[1]
    for t in range(whole):
        usual_ref[:, t * columns : (t + 1) * columns] = rows[t * DEEP : (t + 1) * DEEP].astype(jnp.bfloat16)
    if last:
        share = columns * last // DEEP
        ending = rows[whole * DEEP : usual]
        ending = jnp.concatenate([ending[:, at : at + share] for at in range(0, columns, share)], axis=0)
        usual_ref[:, whole * columns :] = ending.astype(jnp.bfloat16)
    rest_ref[...] = rows[whole * DEEP :].astype(jnp.bfloat16)


def unpacked(ref, usual, columns):
    whole, last = divmod(usual, DEEP)
    blocks = [ref[:, t * columns : (t + 1) * columns] for t in range(whole)]
    if last:
        ending = ref[:, whole * columns :].astype(jnp.float32)
        ending = jnp.concatenate([ending[at : at + last] for at in range(0, DEEP, last)], axis=1)
        ending = jnp.concatenate([ending, jnp.zeros((DEEP - last, columns), jnp.float32)], axis=0)
        blocks.append(ending.astype(jnp.bfloat16))
    return blocks


def load_kernel(start, weights_far, *refs):
    *out_refs, tiles_ref, sems = refs
    slots = tiles_ref.shape[0]
    tiles = []
    for ref in out_refs:
        size = ref.shape[1]
        tiles += [(ref, at, min(TILE, size - at), start + at) for at in range(0, size, TILE)]
        start += size
    copies = [
        pltpu.make_async_copy(
            weights_far.at[pl.ds(column, rows)],
            tiles_ref.at[i % slots, pl.ds(0, rows)],
            sems.at[i % slots],
        )
        for i, (_, _, rows, column) in enumerate(tiles)
    ]
    for copy in copies[:slots]:
        copy.start()
    for i, (ref, at, rows, _) in enumerate(tiles):
        copies[i].wait()
        ref[:, at : at + rows] = tiles_ref[i % slots, :rows].T
        if i + slots < len(tiles):
            copies[i + slots].start()


def first_rank(positions_ref, at):
    return jnp.sum((positions_ref[...] < at).astype(jnp.float32), axis=1, keepdims=True).astype(jnp.int32)


def compact_kernel(usual, n_z, positions_ref, out_ref, crowded_ref):
    block, masked = out_ref.shape[0], positions_ref.shape[1]
    ranks = [first_rank(positions_ref, b * block) for b in range(n_z + 1)]
    most = functools.reduce(jnp.maximum, [end - first for first, end in zip(ranks, ranks[1:])])
    crowded_ref[0, 0] = (jnp.max(most) > usual).astype(jnp.int32)
    at = lax.axis_index("vocab") * block
    first = first_rank(positions_ref, at)
    rank = lax.broadcasted_iota(jnp.int32, (block, masked), 1)
    match = rank == first + lax.broadcasted_iota(jnp.int32, (block, masked), 0)
    places = (positions_ref[...] + 1).astype(jnp.float32)
    wanted = jnp.sum(jnp.where(match, places, 0.0), axis=1, keepdims=True).astype(jnp.int32) - 1
    held = at + lax.broadcasted_iota(jnp.int32, (block, block), 1)
    out_ref[...] = (wanted == held).astype(jnp.float32).astype(jnp.bfloat16)


def chooser_kernel(own, block, usual, offsets, n_z, n_x, n_c, positions_ref, early_ref, last_ref):
    z, x, c = (lax.axis_index(axis) for axis in ("vocab", "rows", "cfg"))
    rows, deep = last_ref.shape
    segment = rows // (n_x * n_c)
    row = lax.broadcasted_iota(jnp.int32, (rows, 1), 0)
    wanted = jnp.full((rows, 1), -1, jnp.int32)
    for t in range(n_c):
        for s in range(n_x):
            owner = lax.rem(x + s, n_x) * n_c + lax.rem(c + t, n_c)
            i = row - (t * n_x + s) * segment
            wanted = jnp.where((i >= 0) & (i < own), owner * own + i, wanted)
    lane = lax.broadcasted_iota(jnp.int32, (1, early_ref.shape[1]), 1)
    held = jnp.full(lane.shape, -2, jnp.int32)
    skipped = usual // DEEP * DEEP
    for k, offset in enumerate(offsets):
        at = lax.rem(z - offset + n_z, n_z) * block
        first, end = first_rank(positions_ref, at), first_rank(positions_ref, at + block)
        if k < n_z - 1:
            i = lane - k * deep
            held = jnp.where((i >= 0) & (i < usual) & (first + i < end), first + i, held)
        else:
            i = lax.broadcasted_iota(jnp.int32, (1, deep), 1)
            last = jnp.where((i < usual) & (first + i < end), first + i, -2)
        i = lane - (n_z - 1) * deep - k * (block - skipped) + skipped
        held = jnp.where((i >= usual) & (i < block) & (first + i < end), first + i, held)
    early_ref[...] = (wanted == held).astype(jnp.float32).astype(jnp.bfloat16)
    last_ref[...] = (wanted == last).astype(jnp.float32).astype(jnp.bfloat16)


def multiply(start, size, rows_ref, weights_refs, keep_ref, send_ref):
    half, width = keep_ref.shape
    at, skip = 0, start
    for ref in weights_refs:
        held = ref.shape[1]
        while at < size and skip < held:
            step = min(TILE, size - at, held - skip)
            product = jnp.dot(rows_ref[...], ref[:, skip : skip + step], preferred_element_type=jnp.float32)
            keep_ref[:, at : at + step] = product[:half]
            send_ref[:, at : at + step] = product[half:]
            at, skip = at + step, skip + step
        skip = max(0, skip - held)
    for ref in (keep_ref, send_ref):
        ref[:, size:] = jnp.zeros((half, width - size), jnp.float32)


def early_kernel(usual, chooser_ref, *refs):
    *block_refs, rest_ref, rows_ref = refs
    blocks = [part for ref in block_refs for part in unpacked(ref, usual, rows_ref.shape[1])]
    blocks = jnp.concatenate([*blocks, rest_ref[...]], axis=0)
    rows_ref[...] = jnp.dot(chooser_ref[...], blocks, preferred_element_type=jnp.float32).astype(jnp.bfloat16)


def first_kernel(start, size, usual, chooser_ref, early_ref, block_ref, *refs):
    *weights_refs, rows_ref, keep_ref, send_ref = refs
    block = jnp.concatenate(unpacked(block_ref, usual, rows_ref.shape[1]), axis=0)
    last = jnp.dot(chooser_ref[...], block, preferred_element_type=jnp.float32)
    rows_ref[...] = (early_ref[...].astype(jnp.float32) + last).astype(jnp.bfloat16)
    multiply(start, size, rows_ref, weights_refs, keep_ref, send_ref)


def later_kernel(start, size, rows_ref, *refs):
    *weights_refs, keep_ref, send_ref = refs
    multiply(start, size, rows_ref, weights_refs, keep_ref, send_ref)


def add_kernel(own, size, keep_ref, got_ref, own_ref, *out_refs):
    segment, width = own_ref.shape
    own_ref[...] = keep_ref[:segment] + got_ref[:segment]
    last = width - TILE
    spare = lax.broadcasted_iota(jnp.int32, (ROWS, TILE), 1) >= size - last
    for s, out_ref in enumerate(out_refs, 1):
        for t in range(-(-own // ROWS)):
            rows = slice(s * segment + t * ROWS, s * segment + (t + 1) * ROWS)
            value = keep_ref[rows] + got_ref[rows]
            peak = jnp.max(jnp.abs(value), axis=1, keepdims=True)
            exponent = jnp.clip(jnp.ceil(jnp.log2(jnp.maximum(peak, 1e-30))), -90.0, 127.0)
            scaled = jnp.clip(jnp.round(value * jnp.exp2(15.0 - exponent)), -32767.0, 32767.0)
            ending = jnp.where(spare, exponent, scaled[:, last:])
            scaled = jnp.concatenate([scaled[:, :last], ending], axis=1) if last else ending
            if own - t * ROWS <= ROWS // 2:
                half = ROWS // 2
                scaled = jnp.concatenate([scaled[:half, : width // 2], scaled[:half, width // 2 :]], axis=0)
            out_ref[:, t * width : t * width + scaled.shape[1]] = scaled.astype(jnp.int32).astype(jnp.int16)


def restored(own, size, width, got_ref, t):
    half = own - t * ROWS <= ROWS // 2
    value = got_ref[:, t * width : t * width + (width // 2 if half else width)]
    value = value.astype(jnp.int32).astype(jnp.float32)
    if half:
        value = jnp.concatenate([value[: ROWS // 2], value[ROWS // 2 :]], axis=1)
        value = jnp.concatenate([value, jnp.zeros_like(value)], axis=0)
    return value * jnp.exp2(value[:, size : size + 1] - 15.0)


def stats_kernel(own, size, *refs):
    *in_refs, guided_ref, out_ref = refs
    before = in_refs.pop(0) if in_refs[0].shape == out_ref.shape else None
    segment, width = guided_ref.shape
    real = lax.broadcasted_iota(jnp.int32, (ROWS, width), 1) < size
    tops, totals = [], []
    for t in range(segment // ROWS):
        rows = slice(t * ROWS, (t + 1) * ROWS)
        guided = in_refs[0][rows]
        if t * ROWS < own:
            for got in in_refs[1:]:
                guided = guided + restored(own, size, width, got, t)
        guided_ref[rows] = guided
        top = jnp.max(jnp.where(real, guided, -jnp.inf), axis=1, keepdims=True)
        tops.append(top)
        totals.append(jnp.sum(jnp.where(real, jnp.exp(guided - top), 0.0), axis=1, keepdims=True))
    top, total = as_row(jnp.concatenate(tops, axis=0)), as_row(jnp.concatenate(totals, axis=0))
    if before is not None:
        top, total = merged((top, total), (before[0:1, :segment], before[1:2, :segment]))
    out_ref[0:1, :segment] = top
    out_ref[1:2, :segment] = total


def merged(one, other):
    top = jnp.maximum(one[0], other[0])
    return top, one[1] * jnp.exp(one[0] - top) + other[1] * jnp.exp(other[0] - top)


def merge_kernel(one_ref, *refs):
    *other_refs, out_ref = refs
    top, total = one_ref[0:1], one_ref[1:2]
    for ref in other_refs:
        top, total = merged((top, total), (ref[0:1], ref[1:2]))
    out_ref[0:1] = top
    out_ref[1:2] = total


def final_kernel(sizes, segment, *refs):
    guided_refs, stats, (out_far, out_ref, sems) = refs[: len(sizes)], refs[len(sizes) : -3], refs[-3:]
    top, total = stats[0][0:1, :segment], stats[0][1:2, :segment]
    for ref in stats[1:]:
        top, total = merged((top, total), (ref[0:1, :segment], ref[1:2, :segment]))
    own = out_ref.shape[0]
    shift, log_total = as_column(top), as_column(jnp.log(total))
    copies = []
    for t, first in enumerate(range(0, own, ROWS)):
        rows = slice(first, min(first + ROWS, own))
        at = 0
        for ref, size in zip(guided_refs, sizes):
            out_ref[rows, at : at + size] = ref[rows, :size] - shift[rows] - log_total[rows]
            at += size
        copies.append(pltpu.make_async_copy(out_ref.at[rows], out_far.at[rows], sems.at[t]))
        copies[-1].start()
    for copy in copies:
        copy.wait()


def shifted(value, axis, by):
    size = lax.axis_size(axis)
    return lax.ppermute(value, axis, [(i, (i + by) % size) for i in range(size)])


def cut(vocab, widths):
    edges = [0]
    for width in widths:
        edges.append(min(vocab, edges[-1] + width))
    edges.append(vocab)
    return [(start, end - start) for start, end in zip(edges, edges[1:]) if end > start]


def padded(size):
    return -(-(size + 1) // TILE) * TILE


def packed_shape(own, width):
    blocks, rest = divmod(own, ROWS)
    lanes = blocks * width + (0 if rest == 0 else width // 2 if rest <= ROWS // 2 else width)
    return (ROWS, lanes)


def per_device(final_hidden, positions, norm_gain, unembedding):
    bf16, f32 = jnp.bfloat16, jnp.float32
    _, block, width_local = final_hidden.shape
    masked = positions.shape[0]
    vocab = unembedding.shape[1]
    n_z, n_x, n_c = lax.axis_size("vocab"), lax.axis_size("rows"), lax.axis_size("cfg")
    z, x, c = lax.axis_index("vocab"), lax.axis_index("rows"), lax.axis_index("cfg")
    own = masked // (n_x * n_c)
    segment = -(-(own + 1) // 16) * 16

    normed, squares, places = call(
        squares_kernel,
        [((2, block, width_local), bf16), ((2, block), f32), ((1, masked), jnp.int32)],
        [],
        far=[final_hidden, norm_gain[None, :], positions[None, :]],
        scratch_shapes=[
            pltpu.VMEM((2, block, width_local), bf16),
            pltpu.VMEM((1, width_local), f32),
            pltpu.SemaphoreType.DMA((4,)),
        ],
    )
    for axis in ("cfg", "rows"):
        squares = sum([shifted(squares, axis, s) for s in range(1, lax.axis_size(axis))], squares)
    usual = int(block * USUAL)
    skipped = usual // DEEP * DEEP
    compact, crowded = pl.pallas_call(
        functools.partial(compact_kernel, usual, n_z),
        out_shape=[pltpu.VMEM((block, block), bf16), jax.ShapeDtypeStruct((1, 1), jnp.int32)],
        in_specs=in_vmem(1),
        out_specs=[*in_vmem(1), pl.BlockSpec(memory_space=pltpu.SMEM)],
        compiler_params=pltpu.CompilerParams(vmem_limit_bytes=8 * MIB),
    )(*keep_in_vmem(places))
    block_rows, rest_rows = call(
        functools.partial(combine_kernel, width_local * n_x * n_c, usual),
        [((DEEP, usual * width_local // DEEP), bf16), ((block - skipped, width_local), bf16)],
        [normed, squares, compact],
    )

    weights = unembedding.T
    loads, loaded = cut(vocab, [width for group in LOADS for width in group]), []

    def load(count, after):
        nonlocal weights
        pieces = loads[len(loaded) : len(loaded) + count]
        if not pieces:
            return after
        weights, after = lax.optimization_barrier((weights, after))
        arrays = call(
            functools.partial(load_kernel, pieces[0][0]),
            [((width_local, size), bf16) for _, size in pieces],
            [],
            far=[weights],
            cost=(0, 2 * sum(size for _, size in pieces) * width_local),
            scratch_shapes=[pltpu.VMEM((SLOTS, TILE, width_local), bf16), pltpu.SemaphoreType.DMA((SLOTS,))],
        )
        *arrays, after = lax.optimization_barrier((*arrays, after))
        loaded.extend(arrays)
        return after

    def both_ways(own_block):
        ahead = behind = own_block
        gathered = [own_block]
        for step in range(1, n_z // 2 + 1):
            ahead = shifted(ahead, "vocab", 1)
            gathered.append(ahead)
            if 2 * step < n_z:
                behind = shifted(behind, "vocab", -1)
                gathered.append(behind)
        return gathered

    offsets = [0] + [sign * step for step in range(1, n_z // 2 + 1) for sign in (1, -1) if sign > 0 or 2 * step < n_z]
    rest = lax.cond(
        crowded[0, 0] > 0,
        lambda rest: jnp.concatenate(both_ways(rest), axis=0),
        lambda rest: jnp.zeros((n_z * rest.shape[0], rest.shape[1]), rest.dtype),
        rest_rows,
    )
    weights, places, rest = lax.optimization_barrier((weights, places, rest))
    ahead = shifted(block_rows, "vocab", 1)
    behind = load(len(LOADS[0]), block_rows)
    aheads, behinds = [ahead], []
    for step in range(1, (n_z - 1) // 2 + 1):
        behind = shifted(behind, "vocab", -1)
        behinds.append(behind)
    for step in range(2, n_z // 2 + 1):
        ahead = shifted(ahead, "vocab", 1)
        aheads.append(ahead)
    arrivals = [block_rows]
    for step in range(n_z // 2):
        arrivals += aheads[step : step + 1] + behinds[step : step + 1]

    selected, deep = n_x * n_c * segment, -(-usual // DEEP) * DEEP
    early_chooser, last_chooser = call(
        functools.partial(chooser_kernel, own, block, usual, offsets, n_z, n_x, n_c),
        [((selected, (n_z - 1) * deep + n_z * (block - skipped)), bf16), ((selected, deep), bf16)],
        [places],
    )
    load(len(loads), aheads[0])
    early_chooser, last_chooser, *loaded = lax.optimization_barrier((early_chooser, last_chooser, *loaded))
    (early,) = call(
        functools.partial(early_kernel, usual),
        [((selected, width_local), bf16)],
        [early_chooser, *arrivals[:-1], rest],
    )

    half = n_x * segment
    chunks = cut(vocab, CHUNKS)
    parts, leaving = [], []
    for j, (start, size) in enumerate(chunks):
        width = padded(size)
        outs = [((half, width), f32)] * 2
        cost = (4 * half * width_local * size, 2 * width_local * size)
        needed = [i for i, (at, held) in enumerate(loads) if at < start + size and start < at + held]
        skip = start - loads[needed[0]][0]
        pieces = [loaded[i] for i in needed]
        if j == 0:
            rows, keep, send = call(
                functools.partial(first_kernel, skip, size, usual),
                [((selected, width_local), bf16)] + outs,
                [last_chooser, early, arrivals[-1], *pieces],
                cost=cost,
            )
        else:
            keep, send = call(functools.partial(later_kernel, skip, size), outs, [rows, *pieces], cost=cost)
        got = shifted(send, "cfg", 1)
        own_sum, *sends = call(
            functools.partial(add_kernel, own, size),
            [((segment, width), f32)] + [(packed_shape(own, width), jnp.int16)] * (n_x - 1),
            [keep, got],
        )
        parts.append(own_sum)
        leaving.append(sends)
    guided, stats = [], None
    for (_, size), own_sum, sends in zip(chunks, parts, leaving):
        got = [shifted(s_rows, "rows", s) for s, s_rows in enumerate(sends, 1)]
        chunk, stats = call(
            functools.partial(stats_kernel, own, size),
            [(own_sum.shape, f32), ((2, LANES), f32)],
            ([] if stats is None else [stats]) + [own_sum, *got],
        )
        guided.append(chunk)
    if n_z & (n_z - 1) == 0:
        all_stats = [stats] + [
            lax.ppermute(stats, "vocab", [(i, i ^ far) for i in range(n_z)]) for far in sorted(range(1, n_z), key=lambda far: [0,1,3,2][far % 4])
        ]
    else:
        all_stats = [stats] + [shifted(stats, "vocab", s) for s in range(1, n_z)]
    return pl.pallas_call(
        functools.partial(final_kernel, [size for _, size in chunks], segment),
        out_shape=jax.ShapeDtypeStruct((own, vocab), f32),
        in_specs=in_vmem(len(guided) + len(all_stats)),
        out_specs=pl.BlockSpec(memory_space=pltpu.HBM),
        scratch_shapes=[pltpu.VMEM((own, vocab), f32), pltpu.SemaphoreType.DMA((-(-own // ROWS),))],
        compiler_params=pltpu.CompilerParams(vmem_limit_bytes=8 * MIB),
    )(*keep_in_vmem(*guided, *all_stats))


def solution(mesh):
    placed = (
        P(None, ("groups", "vocab"), ("rows", "cfg")),
        P("groups"),
        P(("rows", "cfg")),
        P(("rows", "cfg"), "vocab"),
    )
    return jax.shard_map(
        per_device,
        mesh=mesh,
        in_specs=placed,
        out_specs=P(("groups", "rows", "cfg"), "vocab"),
        check_vma=False,
    )
```

```python
import functools

import jax
import jax.numpy as jnp
from jax import lax
from jax.experimental import pallas as pl
from jax.experimental.pallas import tpu as pltpu
from jax.sharding import PartitionSpec as P

epsilon = 1e-06
guidance = 2.0
TILE = 256
LANES = 128
MIB = 1 << 20
LOADS = ((768,), (1728,))
SLOTS = 5
CHUNKS = (2496,)
ROWS = 8
USUAL = 13 / 16
DEEP = 16


def in_vmem(count):
    return [pl.BlockSpec(memory_space=pltpu.VMEM)] * count


def keep_in_vmem(*arrays):
    return [pltpu.with_memory_space_constraint(a, pltpu.VMEM) for a in arrays]


def call(body, outs, args, far=(), limit=8, cost=None, **kwargs):
    return pl.pallas_call(
        body,
        out_shape=[pltpu.VMEM(shape, dtype) for shape, dtype in outs],
        in_specs=[pl.BlockSpec(memory_space=pltpu.HBM)] * len(far) + in_vmem(len(args)),
        out_specs=in_vmem(len(outs)),
        compiler_params=pltpu.CompilerParams(vmem_limit_bytes=limit * MIB),
        cost_estimate=cost and pl.CostEstimate(flops=cost[0], bytes_accessed=cost[1], transcendentals=0),
        **kwargs,
    )(*[pltpu.with_memory_space_constraint(a, pltpu.HBM) for a in far], *keep_in_vmem(*args))


def diagonal(n):
    return lax.broadcasted_iota(jnp.int32, (n, n), 0) == lax.broadcasted_iota(jnp.int32, (n, n), 1)


def as_column(row):
    return jnp.sum(jnp.where(diagonal(row.shape[1]), row, 0.0), axis=1, keepdims=True)


def as_row(column):
    return jnp.sum(jnp.where(diagonal(column.shape[0]), column, 0.0), axis=0, keepdims=True)


def squares_kernel(hidden_far, gain_far, places_far, normed_ref, out_ref, places_ref, hidden_ref, gain_ref, sems):
    copies = [
        pltpu.make_async_copy(hidden_far.at[0], hidden_ref.at[0], sems.at[0]),
        pltpu.make_async_copy(hidden_far.at[1], hidden_ref.at[1], sems.at[1]),
        pltpu.make_async_copy(gain_far, gain_ref, sems.at[2]),
        pltpu.make_async_copy(places_far, places_ref, sems.at[3]),
    ]
    for copy in copies:
        copy.start()
    for b in range(2):
        copies[b].wait()
        widened = hidden_ref[b].astype(jnp.float32)
        out_ref[b : b + 1] = as_row(jnp.sum(widened * widened, axis=1, keepdims=True))
    copies[2].wait()
    gain = gain_ref[...]
    for b in range(2):
        normed_ref[b] = (hidden_ref[b].astype(jnp.float32) * gain).astype(jnp.bfloat16)
    copies[3].wait()


def combine_kernel(width, usual, normed_ref, totals_ref, compact_ref, usual_ref, rest_ref):
    inv_rms = lax.rsqrt(totals_ref[...] / width + epsilon)
    factor = [as_column((1.0 + guidance) * inv_rms[0:1]), as_column(guidance * inv_rms[1:2])]
    terms = [factor[b] * normed_ref[b].astype(jnp.float32) for b in range(2)]
    rows = (terms[0] - terms[1]).astype(jnp.bfloat16)
    rows = jnp.dot(compact_ref[...], rows, preferred_element_type=jnp.float32)
    whole, last = divmod(usual, DEEP)
    columns = rows.shape[1]
    for t in range(whole):
        usual_ref[:, t * columns : (t + 1) * columns] = rows[t * DEEP : (t + 1) * DEEP].astype(jnp.bfloat16)
    if last:
        share = columns * last // DEEP
        ending = rows[whole * DEEP : usual]
        ending = jnp.concatenate([ending[:, at : at + share] for at in range(0, columns, share)], axis=0)
        usual_ref[:, whole * columns :] = ending.astype(jnp.bfloat16)
    rest_ref[...] = rows[whole * DEEP :].astype(jnp.bfloat16)


def unpacked(ref, usual, columns):
    whole, last = divmod(usual, DEEP)
    blocks = [ref[:, t * columns : (t + 1) * columns] for t in range(whole)]
    if last:
        ending = ref[:, whole * columns :].astype(jnp.float32)
        ending = jnp.concatenate([ending[at : at + last] for at in range(0, DEEP, last)], axis=1)
        ending = jnp.concatenate([ending, jnp.zeros((DEEP - last, columns), jnp.float32)], axis=0)
        blocks.append(ending.astype(jnp.bfloat16))
    return blocks


def load_kernel(start, weights_far, *refs):
    *out_refs, tiles_ref, sems = refs
    slots = tiles_ref.shape[0]
    tiles = []
    for ref in out_refs:
        size = ref.shape[1]
        tiles += [(ref, at, min(TILE, size - at), start + at) for at in range(0, size, TILE)]
        start += size
    copies = [
        pltpu.make_async_copy(
            weights_far.at[pl.ds(column, rows)],
            tiles_ref.at[i % slots, pl.ds(0, rows)],
            sems.at[i % slots],
        )
        for i, (_, _, rows, column) in enumerate(tiles)
    ]
    for copy in copies[:slots]:
        copy.start()
    for i, (ref, at, rows, _) in enumerate(tiles):
        copies[i].wait()
        ref[:, at : at + rows] = tiles_ref[i % slots, :rows].T
        if i + slots < len(tiles):
            copies[i + slots].start()


def first_rank(positions_ref, at):
    return jnp.sum((positions_ref[...] < at).astype(jnp.float32), axis=1, keepdims=True).astype(jnp.int32)


def compact_kernel(usual, n_z, positions_ref, out_ref, crowded_ref):
    block, masked = out_ref.shape[0], positions_ref.shape[1]
    ranks = [first_rank(positions_ref, b * block) for b in range(n_z + 1)]
    most = functools.reduce(jnp.maximum, [end - first for first, end in zip(ranks, ranks[1:])])
    crowded_ref[0, 0] = (jnp.max(most) > usual).astype(jnp.int32)
    at = lax.axis_index("vocab") * block
    first = first_rank(positions_ref, at)
    rank = lax.broadcasted_iota(jnp.int32, (block, masked), 1)
    match = rank == first + lax.broadcasted_iota(jnp.int32, (block, masked), 0)
    places = (positions_ref[...] + 1).astype(jnp.float32)
    wanted = jnp.sum(jnp.where(match, places, 0.0), axis=1, keepdims=True).astype(jnp.int32) - 1
    held = at + lax.broadcasted_iota(jnp.int32, (block, block), 1)
    out_ref[...] = (wanted == held).astype(jnp.float32).astype(jnp.bfloat16)


def chooser_kernel(own, block, usual, offsets, n_z, n_x, n_c, positions_ref, early_ref, last_ref):
    z, x, c = (lax.axis_index(axis) for axis in ("vocab", "rows", "cfg"))
    rows, deep = last_ref.shape
    half = rows // n_c
    segment = -(-own // ROWS) * ROWS if tight(own, n_x) else half // n_x
    row = lax.broadcasted_iota(jnp.int32, (rows, 1), 0)
    wanted = jnp.full((rows, 1), -1, jnp.int32)
    for t in range(n_c):
        for s in range(n_x):
            owner = lax.rem(x + s, n_x) * n_c + lax.rem(c + t, n_c)
            for at, first, end in row_ranges(own, segment, n_x, s):
                i = row - (t * half + at) + first
                wanted = jnp.where((i >= first) & (i < end), owner * own + i, wanted)
    lane = lax.broadcasted_iota(jnp.int32, (1, early_ref.shape[1]), 1)
    held = jnp.full(lane.shape, -2, jnp.int32)
    skipped = usual // DEEP * DEEP
    for k, offset in enumerate(offsets):
        at = lax.rem(z - offset + n_z, n_z) * block
        first, end = first_rank(positions_ref, at), first_rank(positions_ref, at + block)
        if k < n_z - 1:
            i = lane - k * deep
            held = jnp.where((i >= 0) & (i < usual) & (first + i < end), first + i, held)
        else:
            i = lax.broadcasted_iota(jnp.int32, (1, deep), 1)
            last = jnp.where((i < usual) & (first + i < end), first + i, -2)
        i = lane - (n_z - 1) * deep - k * (block - skipped) + skipped
        held = jnp.where((i >= usual) & (i < block) & (first + i < end), first + i, held)
    early_ref[...] = (wanted == held).astype(jnp.float32).astype(jnp.bfloat16)
    last_ref[...] = (wanted == last).astype(jnp.float32).astype(jnp.bfloat16)


def multiply(start, size, rows_ref, weights_refs, keep_ref, send_ref):
    half, width = keep_ref.shape
    at, skip = 0, start
    for ref in weights_refs:
        held = ref.shape[1]
        while at < size and skip < held:
            step = min(TILE, size - at, held - skip)
            product = jnp.dot(rows_ref[...], ref[:, skip : skip + step], preferred_element_type=jnp.float32)
            keep_ref[:, at : at + step] = product[:half]
            send_ref[:, at : at + step] = product[half:]
            at, skip = at + step, skip + step
        skip = max(0, skip - held)
    for ref in (keep_ref, send_ref):
        ref[:, size:] = jnp.zeros((half, width - size), jnp.float32)


def early_kernel(usual, chooser_ref, *refs):
    *block_refs, rest_ref, rows_ref = refs
    blocks = [part for ref in block_refs for part in unpacked(ref, usual, rows_ref.shape[1])]
    blocks = jnp.concatenate([*blocks, rest_ref[...]], axis=0)
    rows_ref[...] = jnp.dot(chooser_ref[...], blocks, preferred_element_type=jnp.float32).astype(jnp.bfloat16)


def first_kernel(start, size, usual, chooser_ref, early_ref, block_ref, *refs):
    *weights_refs, rows_ref, keep_ref, send_ref = refs
    block = jnp.concatenate(unpacked(block_ref, usual, rows_ref.shape[1]), axis=0)
    last = jnp.dot(chooser_ref[...], block, preferred_element_type=jnp.float32)
    rows_ref[...] = (early_ref[...].astype(jnp.float32) + last).astype(jnp.bfloat16)
    multiply(start, size, rows_ref, weights_refs, keep_ref, send_ref)


def later_kernel(start, size, rows_ref, *refs):
    *weights_refs, keep_ref, send_ref = refs
    multiply(start, size, rows_ref, weights_refs, keep_ref, send_ref)


def tight(own, n_x):
    return n_x == 2 and own % ROWS == ROWS // 2


def half_rows(own, segment, n_x):
    return 2 * own if tight(own, n_x) else n_x * segment


def row_ranges(own, segment, n_x, s):
    if not tight(own, n_x):
        return [(s * segment, 0, own)]
    whole = own // ROWS * ROWS
    return [(0, 0, own)] if s == 0 else [(own, whole, own), (whole + ROWS, 0, whole)]


def add_kernel(own, size, keep_ref, got_ref, own_ref, *out_refs):
    segment, width = own_ref.shape
    own_ref[...] = keep_ref[:segment] + got_ref[:segment]
    last = width - TILE
    spare = lax.broadcasted_iota(jnp.int32, (ROWS, TILE), 1) >= size - last
    for s, out_ref in enumerate(out_refs, 1):
        for t in range(-(-own // ROWS)):
            half = own - t * ROWS <= ROWS // 2
            shared = half and keep_ref.shape[0] == 2 * own
            at = t * ROWS if shared else s * segment + t * ROWS
            value = keep_ref[at : at + ROWS] + got_ref[at : at + ROWS]
            peak = jnp.max(jnp.abs(value), axis=1, keepdims=True)
            exponent = jnp.clip(jnp.ceil(jnp.log2(jnp.maximum(peak, 1e-30))), -90.0, 127.0)
            scaled = jnp.clip(jnp.round(value * jnp.exp2(15.0 - exponent)), -32767.0, 32767.0)
            ending = jnp.where(spare, exponent, scaled[:, last:])
            scaled = jnp.concatenate([scaled[:, :last], ending], axis=1) if last else ending
            if half:
                kept = slice(ROWS // 2, ROWS) if shared else slice(0, ROWS // 2)
                scaled = jnp.concatenate([scaled[kept, : width // 2], scaled[kept, width // 2 :]], axis=0)
            out_ref[:, t * width : t * width + scaled.shape[1]] = scaled.astype(jnp.int32).astype(jnp.int16)


def restored(own, size, width, got_ref, t):
    half = own - t * ROWS <= ROWS // 2
    value = got_ref[:, t * width : t * width + (width // 2 if half else width)]
    value = value.astype(jnp.int32).astype(jnp.float32)
    if half:
        value = jnp.concatenate([value[: ROWS // 2], value[ROWS // 2 :]], axis=1)
        value = jnp.concatenate([value, jnp.zeros_like(value)], axis=0)
    return value * jnp.exp2(value[:, size : size + 1] - 15.0)


def stats_kernel(own, size, *refs):
    *in_refs, guided_ref, out_ref = refs
    before = in_refs.pop(0) if in_refs[0].shape == out_ref.shape else None
    segment, width = guided_ref.shape
    real = lax.broadcasted_iota(jnp.int32, (ROWS, width), 1) < size
    tops, totals = [], []
    for t in range(segment // ROWS):
        rows = slice(t * ROWS, (t + 1) * ROWS)
        guided = in_refs[0][rows]
        if t * ROWS < own:
            for got in in_refs[1:]:
                guided = guided + restored(own, size, width, got, t)
        guided_ref[rows] = guided
        top = jnp.max(jnp.where(real, guided, -jnp.inf), axis=1, keepdims=True)
        tops.append(top)
        totals.append(jnp.sum(jnp.where(real, jnp.exp(guided - top), 0.0), axis=1, keepdims=True))
    top, total = as_row(jnp.concatenate(tops, axis=0)), as_row(jnp.concatenate(totals, axis=0))
    if before is not None:
        top, total = merged((top, total), (before[0:1, :segment], before[1:2, :segment]))
    out_ref[0:1, :segment] = top
    out_ref[1:2, :segment] = total


def merged(one, other):
    top = jnp.maximum(one[0], other[0])
    return top, one[1] * jnp.exp(one[0] - top) + other[1] * jnp.exp(other[0] - top)


def merge_kernel(one_ref, *refs):
    *other_refs, out_ref = refs
    top, total = one_ref[0:1], one_ref[1:2]
    for ref in other_refs:
        top, total = merged((top, total), (ref[0:1], ref[1:2]))
    out_ref[0:1] = top
    out_ref[1:2] = total


def final_kernel(sizes, segment, *refs):
    guided_refs, stats, (out_far, out_ref, sems) = refs[: len(sizes)], refs[len(sizes) : -3], refs[-3:]
    top, total = stats[0][0:1, :segment], stats[0][1:2, :segment]
    for ref in stats[1:]:
        top, total = merged((top, total), (ref[0:1, :segment], ref[1:2, :segment]))
    own = out_ref.shape[0]
    shift, log_total = as_column(top), as_column(jnp.log(total))
    copies = []
    for t, first in enumerate(range(0, own, ROWS)):
        rows = slice(first, min(first + ROWS, own))
        at = 0
        for ref, size in zip(guided_refs, sizes):
            out_ref[rows, at : at + size] = ref[rows, :size] - shift[rows] - log_total[rows]
            at += size
        copies.append(pltpu.make_async_copy(out_ref.at[rows], out_far.at[rows], sems.at[t]))
        copies[-1].start()
    for copy in copies:
        copy.wait()


def shifted(value, axis, by):
    size = lax.axis_size(axis)
    return lax.ppermute(value, axis, [(i, (i + by) % size) for i in range(size)])


def cut(vocab, widths):
    edges = [0]
    for width in widths:
        edges.append(min(vocab, edges[-1] + width))
    edges.append(vocab)
    return [(start, end - start) for start, end in zip(edges, edges[1:]) if end > start]


def padded(size):
    return -(-(size + 1) // TILE) * TILE


def packed_shape(own, width):
    blocks, rest = divmod(own, ROWS)
    lanes = blocks * width + (0 if rest == 0 else width // 2 if rest <= ROWS // 2 else width)
    return (ROWS, lanes)


def per_device(final_hidden, positions, norm_gain, unembedding):
    bf16, f32 = jnp.bfloat16, jnp.float32
    _, block, width_local = final_hidden.shape
    masked = positions.shape[0]
    vocab = unembedding.shape[1]
    n_z, n_x, n_c = lax.axis_size("vocab"), lax.axis_size("rows"), lax.axis_size("cfg")
    z, x, c = lax.axis_index("vocab"), lax.axis_index("rows"), lax.axis_index("cfg")
    own = masked // (n_x * n_c)
    segment = -(-(own + 1) // 16) * 16

    normed, squares, places = call(
        squares_kernel,
        [((2, block, width_local), bf16), ((2, block), f32), ((1, masked), jnp.int32)],
        [],
        far=[final_hidden, norm_gain[None, :], positions[None, :]],
        scratch_shapes=[
            pltpu.VMEM((2, block, width_local), bf16),
            pltpu.VMEM((1, width_local), f32),
            pltpu.SemaphoreType.DMA((4,)),
        ],
    )
    for axis in ("cfg", "rows"):
        squares = sum([shifted(squares, axis, s) for s in range(1, lax.axis_size(axis))], squares)
    usual = int(block * USUAL)
    skipped = usual // DEEP * DEEP
    compact, crowded = pl.pallas_call(
        functools.partial(compact_kernel, usual, n_z),
        out_shape=[pltpu.VMEM((block, block), bf16), jax.ShapeDtypeStruct((1, 1), jnp.int32)],
        in_specs=in_vmem(1),
        out_specs=[*in_vmem(1), pl.BlockSpec(memory_space=pltpu.SMEM)],
        compiler_params=pltpu.CompilerParams(vmem_limit_bytes=8 * MIB),
    )(*keep_in_vmem(places))
    block_rows, rest_rows = call(
        functools.partial(combine_kernel, width_local * n_x * n_c, usual),
        [((DEEP, usual * width_local // DEEP), bf16), ((block - skipped, width_local), bf16)],
        [normed, squares, compact],
    )

    weights = unembedding.T
    loads, loaded = cut(vocab, [width for group in LOADS for width in group]), []

    def load(count, after):
        nonlocal weights
        pieces = loads[len(loaded) : len(loaded) + count]
        if not pieces:
            return after
        weights, after = lax.optimization_barrier((weights, after))
        arrays = call(
            functools.partial(load_kernel, pieces[0][0]),
            [((width_local, size), bf16) for _, size in pieces],
            [],
            far=[weights],
            cost=(0, 2 * sum(size for _, size in pieces) * width_local),
            scratch_shapes=[pltpu.VMEM((SLOTS, TILE, width_local), bf16), pltpu.SemaphoreType.DMA((SLOTS,))],
        )
        *arrays, after = lax.optimization_barrier((*arrays, after))
        loaded.extend(arrays)
        return after

    def both_ways(own_block):
        ahead = behind = own_block
        gathered = [own_block]
        for step in range(1, n_z // 2 + 1):
            ahead = shifted(ahead, "vocab", 1)
            gathered.append(ahead)
            if 2 * step < n_z:
                behind = shifted(behind, "vocab", -1)
                gathered.append(behind)
        return gathered

    offsets = [0] + [sign * step for step in range(1, n_z // 2 + 1) for sign in (1, -1) if sign > 0 or 2 * step < n_z]
    rest = lax.cond(
        crowded[0, 0] > 0,
        lambda rest: jnp.concatenate(both_ways(rest), axis=0),
        lambda rest: jnp.zeros((n_z * rest.shape[0], rest.shape[1]), rest.dtype),
        rest_rows,
    )
    weights, places, rest = lax.optimization_barrier((weights, places, rest))
    ahead = shifted(block_rows, "vocab", 1)
    behind = load(len(LOADS[0]), block_rows)
    aheads, behinds = [ahead], []
    for step in range(1, (n_z - 1) // 2 + 1):
        behind = shifted(behind, "vocab", -1)
        behinds.append(behind)
    for step in range(2, n_z // 2 + 1):
        ahead = shifted(ahead, "vocab", 1)
        aheads.append(ahead)
    arrivals = [block_rows]
    for step in range(n_z // 2):
        arrivals += aheads[step : step + 1] + behinds[step : step + 1]

    half = half_rows(own, segment, n_x)
    selected, deep = n_c * half, -(-usual // DEEP) * DEEP
    early_chooser, last_chooser = call(
        functools.partial(chooser_kernel, own, block, usual, offsets, n_z, n_x, n_c),
        [((selected, (n_z - 1) * deep + n_z * (block - skipped)), bf16), ((selected, deep), bf16)],
        [places],
    )
    load(len(loads), aheads[0])
    early_chooser, last_chooser, *loaded = lax.optimization_barrier((early_chooser, last_chooser, *loaded))
    (early,) = call(
        functools.partial(early_kernel, usual),
        [((selected, width_local), bf16)],
        [early_chooser, *arrivals[:-1], rest],
    )

    chunks = cut(vocab, CHUNKS)
    parts, leaving = [], []
    for j, (start, size) in enumerate(chunks):
        width = padded(size)
        outs = [((half, width), f32)] * 2
        cost = (4 * half * width_local * size, 2 * width_local * size)
        needed = [i for i, (at, held) in enumerate(loads) if at < start + size and start < at + held]
        skip = start - loads[needed[0]][0]
        pieces = [loaded[i] for i in needed]
        if j == 0:
            rows, keep, send = call(
                functools.partial(first_kernel, skip, size, usual),
                [((selected, width_local), bf16)] + outs,
                [last_chooser, early, arrivals[-1], *pieces],
                cost=cost,
            )
        else:
            keep, send = call(functools.partial(later_kernel, skip, size), outs, [rows, *pieces], cost=cost)
        got = shifted(send, "cfg", 1)
        own_sum, *sends = call(
            functools.partial(add_kernel, own, size),
            [((segment, width), f32)] + [(packed_shape(own, width), jnp.int16)] * (n_x - 1),
            [keep, got],
        )
        parts.append(own_sum)
        leaving.append(sends)
    guided, stats = [], None
    for (_, size), own_sum, sends in zip(chunks, parts, leaving):
        got = [shifted(s_rows, "rows", s) for s, s_rows in enumerate(sends, 1)]
        chunk, stats = call(
            functools.partial(stats_kernel, own, size),
            [(own_sum.shape, f32), ((2, LANES), f32)],
            ([] if stats is None else [stats]) + [own_sum, *got],
        )
        guided.append(chunk)
    if n_z & (n_z - 1) == 0:
        all_stats = [stats] + [
            lax.ppermute(stats, "vocab", [(i, i ^ far) for i in range(n_z)]) for far in sorted(range(1, n_z), key=lambda far: [0,1,3,2][far % 4])
        ]
    else:
        all_stats = [stats] + [shifted(stats, "vocab", s) for s in range(1, n_z)]
    return pl.pallas_call(
        functools.partial(final_kernel, [size for _, size in chunks], segment),
        out_shape=jax.ShapeDtypeStruct((own, vocab), f32),
        in_specs=in_vmem(len(guided) + len(all_stats)),
        out_specs=pl.BlockSpec(memory_space=pltpu.HBM),
        scratch_shapes=[pltpu.VMEM((own, vocab), f32), pltpu.SemaphoreType.DMA((-(-own // ROWS),))],
        compiler_params=pltpu.CompilerParams(vmem_limit_bytes=8 * MIB),
    )(*keep_in_vmem(*guided, *all_stats))


def solution(mesh):
    placed = (
        P(None, ("groups", "vocab"), ("rows", "cfg")),
        P("groups"),
        P(("rows", "cfg")),
        P(("rows", "cfg"), "vocab"),
    )
    return jax.shard_map(
        per_device,
        mesh=mesh,
        in_specs=placed,
        out_specs=P(("groups", "rows", "cfg"), "vocab"),
        check_vma=False,
    )
```

```python
import functools

import jax
import jax.numpy as jnp
from jax import lax
from jax.experimental import pallas as pl
from jax.experimental.pallas import tpu as pltpu
from jax.sharding import PartitionSpec as P

epsilon = 1e-06
guidance = 2.0
TILE = 256
LANES = 128
MIB = 1 << 20
LOADS = ((512,), (1984,))
SLOTS = 5
CHUNKS = (2496,)
ROWS = 8
USUAL = 13 / 16
DEEP = 16


def in_vmem(count):
    return [pl.BlockSpec(memory_space=pltpu.VMEM)] * count


def keep_in_vmem(*arrays):
    return [pltpu.with_memory_space_constraint(a, pltpu.VMEM) for a in arrays]


def call(body, outs, args, far=(), limit=8, cost=None, **kwargs):
    return pl.pallas_call(
        body,
        out_shape=[pltpu.VMEM(shape, dtype) for shape, dtype in outs],
        in_specs=[pl.BlockSpec(memory_space=pltpu.HBM)] * len(far) + in_vmem(len(args)),
        out_specs=in_vmem(len(outs)),
        compiler_params=pltpu.CompilerParams(vmem_limit_bytes=limit * MIB),
        cost_estimate=cost and pl.CostEstimate(flops=cost[0], bytes_accessed=cost[1], transcendentals=0),
        **kwargs,
    )(*[pltpu.with_memory_space_constraint(a, pltpu.HBM) for a in far], *keep_in_vmem(*args))


def diagonal(n):
    return lax.broadcasted_iota(jnp.int32, (n, n), 0) == lax.broadcasted_iota(jnp.int32, (n, n), 1)


def as_column(row):
    return jnp.sum(jnp.where(diagonal(row.shape[1]), row, 0.0), axis=1, keepdims=True)


def as_row(column):
    return jnp.sum(jnp.where(diagonal(column.shape[0]), column, 0.0), axis=0, keepdims=True)


def squares_kernel(hidden_far, gain_far, places_far, hidden_ref, gain_ref, places_ref, out_ref, sems):
    block = hidden_ref.shape[1]
    copies = [pltpu.make_async_copy(hidden_far.at[b], hidden_ref.at[b], sems.at[b]) for b in range(2)]
    copies += [
        pltpu.make_async_copy(gain_far, gain_ref, sems.at[2]),
        pltpu.make_async_copy(places_far, places_ref, sems.at[3]),
    ]
    for copy in copies:
        copy.start()
    for b in range(2):
        copies[b].wait()
        widened = hidden_ref[b].astype(jnp.float32)
        out_ref[b : b + 1] = as_row(jnp.sum(widened * widened, axis=1, keepdims=True))
    for copy in copies[2:]:
        copy.wait()


def first_rank(positions_ref, at):
    return jnp.sum((positions_ref[...] < at).astype(jnp.float32), axis=1, keepdims=True).astype(jnp.int32)


def compact_kernel(usual, n_z, positions_ref, hidden_ref, gain_ref, compact_ref, normed_ref, crowded_ref):
    block, masked = compact_ref.shape[0], positions_ref.shape[1]
    ranks = [first_rank(positions_ref, b * block) for b in range(n_z + 1)]
    most = functools.reduce(jnp.maximum, [end - first for first, end in zip(ranks, ranks[1:])])
    crowded_ref[0, 0] = (jnp.max(most) > usual).astype(jnp.int32)
    at = lax.axis_index("vocab") * block
    first = first_rank(positions_ref, at)
    rank = lax.broadcasted_iota(jnp.int32, (block, masked), 1)
    match = rank == first + lax.broadcasted_iota(jnp.int32, (block, masked), 0)
    places = (positions_ref[...] + 1).astype(jnp.float32)
    wanted = jnp.sum(jnp.where(match, places, 0.0), axis=1, keepdims=True).astype(jnp.int32) - 1
    held = at + lax.broadcasted_iota(jnp.int32, (block, block), 1)
    compact = (wanted == held).astype(jnp.float32)
    compact_ref[...] = compact
    for b in range(2):
        normed = (hidden_ref[b].astype(jnp.float32) * gain_ref[...]).astype(jnp.bfloat16)
        normed = jnp.dot(compact.astype(jnp.bfloat16), normed, preferred_element_type=jnp.float32)
        normed_ref[b] = normed.astype(jnp.bfloat16)


def combine_kernel(width, usual, normed_ref, totals_ref, compact_ref, usual_ref, rest_ref):
    inv_rms = lax.rsqrt(totals_ref[...] / width + epsilon)
    place = compact_ref[...] > 0.5
    weight = [(1.0 + guidance) * inv_rms[0:1], guidance * inv_rms[1:2]]
    factor = [jnp.sum(jnp.where(place, row, 0.0), axis=1, keepdims=True) for row in weight]
    terms = [factor[b] * normed_ref[b].astype(jnp.float32) for b in range(2)]
    rows = terms[0] - terms[1]
    whole, last = divmod(usual, DEEP)
    columns = rows.shape[1]
    for t in range(whole):
        usual_ref[:, t * columns : (t + 1) * columns] = rows[t * DEEP : (t + 1) * DEEP].astype(jnp.bfloat16)
    if last:
        share = columns * last // DEEP
        ending = rows[whole * DEEP : usual]
        ending = jnp.concatenate([ending[:, at : at + share] for at in range(0, columns, share)], axis=0)
        usual_ref[:, whole * columns :] = ending.astype(jnp.bfloat16)
    rest_ref[...] = rows[whole * DEEP :].astype(jnp.bfloat16)


def unpacked(ref, usual, columns):
    whole, last = divmod(usual, DEEP)
    blocks = [ref[:, t * columns : (t + 1) * columns] for t in range(whole)]
    if last:
        ending = ref[:, whole * columns :].astype(jnp.float32)
        ending = jnp.concatenate([ending[at : at + last] for at in range(0, DEEP, last)], axis=1)
        ending = jnp.concatenate([ending, jnp.zeros((DEEP - last, columns), jnp.float32)], axis=0)
        blocks.append(ending.astype(jnp.bfloat16))
    return blocks


def load_kernel(start, weights_far, *refs):
    *out_refs, tiles_ref, sems = refs
    slots = tiles_ref.shape[0]
    tiles = []
    for ref in out_refs:
        size = ref.shape[1]
        tiles += [(ref, at, min(TILE, size - at), start + at) for at in range(0, size, TILE)]
        start += size
    copies = [
        pltpu.make_async_copy(
            weights_far.at[pl.ds(column, rows)],
            tiles_ref.at[i % slots, pl.ds(0, rows)],
            sems.at[i % slots],
        )
        for i, (_, _, rows, column) in enumerate(tiles)
    ]
    for copy in copies[:slots]:
        copy.start()
    for i, (ref, at, rows, _) in enumerate(tiles):
        copies[i].wait()
        ref[:, at : at + rows] = tiles_ref[i % slots, :rows].T
        if i + slots < len(tiles):
            copies[i + slots].start()


def chooser_kernel(own, block, usual, offsets, n_z, n_x, n_c, positions_ref, early_ref, last_ref):
    z, x, c = (lax.axis_index(axis) for axis in ("vocab", "rows", "cfg"))
    rows, deep = last_ref.shape
    half = rows // n_c
    segment = -(-own // ROWS) * ROWS if tight(own, n_x) else half // n_x
    row = lax.broadcasted_iota(jnp.int32, (rows, 1), 0)
    wanted = jnp.full((rows, 1), -1, jnp.int32)
    for t in range(n_c):
        for s in range(n_x):
            owner = lax.rem(x + s, n_x) * n_c + lax.rem(c + t, n_c)
            for at, first, end in row_ranges(own, segment, n_x, s):
                i = row - (t * half + at) + first
                wanted = jnp.where((i >= first) & (i < end), owner * own + i, wanted)
    lane = lax.broadcasted_iota(jnp.int32, (1, early_ref.shape[1]), 1)
    held = jnp.full(lane.shape, -2, jnp.int32)
    skipped = usual // DEEP * DEEP
    for k, offset in enumerate(offsets):
        at = lax.rem(z - offset + n_z, n_z) * block
        first, end = first_rank(positions_ref, at), first_rank(positions_ref, at + block)
        if k < n_z - 1:
            i = lane - k * deep
            held = jnp.where((i >= 0) & (i < usual) & (first + i < end), first + i, held)
        else:
            i = lax.broadcasted_iota(jnp.int32, (1, deep), 1)
            last = jnp.where((i < usual) & (first + i < end), first + i, -2)
        i = lane - (n_z - 1) * deep - k * (block - skipped) + skipped
        held = jnp.where((i >= usual) & (i < block) & (first + i < end), first + i, held)
    early_ref[...] = (wanted == held).astype(jnp.float32).astype(jnp.bfloat16)
    last_ref[...] = (wanted == last).astype(jnp.float32).astype(jnp.bfloat16)


def multiply(start, size, rows_ref, weights_refs, keep_ref, send_ref):
    half, width = keep_ref.shape
    at, skip = 0, start
    for ref in weights_refs:
        held = ref.shape[1]
        while at < size and skip < held:
            step = min(TILE, size - at, held - skip)
            product = jnp.dot(rows_ref[...], ref[:, skip : skip + step], preferred_element_type=jnp.float32)
            keep_ref[:, at : at + step] = product[:half]
            send_ref[:, at : at + step] = product[half:]
            at, skip = at + step, skip + step
        skip = max(0, skip - held)
    for ref in (keep_ref, send_ref):
        ref[:, size:] = jnp.zeros((half, width - size), jnp.float32)


def early_kernel(usual, chooser_ref, *refs):
    *block_refs, rest_ref, rows_ref = refs
    blocks = [part for ref in block_refs for part in unpacked(ref, usual, rows_ref.shape[1])]
    blocks = jnp.concatenate([*blocks, rest_ref[...]], axis=0)
    rows_ref[...] = jnp.dot(chooser_ref[...], blocks, preferred_element_type=jnp.float32).astype(jnp.bfloat16)


def first_kernel(start, size, usual, chooser_ref, early_ref, block_ref, *refs):
    *weights_refs, rows_ref, keep_ref, send_ref = refs
    block = jnp.concatenate(unpacked(block_ref, usual, rows_ref.shape[1]), axis=0)
    last = jnp.dot(chooser_ref[...], block, preferred_element_type=jnp.float32)
    rows_ref[...] = (early_ref[...].astype(jnp.float32) + last).astype(jnp.bfloat16)
    multiply(start, size, rows_ref, weights_refs, keep_ref, send_ref)


def later_kernel(start, size, rows_ref, *refs):
    *weights_refs, keep_ref, send_ref = refs
    multiply(start, size, rows_ref, weights_refs, keep_ref, send_ref)


def tight(own, n_x):
    return n_x == 2 and own % ROWS == ROWS // 2


def half_rows(own, segment, n_x):
    return 2 * own if tight(own, n_x) else n_x * segment


def row_ranges(own, segment, n_x, s):
    if not tight(own, n_x):
        return [(s * segment, 0, own)]
    whole = own // ROWS * ROWS
    return [(0, 0, own)] if s == 0 else [(own, whole, own), (whole + ROWS, 0, whole)]


def add_kernel(own, size, keep_ref, got_ref, own_ref, *out_refs):
    segment, width = own_ref.shape
    own_ref[...] = keep_ref[:segment] + got_ref[:segment]
    last = width - TILE
    spare = lax.broadcasted_iota(jnp.int32, (ROWS, TILE), 1) >= size - last
    for s, out_ref in enumerate(out_refs, 1):
        for t in range(-(-own // ROWS)):
            half = own - t * ROWS <= ROWS // 2
            shared = half and keep_ref.shape[0] == 2 * own
            at = t * ROWS if shared else s * segment + t * ROWS
            value = keep_ref[at : at + ROWS] + got_ref[at : at + ROWS]
            peak = jnp.max(jnp.abs(value), axis=1, keepdims=True)
            exponent = jnp.clip(jnp.ceil(jnp.log2(jnp.maximum(peak, 1e-30))), -90.0, 127.0)
            scaled = jnp.clip(jnp.round(value * jnp.exp2(15.0 - exponent)), -32767.0, 32767.0)
            ending = jnp.where(spare, exponent, scaled[:, last:])
            scaled = jnp.concatenate([scaled[:, :last], ending], axis=1) if last else ending
            if half:
                kept = slice(ROWS // 2, ROWS) if shared else slice(0, ROWS // 2)
                scaled = jnp.concatenate([scaled[kept, : width // 2], scaled[kept, width // 2 :]], axis=0)
            out_ref[:, t * width : t * width + scaled.shape[1]] = scaled.astype(jnp.int32).astype(jnp.int16)


def restored(own, size, width, got_ref, t):
    half = own - t * ROWS <= ROWS // 2
    value = got_ref[:, t * width : t * width + (width // 2 if half else width)]
    value = value.astype(jnp.int32).astype(jnp.float32)
    if half:
        value = jnp.concatenate([value[: ROWS // 2], value[ROWS // 2 :]], axis=1)
        value = jnp.concatenate([value, jnp.zeros_like(value)], axis=0)
    return value * jnp.exp2(value[:, size : size + 1] - 15.0)


def stats_kernel(own, size, *refs):
    *in_refs, guided_ref, out_ref = refs
    before = in_refs.pop(0) if in_refs[0].shape == out_ref.shape else None
    segment, width = guided_ref.shape
    real = lax.broadcasted_iota(jnp.int32, (ROWS, width), 1) < size
    tops, totals = [], []
    for t in range(segment // ROWS):
        rows = slice(t * ROWS, (t + 1) * ROWS)
        guided = in_refs[0][rows]
        if t * ROWS < own:
            for got in in_refs[1:]:
                guided = guided + restored(own, size, width, got, t)
        guided_ref[rows] = guided
        top = jnp.max(jnp.where(real, guided, -jnp.inf), axis=1, keepdims=True)
        tops.append(top)
        totals.append(jnp.sum(jnp.where(real, jnp.exp(guided - top), 0.0), axis=1, keepdims=True))
    top, total = as_row(jnp.concatenate(tops, axis=0)), as_row(jnp.concatenate(totals, axis=0))
    if before is not None:
        top, total = merged((top, total), (before[0:1, :segment], before[1:2, :segment]))
    out_ref[0:1, :segment] = top
    out_ref[1:2, :segment] = total


def merged(one, other):
    top = jnp.maximum(one[0], other[0])
    return top, one[1] * jnp.exp(one[0] - top) + other[1] * jnp.exp(other[0] - top)


def merge_kernel(one_ref, *refs):
    *other_refs, out_ref = refs
    top, total = one_ref[0:1], one_ref[1:2]
    for ref in other_refs:
        top, total = merged((top, total), (ref[0:1], ref[1:2]))
    out_ref[0:1] = top
    out_ref[1:2] = total


def final_kernel(sizes, segment, *refs):
    guided_refs, stats, (out_far, out_ref, sems) = refs[: len(sizes)], refs[len(sizes) : -3], refs[-3:]
    top, total = stats[0][0:1, :segment], stats[0][1:2, :segment]
    for ref in stats[1:]:
        top, total = merged((top, total), (ref[0:1, :segment], ref[1:2, :segment]))
    own = out_ref.shape[0]
    shift, log_total = as_column(top), as_column(jnp.log(total))
    copies = []
    for t, first in enumerate(range(0, own, ROWS)):
        rows = slice(first, min(first + ROWS, own))
        at = 0
        for ref, size in zip(guided_refs, sizes):
            out_ref[rows, at : at + size] = ref[rows, :size] - shift[rows] - log_total[rows]
            at += size
        copies.append(pltpu.make_async_copy(out_ref.at[rows], out_far.at[rows], sems.at[t]))
        copies[-1].start()
    for copy in copies:
        copy.wait()


def shifted(value, axis, by):
    size = lax.axis_size(axis)
    return lax.ppermute(value, axis, [(i, (i + by) % size) for i in range(size)])


def cut(vocab, widths):
    edges = [0]
    for width in widths:
        edges.append(min(vocab, edges[-1] + width))
    edges.append(vocab)
    return [(start, end - start) for start, end in zip(edges, edges[1:]) if end > start]


def padded(size):
    return -(-(size + 1) // TILE) * TILE


def packed_shape(own, width):
    blocks, rest = divmod(own, ROWS)
    lanes = blocks * width + (0 if rest == 0 else width // 2 if rest <= ROWS // 2 else width)
    return (ROWS, lanes)


def per_device(final_hidden, positions, norm_gain, unembedding):
    bf16, f32 = jnp.bfloat16, jnp.float32
    _, block, width_local = final_hidden.shape
    masked = positions.shape[0]
    vocab = unembedding.shape[1]
    n_z, n_x, n_c = lax.axis_size("vocab"), lax.axis_size("rows"), lax.axis_size("cfg")
    z, x, c = lax.axis_index("vocab"), lax.axis_index("rows"), lax.axis_index("cfg")
    own = masked // (n_x * n_c)
    segment = -(-(own + 1) // 16) * 16

    hidden, gain, places, squares = call(
        squares_kernel,
        [((2, block, width_local), bf16), ((1, width_local), f32), ((1, masked), jnp.int32), ((2, block), f32)],
        [],
        far=[final_hidden, norm_gain[None, :], positions[None, :]],
        scratch_shapes=[pltpu.SemaphoreType.DMA((4,))],
    )
    for axis in ("cfg", "rows"):
        squares = sum([shifted(squares, axis, s) for s in range(1, lax.axis_size(axis))], squares)
    usual = int(block * USUAL)
    skipped = usual // DEEP * DEEP
    compact, normed, crowded = pl.pallas_call(
        functools.partial(compact_kernel, usual, n_z),
        out_shape=[
            pltpu.VMEM((block, block), f32),
            pltpu.VMEM((2, block, width_local), bf16),
            jax.ShapeDtypeStruct((1, 1), jnp.int32),
        ],
        in_specs=in_vmem(3),
        out_specs=[*in_vmem(2), pl.BlockSpec(memory_space=pltpu.SMEM)],
        compiler_params=pltpu.CompilerParams(vmem_limit_bytes=8 * MIB),
    )(*keep_in_vmem(places, hidden, gain))
    block_rows, rest_rows = call(
        functools.partial(combine_kernel, width_local * n_x * n_c, usual),
        [((DEEP, usual * width_local // DEEP), bf16), ((block - skipped, width_local), bf16)],
        [normed, squares, compact],
    )

    weights = unembedding.T
    loads, loaded = cut(vocab, [width for group in LOADS for width in group]), []

    def load(count, after):
        nonlocal weights
        pieces = loads[len(loaded) : len(loaded) + count]
        if not pieces:
            return after
        weights, after = lax.optimization_barrier((weights, after))
        arrays = call(
            functools.partial(load_kernel, pieces[0][0]),
            [((width_local, size), bf16) for _, size in pieces],
            [],
            far=[weights],
            cost=(0, 2 * sum(size for _, size in pieces) * width_local),
            scratch_shapes=[pltpu.VMEM((SLOTS, TILE, width_local), bf16), pltpu.SemaphoreType.DMA((SLOTS,))],
        )
        *arrays, after = lax.optimization_barrier((*arrays, after))
        loaded.extend(arrays)
        return after

    def both_ways(own_block):
        ahead = behind = own_block
        gathered = [own_block]
        for step in range(1, n_z // 2 + 1):
            ahead = shifted(ahead, "vocab", 1)
            gathered.append(ahead)
            if 2 * step < n_z:
                behind = shifted(behind, "vocab", -1)
                gathered.append(behind)
        return gathered

    offsets = [0] + [sign * step for step in range(1, n_z // 2 + 1) for sign in (1, -1) if sign > 0 or 2 * step < n_z]
    rest = lax.cond(
        crowded[0, 0] > 0,
        lambda rest: jnp.concatenate(both_ways(rest), axis=0),
        lambda rest: jnp.zeros((n_z * rest.shape[0], rest.shape[1]), rest.dtype),
        rest_rows,
    )
    weights, places, rest = lax.optimization_barrier((weights, places, rest))
    ahead = shifted(block_rows, "vocab", 1)
    behind = load(len(LOADS[0]), block_rows)
    aheads, behinds = [ahead], []
    for step in range(1, (n_z - 1) // 2 + 1):
        behind = shifted(behind, "vocab", -1)
        behinds.append(behind)
    for step in range(2, n_z // 2 + 1):
        ahead = shifted(ahead, "vocab", 1)
        aheads.append(ahead)
    arrivals = [block_rows]
    for step in range(n_z // 2):
        arrivals += aheads[step : step + 1] + behinds[step : step + 1]

    half = half_rows(own, segment, n_x)
    selected, deep = n_c * half, -(-usual // DEEP) * DEEP
    early_chooser, last_chooser = call(
        functools.partial(chooser_kernel, own, block, usual, offsets, n_z, n_x, n_c),
        [((selected, (n_z - 1) * deep + n_z * (block - skipped)), bf16), ((selected, deep), bf16)],
        [places],
    )
    load(len(loads), aheads[0])
    early_chooser, last_chooser, *loaded = lax.optimization_barrier((early_chooser, last_chooser, *loaded))
    (early,) = call(
        functools.partial(early_kernel, usual),
        [((selected, width_local), bf16)],
        [early_chooser, *arrivals[:-1], rest],
    )

    chunks = cut(vocab, CHUNKS)
    parts, leaving = [], []
    for j, (start, size) in enumerate(chunks):
        width = padded(size)
        outs = [((half, width), f32)] * 2
        cost = (4 * half * width_local * size, 2 * width_local * size)
        needed = [i for i, (at, held) in enumerate(loads) if at < start + size and start < at + held]
        skip = start - loads[needed[0]][0]
        pieces = [loaded[i] for i in needed]
        if j == 0:
            rows, keep, send = call(
                functools.partial(first_kernel, skip, size, usual),
                [((selected, width_local), bf16)] + outs,
                [last_chooser, early, arrivals[-1], *pieces],
                cost=cost,
            )
        else:
            keep, send = call(functools.partial(later_kernel, skip, size), outs, [rows, *pieces], cost=cost)
        got = shifted(send, "cfg", 1)
        own_sum, *sends = call(
            functools.partial(add_kernel, own, size),
            [((segment, width), f32)] + [(packed_shape(own, width), jnp.int16)] * (n_x - 1),
            [keep, got],
        )
        parts.append(own_sum)
        leaving.append(sends)
    guided, stats = [], None
    for (_, size), own_sum, sends in zip(chunks, parts, leaving):
        got = [shifted(s_rows, "rows", s) for s, s_rows in enumerate(sends, 1)]
        chunk, stats = call(
            functools.partial(stats_kernel, own, size),
            [(own_sum.shape, f32), ((2, LANES), f32)],
            ([] if stats is None else [stats]) + [own_sum, *got],
        )
        guided.append(chunk)
    if n_z & (n_z - 1) == 0:
        all_stats = [stats] + [
            lax.ppermute(stats, "vocab", [(i, i ^ far) for i in range(n_z)]) for far in sorted(range(1, n_z), key=lambda far: [0,1,3,2][far % 4])
        ]
    else:
        all_stats = [stats] + [shifted(stats, "vocab", s) for s in range(1, n_z)]
    return pl.pallas_call(
        functools.partial(final_kernel, [size for _, size in chunks], segment),
        out_shape=jax.ShapeDtypeStruct((own, vocab), f32),
        in_specs=in_vmem(len(guided) + len(all_stats)),
        out_specs=pl.BlockSpec(memory_space=pltpu.HBM),
        scratch_shapes=[pltpu.VMEM((own, vocab), f32), pltpu.SemaphoreType.DMA((-(-own // ROWS),))],
        compiler_params=pltpu.CompilerParams(vmem_limit_bytes=8 * MIB),
    )(*keep_in_vmem(*guided, *all_stats))


def solution(mesh):
    placed = (
        P(None, ("groups", "vocab"), ("rows", "cfg")),
        P("groups"),
        P(("rows", "cfg")),
        P(("rows", "cfg"), "vocab"),
    )
    return jax.shard_map(
        per_device,
        mesh=mesh,
        in_specs=placed,
        out_specs=P(("groups", "rows", "cfg"), "vocab"),
        check_vma=False,
    )
```

```python
import functools

import jax
import jax.numpy as jnp
from jax import lax
from jax.experimental import pallas as pl
from jax.experimental.pallas import tpu as pltpu
from jax.sharding import PartitionSpec as P

epsilon = 1e-06
guidance = 2.0
TILE = 256
LANES = 128
MIB = 1 << 20
LOADS = ((512,), (1984,))
SLOTS = 8
CHUNKS = (2496,)
ROWS = 8
USUAL = 13 / 16
DEEP = 16


def in_vmem(count):
    return [pl.BlockSpec(memory_space=pltpu.VMEM)] * count


def keep_in_vmem(*arrays):
    return [pltpu.with_memory_space_constraint(a, pltpu.VMEM) for a in arrays]


def call(body, outs, args, far=(), limit=12, cost=None, **kwargs):
    return pl.pallas_call(
        body,
        out_shape=[pltpu.VMEM(shape, dtype) for shape, dtype in outs],
        in_specs=[pl.BlockSpec(memory_space=pltpu.HBM)] * len(far) + in_vmem(len(args)),
        out_specs=in_vmem(len(outs)),
        compiler_params=pltpu.CompilerParams(vmem_limit_bytes=limit * MIB),
        cost_estimate=cost and pl.CostEstimate(flops=cost[0], bytes_accessed=cost[1], transcendentals=0),
        **kwargs,
    )(*[pltpu.with_memory_space_constraint(a, pltpu.HBM) for a in far], *keep_in_vmem(*args))


def diagonal(n):
    return lax.broadcasted_iota(jnp.int32, (n, n), 0) == lax.broadcasted_iota(jnp.int32, (n, n), 1)


def as_column(row):
    return jnp.sum(jnp.where(diagonal(row.shape[1]), row, 0.0), axis=1, keepdims=True)


def as_row(column):
    return jnp.sum(jnp.where(diagonal(column.shape[0]), column, 0.0), axis=0, keepdims=True)


def squares_kernel(hidden_far, gain_far, places_far, hidden_ref, gain_ref, places_ref, out_ref, sems):
    copies = [
        pltpu.make_async_copy(hidden_far, hidden_ref, sems.at[0]),
        pltpu.make_async_copy(gain_far, gain_ref, sems.at[1]),
        pltpu.make_async_copy(places_far, places_ref, sems.at[2]),
    ]
    for copy in copies:
        copy.start()
    copies[0].wait()
    for b in range(2):
        widened = hidden_ref[b].astype(jnp.float32)
        out_ref[b : b + 1] = as_row(jnp.sum(widened * widened, axis=1, keepdims=True))
    for copy in copies[1:]:
        copy.wait()


def first_rank(positions_ref, at):
    return jnp.sum((positions_ref[...] < at).astype(jnp.float32), axis=1, keepdims=True).astype(jnp.int32)


def compact_kernel(usual, n_z, positions_ref, hidden_ref, gain_ref, compact_ref, normed_ref, crowded_ref):
    block, masked = compact_ref.shape[0], positions_ref.shape[1]
    ranks = [first_rank(positions_ref, b * block) for b in range(n_z + 1)]
    most = functools.reduce(jnp.maximum, [end - first for first, end in zip(ranks, ranks[1:])])
    crowded_ref[0, 0] = (jnp.max(most) > usual).astype(jnp.int32)
    at = lax.axis_index("vocab") * block
    first = first_rank(positions_ref, at)
    rank = lax.broadcasted_iota(jnp.int32, (block, masked), 1)
    match = rank == first + lax.broadcasted_iota(jnp.int32, (block, masked), 0)
    places = (positions_ref[...] + 1).astype(jnp.float32)
    wanted = jnp.sum(jnp.where(match, places, 0.0), axis=1, keepdims=True).astype(jnp.int32) - 1
    held = at + lax.broadcasted_iota(jnp.int32, (block, block), 1)
    compact = (wanted == held).astype(jnp.float32)
    compact_ref[...] = compact
    for b in range(2):
        normed = (hidden_ref[b].astype(jnp.float32) * gain_ref[...]).astype(jnp.bfloat16)
        normed = jnp.dot(compact.astype(jnp.bfloat16), normed, preferred_element_type=jnp.float32)
        normed_ref[b] = normed.astype(jnp.bfloat16)


def combine_kernel(width, usual, normed_ref, totals_ref, compact_ref, usual_ref, rest_ref):
    inv_rms = lax.rsqrt(totals_ref[...] / width + epsilon)
    place = compact_ref[...] > 0.5
    weight = [(1.0 + guidance) * inv_rms[0:1], guidance * inv_rms[1:2]]
    factor = [jnp.sum(jnp.where(place, row, 0.0), axis=1, keepdims=True) for row in weight]
    terms = [factor[b] * normed_ref[b].astype(jnp.float32) for b in range(2)]
    rows = terms[0] - terms[1]
    whole, last = divmod(usual, DEEP)
    columns = rows.shape[1]
    for t in range(whole):
        usual_ref[:, t * columns : (t + 1) * columns] = rows[t * DEEP : (t + 1) * DEEP].astype(jnp.bfloat16)
    if last:
        share = columns * last // DEEP
        ending = rows[whole * DEEP : usual]
        ending = jnp.concatenate([ending[:, at : at + share] for at in range(0, columns, share)], axis=0)
        usual_ref[:, whole * columns :] = ending.astype(jnp.bfloat16)
    rest_ref[...] = rows[whole * DEEP :].astype(jnp.bfloat16)


def unpacked(ref, usual, columns):
    whole, last = divmod(usual, DEEP)
    blocks = [ref[:, t * columns : (t + 1) * columns] for t in range(whole)]
    if last:
        ending = ref[:, whole * columns :].astype(jnp.float32)
        ending = jnp.concatenate([ending[at : at + last] for at in range(0, DEEP, last)], axis=1)
        ending = jnp.concatenate([ending, jnp.zeros((DEEP - last, columns), jnp.float32)], axis=0)
        blocks.append(ending.astype(jnp.bfloat16))
    return blocks


def load_kernel(start, weights_far, *refs):
    *out_refs, tiles_ref, sems = refs
    slots = tiles_ref.shape[0]
    tiles = []
    for ref in out_refs:
        size = ref.shape[1]
        tiles += [(ref, at, min(TILE, size - at), start + at) for at in range(0, size, TILE)]
        start += size
    copies = [
        pltpu.make_async_copy(
            weights_far.at[pl.ds(column, rows)],
            tiles_ref.at[i % slots, pl.ds(0, rows)],
            sems.at[i % slots],
        )
        for i, (_, _, rows, column) in enumerate(tiles)
    ]
    for copy in copies[:slots]:
        copy.start()
    for i, (ref, at, rows, _) in enumerate(tiles):
        copies[i].wait()
        ref[:, at : at + rows] = tiles_ref[i % slots, :rows].T
        if i + slots < len(tiles):
            copies[i + slots].start()


def chooser_kernel(own, block, usual, offsets, n_z, n_x, n_c, positions_ref, early_ref, last_ref):
    z, x, c = (lax.axis_index(axis) for axis in ("vocab", "rows", "cfg"))
    rows, deep = last_ref.shape
    half = rows // n_c
    segment = -(-own // ROWS) * ROWS if tight(own, n_x) else half // n_x
    row = lax.broadcasted_iota(jnp.int32, (rows, 1), 0)
    wanted = jnp.full((rows, 1), -1, jnp.int32)
    for t in range(n_c):
        for s in range(n_x):
            owner = lax.rem(x + s, n_x) * n_c + lax.rem(c + t, n_c)
            for at, first, end in row_ranges(own, segment, n_x, s):
                i = row - (t * half + at) + first
                wanted = jnp.where((i >= first) & (i < end), owner * own + i, wanted)
    lane = lax.broadcasted_iota(jnp.int32, (1, early_ref.shape[1]), 1)
    held = jnp.full(lane.shape, -2, jnp.int32)
    skipped = usual // DEEP * DEEP
    for k, offset in enumerate(offsets):
        at = lax.rem(z - offset + n_z, n_z) * block
        first, end = first_rank(positions_ref, at), first_rank(positions_ref, at + block)
        if k < n_z - 1:
            i = lane - k * deep
            held = jnp.where((i >= 0) & (i < usual) & (first + i < end), first + i, held)
        else:
            i = lax.broadcasted_iota(jnp.int32, (1, deep), 1)
            last = jnp.where((i < usual) & (first + i < end), first + i, -2)
        i = lane - (n_z - 1) * deep - k * (block - skipped) + skipped
        held = jnp.where((i >= usual) & (i < block) & (first + i < end), first + i, held)
    early_ref[...] = (wanted == held).astype(jnp.float32).astype(jnp.bfloat16)
    last_ref[...] = (wanted == last).astype(jnp.float32).astype(jnp.bfloat16)


def multiply(start, size, rows_ref, weights_refs, keep_ref, send_ref):
    half, width = keep_ref.shape
    at, skip = 0, start
    for ref in weights_refs:
        held = ref.shape[1]
        while at < size and skip < held:
            step = min(TILE, size - at, held - skip)
            product = jnp.dot(rows_ref[...], ref[:, skip : skip + step], preferred_element_type=jnp.float32)
            keep_ref[:, at : at + step] = product[:half]
            send_ref[:, at : at + step] = product[half:]
            at, skip = at + step, skip + step
        skip = max(0, skip - held)
    for ref in (keep_ref, send_ref):
        ref[:, size:] = jnp.zeros((half, width - size), jnp.float32)


def early_kernel(usual, chooser_ref, *refs):
    *block_refs, rest_ref, rows_ref = refs
    blocks = [part for ref in block_refs for part in unpacked(ref, usual, rows_ref.shape[1])]
    blocks = jnp.concatenate([*blocks, rest_ref[...]], axis=0)
    rows_ref[...] = jnp.dot(chooser_ref[...], blocks, preferred_element_type=jnp.float32).astype(jnp.bfloat16)


def first_kernel(start, size, usual, chooser_ref, early_ref, block_ref, *refs):
    *weights_refs, rows_ref, keep_ref, send_ref = refs
    block = jnp.concatenate(unpacked(block_ref, usual, rows_ref.shape[1]), axis=0)
    last = jnp.dot(chooser_ref[...], block, preferred_element_type=jnp.float32)
    rows_ref[...] = (early_ref[...].astype(jnp.float32) + last).astype(jnp.bfloat16)
    multiply(start, size, rows_ref, weights_refs, keep_ref, send_ref)


def later_kernel(start, size, rows_ref, *refs):
    *weights_refs, keep_ref, send_ref = refs
    multiply(start, size, rows_ref, weights_refs, keep_ref, send_ref)


def tight(own, n_x):
    return n_x == 2 and own % ROWS == ROWS // 2


def half_rows(own, segment, n_x):
    return 2 * own if tight(own, n_x) else n_x * segment


def row_ranges(own, segment, n_x, s):
    if not tight(own, n_x):
        return [(s * segment, 0, own)]
    whole = own // ROWS * ROWS
    return [(0, 0, own)] if s == 0 else [(own, whole, own), (whole + ROWS, 0, whole)]


def add_kernel(own, size, keep_ref, got_ref, own_ref, *out_refs):
    segment, width = own_ref.shape
    own_ref[...] = keep_ref[:segment] + got_ref[:segment]
    last = width - TILE
    spare = lax.broadcasted_iota(jnp.int32, (ROWS, TILE), 1) >= size - last
    for s, out_ref in enumerate(out_refs, 1):
        for t in range(-(-own // ROWS)):
            half = own - t * ROWS <= ROWS // 2
            shared = half and keep_ref.shape[0] == 2 * own
            at = t * ROWS if shared else s * segment + t * ROWS
            value = keep_ref[at : at + ROWS] + got_ref[at : at + ROWS]
            peak = jnp.max(jnp.abs(value), axis=1, keepdims=True)
            exponent = jnp.clip(jnp.ceil(jnp.log2(jnp.maximum(peak, 1e-30))), -90.0, 127.0)
            scaled = jnp.clip(jnp.round(value * jnp.exp2(15.0 - exponent)), -32767.0, 32767.0)
            ending = jnp.where(spare, exponent, scaled[:, last:])
            scaled = jnp.concatenate([scaled[:, :last], ending], axis=1) if last else ending
            if half:
                kept = slice(ROWS // 2, ROWS) if shared else slice(0, ROWS // 2)
                scaled = jnp.concatenate([scaled[kept, : width // 2], scaled[kept, width // 2 :]], axis=0)
            out_ref[:, t * width : t * width + scaled.shape[1]] = scaled.astype(jnp.int32).astype(jnp.int16)


def restored(own, size, width, got_ref, t):
    half = own - t * ROWS <= ROWS // 2
    value = got_ref[:, t * width : t * width + (width // 2 if half else width)]
    value = value.astype(jnp.int32).astype(jnp.float32)
    if half:
        value = jnp.concatenate([value[: ROWS // 2], value[ROWS // 2 :]], axis=1)
        value = jnp.concatenate([value, jnp.zeros_like(value)], axis=0)
    return value * jnp.exp2(value[:, size : size + 1] - 15.0)


def stats_kernel(own, size, *refs):
    *in_refs, guided_ref, out_ref = refs
    before = in_refs.pop(0) if in_refs[0].shape == out_ref.shape else None
    segment, width = guided_ref.shape
    last = width - TILE
    real = lax.broadcasted_iota(jnp.int32, (ROWS, TILE), 1) < size - last
    tops, totals = [], []
    for t in range(segment // ROWS):
        rows = slice(t * ROWS, (t + 1) * ROWS)
        guided = in_refs[0][rows]
        if t * ROWS < own:
            for got in in_refs[1:]:
                guided = guided + restored(own, size, width, got, t)
        guided_ref[rows] = guided
        ending = jnp.where(real, guided[:, last:], -jnp.inf)
        guided = jnp.concatenate([guided[:, :last], ending], axis=1) if last else ending
        top = jnp.max(guided, axis=1, keepdims=True)
        tops.append(top)
        totals.append(jnp.sum(jnp.exp(guided - top), axis=1, keepdims=True))
    top, total = as_row(jnp.concatenate(tops, axis=0)), as_row(jnp.concatenate(totals, axis=0))
    if before is not None:
        top, total = merged((top, total), (before[0:1, :segment], before[1:2, :segment]))
    out_ref[0:1, :segment] = top
    out_ref[1:2, :segment] = total


def merged(one, other):
    top = jnp.maximum(one[0], other[0])
    return top, one[1] * jnp.exp(one[0] - top) + other[1] * jnp.exp(other[0] - top)


def merge_kernel(one_ref, *refs):
    *other_refs, out_ref = refs
    top, total = one_ref[0:1], one_ref[1:2]
    for ref in other_refs:
        top, total = merged((top, total), (ref[0:1], ref[1:2]))
    out_ref[0:1] = top
    out_ref[1:2] = total


def final_kernel(sizes, segment, *refs):
    guided_refs, stats, (out_far, out_ref, sems) = refs[: len(sizes)], refs[len(sizes) : -3], refs[-3:]
    top, total = stats[0][0:1, :segment], stats[0][1:2, :segment]
    for ref in stats[1:]:
        top, total = merged((top, total), (ref[0:1, :segment], ref[1:2, :segment]))
    own = out_ref.shape[0]
    shift, log_total = as_column(top), as_column(jnp.log(total))
    copies = []
    for t, first in enumerate(range(0, own, ROWS)):
        rows = slice(first, min(first + ROWS, own))
        at = 0
        for ref, size in zip(guided_refs, sizes):
            out_ref[rows, at : at + size] = ref[rows, :size] - shift[rows] - log_total[rows]
            at += size
        copies.append(pltpu.make_async_copy(out_ref.at[rows], out_far.at[rows], sems.at[t]))
        copies[-1].start()
    for copy in copies:
        copy.wait()


def shifted(value, axis, by):
    size = lax.axis_size(axis)
    return lax.ppermute(value, axis, [(i, (i + by) % size) for i in range(size)])


def cut(vocab, widths):
    edges = [0]
    for width in widths:
        edges.append(min(vocab, edges[-1] + width))
    edges.append(vocab)
    return [(start, end - start) for start, end in zip(edges, edges[1:]) if end > start]


def padded(size):
    return -(-(size + 1) // TILE) * TILE


def packed_shape(own, width):
    blocks, rest = divmod(own, ROWS)
    lanes = blocks * width + (0 if rest == 0 else width // 2 if rest <= ROWS // 2 else width)
    return (ROWS, lanes)


def per_device(final_hidden, positions, norm_gain, unembedding):
    bf16, f32 = jnp.bfloat16, jnp.float32
    _, block, width_local = final_hidden.shape
    masked = positions.shape[0]
    vocab = unembedding.shape[1]
    n_z, n_x, n_c = lax.axis_size("vocab"), lax.axis_size("rows"), lax.axis_size("cfg")
    z, x, c = lax.axis_index("vocab"), lax.axis_index("rows"), lax.axis_index("cfg")
    own = masked // (n_x * n_c)
    segment = -(-(own + 1) // 16) * 16

    hidden, gain, places, squares = call(
        squares_kernel,
        [((2, block, width_local), bf16), ((1, width_local), f32), ((1, masked), jnp.int32), ((2, block), f32)],
        [],
        far=[final_hidden, norm_gain[None, :], positions[None, :]],
        scratch_shapes=[pltpu.SemaphoreType.DMA((3,))],
    )
    for axis in ("cfg", "rows"):
        squares = sum([shifted(squares, axis, s) for s in range(1, lax.axis_size(axis))], squares)
    usual = int(block * USUAL)
    skipped = usual // DEEP * DEEP
    compact, normed, crowded = pl.pallas_call(
        functools.partial(compact_kernel, usual, n_z),
        out_shape=[
            pltpu.VMEM((block, block), f32),
            pltpu.VMEM((2, block, width_local), bf16),
            jax.ShapeDtypeStruct((1, 1), jnp.int32),
        ],
        in_specs=in_vmem(3),
        out_specs=[*in_vmem(2), pl.BlockSpec(memory_space=pltpu.SMEM)],
        compiler_params=pltpu.CompilerParams(vmem_limit_bytes=8 * MIB),
    )(*keep_in_vmem(places, hidden, gain))
    block_rows, rest_rows = call(
        functools.partial(combine_kernel, width_local * n_x * n_c, usual),
        [((DEEP, usual * width_local // DEEP), bf16), ((block - skipped, width_local), bf16)],
        [normed, squares, compact],
    )

    weights = unembedding.T
    loads, loaded = cut(vocab, [width for group in LOADS for width in group]), []

    def load(count, after):
        nonlocal weights
        pieces = loads[len(loaded) : len(loaded) + count]
        if not pieces:
            return after
        weights, after = lax.optimization_barrier((weights, after))
        arrays = call(
            functools.partial(load_kernel, pieces[0][0]),
            [((width_local, size), bf16) for _, size in pieces],
            [],
            far=[weights],
            cost=(0, 2 * sum(size for _, size in pieces) * width_local),
            scratch_shapes=[pltpu.VMEM((SLOTS, TILE, width_local), bf16), pltpu.SemaphoreType.DMA((SLOTS,))],
        )
        *arrays, after = lax.optimization_barrier((*arrays, after))
        loaded.extend(arrays)
        return after

    def both_ways(own_block):
        ahead = behind = own_block
        gathered = [own_block]
        for step in range(1, n_z // 2 + 1):
            ahead = shifted(ahead, "vocab", 1)
            gathered.append(ahead)
            if 2 * step < n_z:
                behind = shifted(behind, "vocab", -1)
                gathered.append(behind)
        return gathered

    offsets = [0] + [sign * step for step in range(1, n_z // 2 + 1) for sign in (1, -1) if sign > 0 or 2 * step < n_z]
    rest = lax.cond(
        crowded[0, 0] > 0,
        lambda rest: jnp.concatenate(both_ways(rest), axis=0),
        lambda rest: jnp.zeros((n_z * rest.shape[0], rest.shape[1]), rest.dtype),
        rest_rows,
    )
    weights, places, rest = lax.optimization_barrier((weights, places, rest))
    ahead = shifted(block_rows, "vocab", 1)
    behind = load(len(LOADS[0]), block_rows)
    aheads, behinds = [ahead], []
    for step in range(1, (n_z - 1) // 2 + 1):
        behind = shifted(behind, "vocab", -1)
        behinds.append(behind)
    for step in range(2, n_z // 2 + 1):
        ahead = shifted(ahead, "vocab", 1)
        aheads.append(ahead)
    arrivals = [block_rows]
    for step in range(n_z // 2):
        arrivals += aheads[step : step + 1] + behinds[step : step + 1]

    half = half_rows(own, segment, n_x)
    selected, deep = n_c * half, -(-usual // DEEP) * DEEP
    early_chooser, last_chooser = call(
        functools.partial(chooser_kernel, own, block, usual, offsets, n_z, n_x, n_c),
        [((selected, (n_z - 1) * deep + n_z * (block - skipped)), bf16), ((selected, deep), bf16)],
        [places],
    )
    load(len(loads), aheads[0])
    early_chooser, last_chooser, *loaded = lax.optimization_barrier((early_chooser, last_chooser, *loaded))
    (early,) = call(
        functools.partial(early_kernel, usual),
        [((selected, width_local), bf16)],
        [early_chooser, *arrivals[:-1], rest],
    )

    chunks = cut(vocab, CHUNKS)
    parts, leaving = [], []
    for j, (start, size) in enumerate(chunks):
        width = padded(size)
        outs = [((half, width), f32)] * 2
        cost = (4 * half * width_local * size, 2 * width_local * size)
        needed = [i for i, (at, held) in enumerate(loads) if at < start + size and start < at + held]
        skip = start - loads[needed[0]][0]
        pieces = [loaded[i] for i in needed]
        if j == 0:
            rows, keep, send = call(
                functools.partial(first_kernel, skip, size, usual),
                [((selected, width_local), bf16)] + outs,
                [last_chooser, early, arrivals[-1], *pieces],
                cost=cost,
            )
        else:
            keep, send = call(functools.partial(later_kernel, skip, size), outs, [rows, *pieces], cost=cost)
        got = shifted(send, "cfg", 1)
        own_sum, *sends = call(
            functools.partial(add_kernel, own, size),
            [((segment, width), f32)] + [(packed_shape(own, width), jnp.int16)] * (n_x - 1),
            [keep, got],
        )
        parts.append(own_sum)
        leaving.append(sends)
    guided, stats = [], None
    for (_, size), own_sum, sends in zip(chunks, parts, leaving):
        got = [shifted(s_rows, "rows", s) for s, s_rows in enumerate(sends, 1)]
        chunk, stats = call(
            functools.partial(stats_kernel, own, size),
            [(own_sum.shape, f32), ((2, LANES), f32)],
            ([] if stats is None else [stats]) + [own_sum, *got],
        )
        guided.append(chunk)
    if n_z & (n_z - 1) == 0:
        all_stats = [stats] + [
            lax.ppermute(stats, "vocab", [(i, i ^ far) for i in range(n_z)]) for far in sorted(range(1, n_z), key=lambda far: [0,1,3,2][far % 4])
        ]
    else:
        all_stats = [stats] + [shifted(stats, "vocab", s) for s in range(1, n_z)]
    return pl.pallas_call(
        functools.partial(final_kernel, [size for _, size in chunks], segment),
        out_shape=jax.ShapeDtypeStruct((own, vocab), f32),
        in_specs=in_vmem(len(guided) + len(all_stats)),
        out_specs=pl.BlockSpec(memory_space=pltpu.HBM),
        scratch_shapes=[pltpu.VMEM((own, vocab), f32), pltpu.SemaphoreType.DMA((-(-own // ROWS),))],
        compiler_params=pltpu.CompilerParams(vmem_limit_bytes=8 * MIB),
    )(*keep_in_vmem(*guided, *all_stats))


def solution(mesh):
    placed = (
        P(None, ("groups", "vocab"), ("rows", "cfg")),
        P("groups"),
        P(("rows", "cfg")),
        P(("rows", "cfg"), "vocab"),
    )
    return jax.shard_map(
        per_device,
        mesh=mesh,
        in_specs=placed,
        out_specs=P(("groups", "rows", "cfg"), "vocab"),
        check_vma=False,
    )
```

```python
import functools

import jax
import jax.numpy as jnp
from jax import lax
from jax.experimental import pallas as pl
from jax.experimental.pallas import tpu as pltpu
from jax.sharding import PartitionSpec as P

epsilon = 1e-06
guidance = 2.0
TILE = 256
LANES = 128
MIB = 1 << 20
LOADS = ((512,), (1984,))
SLOTS = 5
CHUNKS = (2496,)
ROWS = 8
USUAL = 13 / 16
DEEP = 16


def in_vmem(count):
    return [pl.BlockSpec(memory_space=pltpu.VMEM)] * count


def keep_in_vmem(*arrays):
    return [pltpu.with_memory_space_constraint(a, pltpu.VMEM) for a in arrays]


def call(body, outs, args, far=(), limit=8, cost=None, **kwargs):
    return pl.pallas_call(
        body,
        out_shape=[pltpu.VMEM(shape, dtype) for shape, dtype in outs],
        in_specs=[pl.BlockSpec(memory_space=pltpu.HBM)] * len(far) + in_vmem(len(args)),
        out_specs=in_vmem(len(outs)),
        compiler_params=pltpu.CompilerParams(vmem_limit_bytes=limit * MIB),
        cost_estimate=cost and pl.CostEstimate(flops=cost[0], bytes_accessed=cost[1], transcendentals=0),
        **kwargs,
    )(*[pltpu.with_memory_space_constraint(a, pltpu.HBM) for a in far], *keep_in_vmem(*args))


def diagonal(n):
    return lax.broadcasted_iota(jnp.int32, (n, n), 0) == lax.broadcasted_iota(jnp.int32, (n, n), 1)


def as_column(row):
    return jnp.sum(jnp.where(diagonal(row.shape[1]), row, 0.0), axis=1, keepdims=True)


def as_row(column):
    return jnp.sum(jnp.where(diagonal(column.shape[0]), column, 0.0), axis=0, keepdims=True)


def squares_kernel(hidden_far, gain_far, places_far, hidden_ref, gain_ref, places_ref, out_ref, sems):
    block = hidden_ref.shape[1]
    copies = [pltpu.make_async_copy(hidden_far.at[b], hidden_ref.at[b], sems.at[b]) for b in range(2)]
    copies += [
        pltpu.make_async_copy(gain_far, gain_ref, sems.at[2]),
        pltpu.make_async_copy(places_far, places_ref, sems.at[3]),
    ]
    for copy in copies:
        copy.start()
    for b in range(2):
        copies[b].wait()
        widened = hidden_ref[b].astype(jnp.float32)
        out_ref[b : b + 1] = as_row(jnp.sum(widened * widened, axis=1, keepdims=True))
    for copy in copies[2:]:
        copy.wait()


def first_rank(positions_ref, at):
    return jnp.sum((positions_ref[...] < at).astype(jnp.float32), axis=1, keepdims=True).astype(jnp.int32)


def compact_kernel(usual, n_z, positions_ref, hidden_ref, gain_ref, compact_ref, normed_ref, crowded_ref):
    block, masked = compact_ref.shape[0], positions_ref.shape[1]
    ranks = [first_rank(positions_ref, b * block) for b in range(n_z + 1)]
    most = functools.reduce(jnp.maximum, [end - first for first, end in zip(ranks, ranks[1:])])
    crowded_ref[0, 0] = (jnp.max(most) > usual).astype(jnp.int32)
    at = lax.axis_index("vocab") * block
    first = first_rank(positions_ref, at)
    rank = lax.broadcasted_iota(jnp.int32, (block, masked), 1)
    match = rank == first + lax.broadcasted_iota(jnp.int32, (block, masked), 0)
    places = (positions_ref[...] + 1).astype(jnp.float32)
    wanted = jnp.sum(jnp.where(match, places, 0.0), axis=1, keepdims=True).astype(jnp.int32) - 1
    held = at + lax.broadcasted_iota(jnp.int32, (block, block), 1)
    compact = (wanted == held).astype(jnp.float32)
    compact_ref[...] = compact
    for b in range(2):
        normed = (hidden_ref[b].astype(jnp.float32) * gain_ref[...]).astype(jnp.bfloat16)
        normed = jnp.dot(compact.astype(jnp.bfloat16), normed, preferred_element_type=jnp.float32)
        normed_ref[b] = normed.astype(jnp.bfloat16)


def combine_kernel(width, usual, normed_ref, totals_ref, compact_ref, usual_ref, rest_ref):
    inv_rms = lax.rsqrt(totals_ref[...] / width + epsilon)
    place = compact_ref[...] > 0.5
    weight = [(1.0 + guidance) * inv_rms[0:1], guidance * inv_rms[1:2]]
    factor = [jnp.sum(jnp.where(place, row, 0.0), axis=1, keepdims=True) for row in weight]
    terms = [factor[b] * normed_ref[b].astype(jnp.float32) for b in range(2)]
    rows = terms[0] - terms[1]
    whole, last = divmod(usual, DEEP)
    columns = rows.shape[1]
    for t in range(whole):
        usual_ref[:, t * columns : (t + 1) * columns] = rows[t * DEEP : (t + 1) * DEEP].astype(jnp.bfloat16)
    if last:
        share = columns * last // DEEP
        ending = rows[whole * DEEP : usual]
        ending = jnp.concatenate([ending[:, at : at + share] for at in range(0, columns, share)], axis=0)
        usual_ref[:, whole * columns :] = ending.astype(jnp.bfloat16)
    rest_ref[...] = rows[whole * DEEP :].astype(jnp.bfloat16)


def unpacked(ref, usual, columns):
    whole, last = divmod(usual, DEEP)
    blocks = [ref[:, t * columns : (t + 1) * columns] for t in range(whole)]
    if last:
        ending = ref[:, whole * columns :].astype(jnp.float32)
        ending = jnp.concatenate([ending[at : at + last] for at in range(0, DEEP, last)], axis=1)
        ending = jnp.concatenate([ending, jnp.zeros((DEEP - last, columns), jnp.float32)], axis=0)
        blocks.append(ending.astype(jnp.bfloat16))
    return blocks


def load_kernel(start, weights_far, *refs):
    *out_refs, tiles_ref, sems = refs
    slots = tiles_ref.shape[0]
    tiles = []
    for ref in out_refs:
        size = ref.shape[1]
        tiles += [(ref, at, min(TILE, size - at), start + at) for at in range(0, size, TILE)]
        start += size
    copies = [
        pltpu.make_async_copy(
            weights_far.at[pl.ds(column, rows)],
            tiles_ref.at[i % slots, pl.ds(0, rows)],
            sems.at[i % slots],
        )
        for i, (_, _, rows, column) in enumerate(tiles)
    ]
    for copy in copies[:slots]:
        copy.start()
    for i, (ref, at, rows, _) in enumerate(tiles):
        copies[i].wait()
        ref[:, at : at + rows] = tiles_ref[i % slots, :rows].T
        if i + slots < len(tiles):
            copies[i + slots].start()


def chooser_kernel(own, block, usual, offsets, n_z, n_x, n_c, positions_ref, early_ref, last_ref):
    z, x, c = (lax.axis_index(axis) for axis in ("vocab", "rows", "cfg"))
    rows, deep = last_ref.shape
    half = rows // n_c
    segment = -(-own // ROWS) * ROWS if tight(own, n_x) else half // n_x
    row = lax.broadcasted_iota(jnp.int32, (rows, 1), 0)
    wanted = jnp.full((rows, 1), -1, jnp.int32)
    for t in range(n_c):
        for s in range(n_x):
            owner = lax.rem(x + s, n_x) * n_c + lax.rem(c + t, n_c)
            for at, first, end in row_ranges(own, segment, n_x, s):
                i = row - (t * half + at) + first
                wanted = jnp.where((i >= first) & (i < end), owner * own + i, wanted)
    lane = lax.broadcasted_iota(jnp.int32, (1, early_ref.shape[1]), 1)
    held = jnp.full(lane.shape, -2, jnp.int32)
    skipped = usual // DEEP * DEEP
    for k, offset in enumerate(offsets):
        at = lax.rem(z - offset + n_z, n_z) * block
        first, end = first_rank(positions_ref, at), first_rank(positions_ref, at + block)
        if k < n_z - 1:
            i = lane - k * deep
            held = jnp.where((i >= 0) & (i < usual) & (first + i < end), first + i, held)
        else:
            i = lax.broadcasted_iota(jnp.int32, (1, deep), 1)
            last = jnp.where((i < usual) & (first + i < end), first + i, -2)
        i = lane - (n_z - 1) * deep - k * (block - skipped) + skipped
        held = jnp.where((i >= usual) & (i < block) & (first + i < end), first + i, held)
    early_ref[...] = (wanted == held).astype(jnp.float32).astype(jnp.bfloat16)
    last_ref[...] = (wanted == last).astype(jnp.float32).astype(jnp.bfloat16)


def multiply(start, size, rows_ref, weights_refs, keep_ref, send_ref):
    half, width = keep_ref.shape
    at, skip = 0, start
    for ref in weights_refs:
        held = ref.shape[1]
        while at < size and skip < held:
            step = min(TILE, size - at, held - skip)
            product = jnp.dot(rows_ref[...], ref[:, skip : skip + step], preferred_element_type=jnp.float32)
            keep_ref[:, at : at + step] = product[:half]
            send_ref[:, at : at + step] = product[half:]
            at, skip = at + step, skip + step
        skip = max(0, skip - held)
    for ref in (keep_ref, send_ref):
        ref[:, size:] = jnp.zeros((half, width - size), jnp.float32)


def early_kernel(usual, chooser_ref, *refs):
    *block_refs, rest_ref, rows_ref = refs
    blocks = [part for ref in block_refs for part in unpacked(ref, usual, rows_ref.shape[1])]
    blocks = jnp.concatenate([*blocks, rest_ref[...]], axis=0)
    rows_ref[...] = jnp.dot(chooser_ref[...], blocks, preferred_element_type=jnp.float32).astype(jnp.bfloat16)


def first_kernel(start, size, usual, chooser_ref, early_ref, block_ref, *refs):
    *weights_refs, rows_ref, keep_ref, send_ref = refs
    block = jnp.concatenate(unpacked(block_ref, usual, rows_ref.shape[1]), axis=0)
    last = jnp.dot(chooser_ref[...], block, preferred_element_type=jnp.float32)
    rows_ref[...] = early_ref[...] + last.astype(jnp.bfloat16)
    multiply(start, size, rows_ref, weights_refs, keep_ref, send_ref)


def later_kernel(start, size, rows_ref, *refs):
    *weights_refs, keep_ref, send_ref = refs
    multiply(start, size, rows_ref, weights_refs, keep_ref, send_ref)


def tight(own, n_x):
    return n_x == 2 and own % ROWS == ROWS // 2


def half_rows(own, segment, n_x):
    return 2 * own if tight(own, n_x) else n_x * segment


def row_ranges(own, segment, n_x, s):
    if not tight(own, n_x):
        return [(s * segment, 0, own)]
    whole = own // ROWS * ROWS
    return [(0, 0, own)] if s == 0 else [(own, whole, own), (whole + ROWS, 0, whole)]


def add_kernel(own, size, keep_ref, got_ref, own_ref, *out_refs):
    segment, width = own_ref.shape
    own_ref[...] = keep_ref[:segment] + got_ref[:segment]
    last = width - TILE
    spare = lax.broadcasted_iota(jnp.int32, (ROWS, TILE), 1) >= size - last
    for s, out_ref in enumerate(out_refs, 1):
        for t in range(-(-own // ROWS)):
            half = own - t * ROWS <= ROWS // 2
            shared = half and keep_ref.shape[0] == 2 * own
            at = t * ROWS if shared else s * segment + t * ROWS
            value = keep_ref[at : at + ROWS] + got_ref[at : at + ROWS]
            peak = jnp.max(jnp.abs(value), axis=1, keepdims=True)
            exponent = jnp.clip(jnp.ceil(jnp.log2(jnp.maximum(peak, 1e-30))), -90.0, 127.0)
            scaled = jnp.clip(jnp.round(value * jnp.exp2(15.0 - exponent)), -32767.0, 32767.0)
            ending = jnp.where(spare, exponent, scaled[:, last:])
            scaled = jnp.concatenate([scaled[:, :last], ending], axis=1) if last else ending
            if half:
                kept = slice(ROWS // 2, ROWS) if shared else slice(0, ROWS // 2)
                scaled = jnp.concatenate([scaled[kept, : width // 2], scaled[kept, width // 2 :]], axis=0)
            out_ref[:, t * width : t * width + scaled.shape[1]] = scaled.astype(jnp.int32).astype(jnp.int16)


def restored(own, size, width, got_ref, t):
    half = own - t * ROWS <= ROWS // 2
    value = got_ref[:, t * width : t * width + (width // 2 if half else width)]
    value = value.astype(jnp.int32).astype(jnp.float32)
    if half:
        value = jnp.concatenate([value[: ROWS // 2], value[ROWS // 2 :]], axis=1)
        value = jnp.concatenate([value, jnp.zeros_like(value)], axis=0)
    return value * jnp.exp2(value[:, size : size + 1] - 15.0)


def stats_kernel(own, size, *refs):
    *in_refs, guided_ref, out_ref = refs
    before = in_refs.pop(0) if in_refs[0].shape == out_ref.shape else None
    segment, width = guided_ref.shape
    real = lax.broadcasted_iota(jnp.int32, (ROWS, width), 1) < size
    tops, totals = [], []
    for t in range(segment // ROWS):
        rows = slice(t * ROWS, (t + 1) * ROWS)
        guided = in_refs[0][rows]
        if t * ROWS < own:
            for got in in_refs[1:]:
                guided = guided + restored(own, size, width, got, t)
        guided_ref[rows] = guided
        top = jnp.max(jnp.where(real, guided, -jnp.inf), axis=1, keepdims=True)
        tops.append(top)
        totals.append(jnp.sum(jnp.where(real, jnp.exp(guided - top), 0.0), axis=1, keepdims=True))
    top, total = as_row(jnp.concatenate(tops, axis=0)), as_row(jnp.concatenate(totals, axis=0))
    if before is not None:
        top, total = merged((top, total), (before[0:1, :segment], before[1:2, :segment]))
    out_ref[0:1, :segment] = top
    out_ref[1:2, :segment] = total


def merged(one, other):
    top = jnp.maximum(one[0], other[0])
    return top, one[1] * jnp.exp(one[0] - top) + other[1] * jnp.exp(other[0] - top)


def merge_kernel(one_ref, *refs):
    *other_refs, out_ref = refs
    top, total = one_ref[0:1], one_ref[1:2]
    for ref in other_refs:
        top, total = merged((top, total), (ref[0:1], ref[1:2]))
    out_ref[0:1] = top
    out_ref[1:2] = total


def final_kernel(sizes, segment, *refs):
    guided_refs, stats, (out_far, out_ref, sems) = refs[: len(sizes)], refs[len(sizes) : -3], refs[-3:]
    top, total = stats[0][0:1, :segment], stats[0][1:2, :segment]
    for ref in stats[1:]:
        top, total = merged((top, total), (ref[0:1, :segment], ref[1:2, :segment]))
    own = out_ref.shape[0]
    shift, log_total = as_column(top), as_column(jnp.log(total))
    copies = []
    for t, first in enumerate(range(0, own, ROWS)):
        rows = slice(first, min(first + ROWS, own))
        at = 0
        for ref, size in zip(guided_refs, sizes):
            out_ref[rows, at : at + size] = ref[rows, :size] - shift[rows] - log_total[rows]
            at += size
        copies.append(pltpu.make_async_copy(out_ref.at[rows], out_far.at[rows], sems.at[t]))
        copies[-1].start()
    for copy in copies:
        copy.wait()


def shifted(value, axis, by):
    size = lax.axis_size(axis)
    return lax.ppermute(value, axis, [(i, (i + by) % size) for i in range(size)])


def cut(vocab, widths):
    edges = [0]
    for width in widths:
        edges.append(min(vocab, edges[-1] + width))
    edges.append(vocab)
    return [(start, end - start) for start, end in zip(edges, edges[1:]) if end > start]


def padded(size):
    return -(-(size + 1) // TILE) * TILE


def packed_shape(own, width):
    blocks, rest = divmod(own, ROWS)
    lanes = blocks * width + (0 if rest == 0 else width // 2 if rest <= ROWS // 2 else width)
    return (ROWS, lanes)


def per_device(final_hidden, positions, norm_gain, unembedding):
    bf16, f32 = jnp.bfloat16, jnp.float32
    _, block, width_local = final_hidden.shape
    masked = positions.shape[0]
    vocab = unembedding.shape[1]
    n_z, n_x, n_c = lax.axis_size("vocab"), lax.axis_size("rows"), lax.axis_size("cfg")
    z, x, c = lax.axis_index("vocab"), lax.axis_index("rows"), lax.axis_index("cfg")
    own = masked // (n_x * n_c)
    segment = -(-(own + 1) // 16) * 16

    hidden, gain, places, squares = call(
        squares_kernel,
        [((2, block, width_local), bf16), ((1, width_local), f32), ((1, masked), jnp.int32), ((2, block), f32)],
        [],
        far=[final_hidden, norm_gain[None, :], positions[None, :]],
        scratch_shapes=[pltpu.SemaphoreType.DMA((4,))],
    )
    for axis in ("cfg", "rows"):
        squares = sum([shifted(squares, axis, s) for s in range(1, lax.axis_size(axis))], squares)
    usual = int(block * USUAL)
    skipped = usual // DEEP * DEEP
    compact, normed, crowded = pl.pallas_call(
        functools.partial(compact_kernel, usual, n_z),
        out_shape=[
            pltpu.VMEM((block, block), f32),
            pltpu.VMEM((2, block, width_local), bf16),
            jax.ShapeDtypeStruct((1, 1), jnp.int32),
        ],
        in_specs=in_vmem(3),
        out_specs=[*in_vmem(2), pl.BlockSpec(memory_space=pltpu.SMEM)],
        compiler_params=pltpu.CompilerParams(vmem_limit_bytes=8 * MIB),
    )(*keep_in_vmem(places, hidden, gain))
    block_rows, rest_rows = call(
        functools.partial(combine_kernel, width_local * n_x * n_c, usual),
        [((DEEP, usual * width_local // DEEP), bf16), ((block - skipped, width_local), bf16)],
        [normed, squares, compact],
    )

    weights = unembedding.T
    loads, loaded = cut(vocab, [width for group in LOADS for width in group]), []

    def load(count, after):
        nonlocal weights
        pieces = loads[len(loaded) : len(loaded) + count]
        if not pieces:
            return after
        weights, after = lax.optimization_barrier((weights, after))
        arrays = call(
            functools.partial(load_kernel, pieces[0][0]),
            [((width_local, size), bf16) for _, size in pieces],
            [],
            far=[weights],
            cost=(0, 2 * sum(size for _, size in pieces) * width_local),
            scratch_shapes=[pltpu.VMEM((SLOTS, TILE, width_local), bf16), pltpu.SemaphoreType.DMA((SLOTS,))],
        )
        *arrays, after = lax.optimization_barrier((*arrays, after))
        loaded.extend(arrays)
        return after

    def both_ways(own_block):
        ahead = behind = own_block
        gathered = [own_block]
        for step in range(1, n_z // 2 + 1):
            ahead = shifted(ahead, "vocab", 1)
            gathered.append(ahead)
            if 2 * step < n_z:
                behind = shifted(behind, "vocab", -1)
                gathered.append(behind)
        return gathered

    offsets = [0] + [sign * step for step in range(1, n_z // 2 + 1) for sign in (1, -1) if sign > 0 or 2 * step < n_z]
    rest = lax.cond(
        crowded[0, 0] > 0,
        lambda rest: jnp.concatenate(both_ways(rest), axis=0),
        lambda rest: jnp.zeros((n_z * rest.shape[0], rest.shape[1]), rest.dtype),
        rest_rows,
    )
    weights, places, rest = lax.optimization_barrier((weights, places, rest))
    ahead = shifted(block_rows, "vocab", 1)
    behind = load(len(LOADS[0]), block_rows)
    aheads, behinds = [ahead], []
    for step in range(1, (n_z - 1) // 2 + 1):
        behind = shifted(behind, "vocab", -1)
        behinds.append(behind)
    for step in range(2, n_z // 2 + 1):
        ahead = shifted(ahead, "vocab", 1)
        aheads.append(ahead)
    arrivals = [block_rows]
    for step in range(n_z // 2):
        arrivals += aheads[step : step + 1] + behinds[step : step + 1]

    half = half_rows(own, segment, n_x)
    selected, deep = n_c * half, -(-usual // DEEP) * DEEP
    early_chooser, last_chooser = call(
        functools.partial(chooser_kernel, own, block, usual, offsets, n_z, n_x, n_c),
        [((selected, (n_z - 1) * deep + n_z * (block - skipped)), bf16), ((selected, deep), bf16)],
        [places],
    )
    load(len(loads), aheads[0])
    early_chooser, last_chooser, *loaded = lax.optimization_barrier((early_chooser, last_chooser, *loaded))
    (early,) = call(
        functools.partial(early_kernel, usual),
        [((selected, width_local), bf16)],
        [early_chooser, *arrivals[:-1], rest],
    )

    chunks = cut(vocab, CHUNKS)
    parts, leaving = [], []
    for j, (start, size) in enumerate(chunks):
        width = padded(size)
        outs = [((half, width), f32)] * 2
        cost = (4 * half * width_local * size, 2 * width_local * size)
        needed = [i for i, (at, held) in enumerate(loads) if at < start + size and start < at + held]
        skip = start - loads[needed[0]][0]
        pieces = [loaded[i] for i in needed]
        if j == 0:
            rows, keep, send = call(
                functools.partial(first_kernel, skip, size, usual),
                [((selected, width_local), bf16)] + outs,
                [last_chooser, early, arrivals[-1], *pieces],
                cost=cost,
            )
        else:
            keep, send = call(functools.partial(later_kernel, skip, size), outs, [rows, *pieces], cost=cost)
        got = shifted(send, "cfg", 1)
        own_sum, *sends = call(
            functools.partial(add_kernel, own, size),
            [((segment, width), f32)] + [(packed_shape(own, width), jnp.int16)] * (n_x - 1),
            [keep, got],
        )
        parts.append(own_sum)
        leaving.append(sends)
    guided, stats = [], None
    for (_, size), own_sum, sends in zip(chunks, parts, leaving):
        got = [shifted(s_rows, "rows", s) for s, s_rows in enumerate(sends, 1)]
        chunk, stats = call(
            functools.partial(stats_kernel, own, size),
            [(own_sum.shape, f32), ((2, LANES), f32)],
            ([] if stats is None else [stats]) + [own_sum, *got],
        )
        guided.append(chunk)
    if n_z & (n_z - 1) == 0:
        all_stats = [stats] + [
            lax.ppermute(stats, "vocab", [(i, i ^ far) for i in range(n_z)]) for far in sorted(range(1, n_z), key=lambda far: [0,1,3,2][far % 4])
        ]
    else:
        all_stats = [stats] + [shifted(stats, "vocab", s) for s in range(1, n_z)]
    return pl.pallas_call(
        functools.partial(final_kernel, [size for _, size in chunks], segment),
        out_shape=jax.ShapeDtypeStruct((own, vocab), f32),
        in_specs=in_vmem(len(guided) + len(all_stats)),
        out_specs=pl.BlockSpec(memory_space=pltpu.HBM),
        scratch_shapes=[pltpu.VMEM((own, vocab), f32), pltpu.SemaphoreType.DMA((-(-own // ROWS),))],
        compiler_params=pltpu.CompilerParams(vmem_limit_bytes=8 * MIB),
    )(*keep_in_vmem(*guided, *all_stats))


def solution(mesh):
    placed = (
        P(None, ("groups", "vocab"), ("rows", "cfg")),
        P("groups"),
        P(("rows", "cfg")),
        P(("rows", "cfg"), "vocab"),
    )
    return jax.shard_map(
        per_device,
        mesh=mesh,
        in_specs=placed,
        out_specs=P(("groups", "rows", "cfg"), "vocab"),
        check_vma=False,
    )
```
